32 devices in a mesh: parts: 2 (over x), docs: 16 (over z, y, core).
Axes of the slice: x: 2, y: 2, z: 4, core: 2. Of those that a mesh axis runs over, the one named last changes fastest.
Arguments:
- doc_grads: bfloat16 [4096, 8192], P('parts', 'docs'), parts along dimension 0, may hold values from -6 to 6
- query_grads: bfloat16 [16384, 8192], P(('parts', 'docs')), parts along dimension 0, may hold values from -6 to 6
- left_inv: bfloat16 [2, 32, 32], replicated, may hold values from -17 to 17, as said below
- right_inv: bfloat16 [2, 128, 128], replicated, may hold values from -17 to 17, as said below
- cand_owner: int32 [8192, 1], P(('parts', 'docs')), parts along dimension 0, may hold values from 0 to 15; in each aligned block of 256 rows (0 to 255, 256 to 511, ...) at most 32 rows name the same one
- cand_row: int32 [8192], P(('parts', 'docs')), parts along dimension 0, may hold values from 0 to 127
Outputs:
- scores: float32 [16384, 256], P(('parts', 'docs')), parts along dimension 0
The draws below stay inside these ranges and needn't reach their ends.
There are 2 independent parts, one for each index of `parts`. The reference program is written for one: setup_inputs(seed, part) draws one part's arguments, and reference() takes and returns one part's arrays. A program takes and returns all parts, laid end to end along the dimension named above; an argument that names none is the same for every part. Nothing has to cross between parts.
Inputs may be any that keep to these rules, and one draw needn't show every extreme that they name: `cand_owner`: within the 256 entries of one query batch no owner is named more than 32 times, a bound that some block reaches. `left_inv`: symmetric positive definite. `right_inv`: symmetric positive definite.
All inputs are finite; a program needn't handle non-finite values.
Results may differ from the reference program's by a relative error of at most 0.004.
Values may be sent and summed in bfloat16 or wider, within the bound.
No kernel may reach another device: no remote copies, remote signals or barrier semaphores. Data moves between devices by JAX's collectives and lax.ppermute only.
A program may use at most 128 MiB of HBM per device.

```python
import math
import jax
import jax.numpy as jnp
import numpy as np
from jax import lax

LAYERS = 2
K_OUT = 32
K_IN = 128
FEAT = 8192
DOC_DEV = 128
Q_DEV = 512
REQ_DEV = 256
CAP = 32
DOCS = 2048
QUERIES = 8192
REQS = 4096
N_DOCS = 16


def curvature_factor(key, width):
    factor_base = jnp.clip(jax.random.normal(key, (LAYERS, width, width), jnp.float32), -4.0, 4.0)
    square = jnp.einsum('lij,lkj->lik', factor_base, factor_base) / width
    return (0.5 * jnp.eye(width, dtype=jnp.float32)[None] + square).astype(jnp.bfloat16)


def draw_left_inv(key, part):
    return curvature_factor(jax.random.fold_in(key, 11), K_OUT)


def draw_right_inv(key, part):
    return curvature_factor(jax.random.fold_in(key, 23), K_IN)


def place_ends(values, own_key, smallest, largest):
    dims = values.shape
    spot = [jax.random.randint(jax.random.fold_in(own_key, axis), (), 0, dims[axis]) for axis in range(len(dims))]
    values = values.at[tuple(spot)].set(smallest)
    longest = dims.index(max(dims))
    spot[longest] = (spot[longest] + 1) % dims[longest]
    return values.at[tuple(spot)].set(largest)


def block_scale(stream_key, shape, split, low, high):
    factor_of = 1.0
    for position, blocks in split:
        steps = jax.random.uniform(jax.random.fold_in(jax.random.fold_in(stream_key, 6), position), (blocks,), jnp.float32, low / len(split), high / len(split))
        factor_of = factor_of * jnp.repeat(jnp.exp(steps), shape[position] // blocks).reshape((-1,) + (1,) * (len(shape) - 1 - position))
    return factor_of


def assign_block(own_key, own, number, rows, amount, top, bound, slope):
    order = jax.random.permutation(own_key, amount)
    heavy_load, usual = shares(amount, rows * top, bound, slope, True), shares(amount, rows * top, bound, slope, False)
    places = jnp.arange(amount)

    def named(tallies, offset_by):
        used = int((tallies > 0).sum())
        fixed = max(1, used // 4)
        moved = fixed + (places - fixed + offset_by * (used - fixed)) % max(1, amount - fixed)
        return jnp.zeros((amount,), jnp.int32).at[order[jnp.where(places < fixed, places, moved)]].set(jnp.asarray(tallies, jnp.int32))

    tallies = jnp.where(number % 4 == 0, named(heavy_load, number // 4), named(usual, number - number // 4 - 1))
    mixed = jax.random.permutation(jax.random.fold_in(own, 3), amount)
    donor, sink = mixed[0:amount // 2 * 2:2], mixed[1:amount // 2 * 2:2]
    margin = jnp.minimum(tallies[donor] - 1, bound - tallies[sink]) // 2
    margin = jnp.where((donor == order[0]) | (sink == order[0]) | (tallies[sink] == 0), 0, jnp.maximum(margin, 0))
    moved = jax.random.randint(jax.random.fold_in(own, 4), (amount // 2,), 0, 1 << 20) % (margin + 1)
    tallies = tallies.at[donor].add(-moved).at[sink].add(moved)
    items = jnp.searchsorted(jnp.cumsum(tallies), jnp.arange(rows * top), side="right").astype(jnp.int32)
    grid = items.reshape(top, rows).T
    grid = grid[jax.random.permutation(jax.random.fold_in(own, 1), rows)]
    offset_by = jax.random.randint(jax.random.fold_in(own, 2), (rows, 1), 0, top)
    return jnp.take_along_axis(grid, (jnp.arange(top)[None, :] + offset_by) % top, axis=1)


def shares(number_of, total, reach, slope, full):
    weights = [(1 << 20) // math.isqrt(grade ** slope) + 1 for grade in range(1, number_of + 1)]
    largest = reach if full else min(reach, max(-(-total // number_of), total * weights[0] // sum(weights)))
    least = 1 if total - largest >= number_of - 1 else 0
    counts, surplus = [largest] + [least] * (number_of - 1), total - largest - least * (number_of - 1)
    while surplus > 0:
        movable = [i for i in range(1, number_of) if counts[i] < largest] or [i for i in range(1, number_of) if counts[i] < reach]
        whole, left = sum([weights[i] for i in movable]), surplus
        for i in movable:
            addition = min(reach - counts[i], max(1, left * weights[i] // whole), surplus)
            counts[i] = counts[i] + addition
            surplus = surplus - addition
    return np.array(counts)


def scatter_about(rng, dims, deviation, reach, cuts=(), held_as=jnp.bfloat16):
    values = deviation * jax.random.normal(rng, dims, jnp.float32)
    if cuts:
        values = values * block_scale(rng, dims, cuts, -0.22, 0.18)
    return jnp.clip(values, -reach, reach).astype(held_as)


def setup_inputs(seed: int = 0, part: int = 0) -> dict:
    seeds = jax.random.split(jax.random.key(seed), 7)
    part_splits = jax.random.split(jax.random.fold_in(seeds[6], part), 7)
    doc_grads = scatter_about(part_splits[0], (DOCS, FEAT), 1.0, 6.0, ((1, 16),))
    query_grads = scatter_about(part_splits[1], (QUERIES, FEAT), 1.0, 6.0, ((0, 16),))
    left_inv = draw_left_inv(jax.random.fold_in(seeds[6], 71), part)
    right_inv = draw_right_inv(jax.random.fold_in(seeds[6], 71), part)
    cand_owner_keys = jax.random.split(jax.random.fold_in(part_splits[4], 1), REQS // REQ_DEV)
    cand_owner_turns = jax.random.permutation(jax.random.fold_in(part_splits[4], 3), REQS // REQ_DEV)
    cand_owner = jax.vmap(lambda own, number: assign_block(jax.random.fold_in(part_splits[4], 2), own, number, REQ_DEV, N_DOCS, 1, CAP, 2))(cand_owner_keys, cand_owner_turns).reshape((REQS, 1))
    cand_row = place_ends(jax.random.randint(part_splits[5], (REQS,), 0, DOC_DEV), jax.random.fold_in(part_splits[5], 1), 0, DOC_DEV - 1).astype(jnp.int32)
    return {"doc_grads": doc_grads, "query_grads": query_grads, "left_inv": left_inv, "right_inv": right_inv, "cand_owner": cand_owner, "cand_row": cand_row}


def precondition(queries, left_inv, right_inv):
    total = queries.shape[0]
    block_size = K_OUT * K_IN
    pieces = []
    for layer_index in range(LAYERS):
        block = queries[:, layer_index * block_size:(layer_index + 1) * block_size].reshape(total, K_OUT, K_IN)
        middle = jnp.einsum("qij,jk->qik", block.astype(jnp.float32), right_inv[layer_index].astype(jnp.float32)).astype(jnp.bfloat16)
        middle = lax.optimization_barrier(middle)
        result = jnp.einsum("ai,qik->qak", left_inv[layer_index].astype(jnp.float32), middle.astype(jnp.float32)).astype(jnp.bfloat16)
        pieces.append(result.reshape(total, block_size))
    return jnp.concatenate(pieces, axis=1)


def reference(doc_grads, query_grads, left_inv, right_inv, cand_owner, cand_row):
    def one_batch(inputs):
        queries, owners, rows_given = inputs
        prepared = precondition(queries, left_inv, right_inv)
        doc_ids = (owners * DOC_DEV + rows_given).astype(jnp.int32)
        chosen = jnp.take(doc_grads, doc_ids, axis=0)
        return jnp.dot(prepared, chosen.T, preferred_element_type=jnp.float32) * (FEAT ** -0.5)

    batches = (query_grads.reshape(N_DOCS, Q_DEV, FEAT), cand_owner[:, 0].reshape(N_DOCS, REQ_DEV), cand_row.reshape(N_DOCS, REQ_DEV))
    result = lax.map(one_batch, batches)
    return result.reshape(N_DOCS * Q_DEV, REQ_DEV)
```

```python
import jax
import jax.numpy as jnp
from jax import lax
from jax.experimental import pallas as pl
from jax.experimental.pallas import tpu as pltpu
from jax.sharding import PartitionSpec as P

LANES = 128


def gather_kernel(ids_ref, table_ref, out_ref):
    ids = ids_ref[0]
    docs, entries = table_ref.shape[1], ids.shape[1]
    group, row = ids // LANES, ids % LANES
    in_group = (lax.broadcasted_iota(jnp.int32, (LANES, entries), 0) == row).astype(jnp.bfloat16)
    one_hot = jnp.concatenate(
        [in_group * (group == g).astype(jnp.bfloat16) for g in range(docs // LANES)], axis=0
    )
    out_ref[0] = jnp.dot(table_ref[...], one_hot, preferred_element_type=jnp.float32).astype(
        out_ref.dtype
    )


def gather_columns(ids, table):
    batches, _, entries = ids.shape
    features, docs = table.shape
    return pl.pallas_call(
        gather_kernel,
        grid=(batches,),
        in_specs=[
            pl.BlockSpec((1, 1, entries), lambda b: (b, 0, 0)),
            pl.BlockSpec((features, docs), lambda b: (0, 0)),
        ],
        out_specs=pl.BlockSpec((1, features, entries), lambda b: (b, 0, 0)),
        out_shape=jax.ShapeDtypeStruct((batches, features, entries), table.dtype),
        compiler_params=pltpu.CompilerParams(vmem_limit_bytes=48 << 20),
        cost_estimate=pl.CostEstimate(
            flops=2 * batches * features * docs * entries,
            bytes_accessed=2 * features * (docs + batches * entries),
            transcendentals=0,
        ),
    )(ids, table)


def score_kernel(scale, prepared_ref, chosen_ref, total_ref, out_ref):
    part = jnp.dot(prepared_ref[...], chosen_ref[...], preferred_element_type=jnp.float32)
    out_ref[...] = (total_ref[...] + part) * scale


def add_scores(prepared, chosen, total, scale):
    return pl.pallas_call(
        lambda *refs: score_kernel(scale, *refs),
        in_specs=[pl.BlockSpec(memory_space=pltpu.VMEM)] * 3,
        out_specs=pl.BlockSpec(memory_space=pltpu.VMEM),
        out_shape=jax.ShapeDtypeStruct(total.shape, total.dtype),
        compiler_params=pltpu.CompilerParams(vmem_limit_bytes=48 << 20),
        cost_estimate=pl.CostEstimate(
            flops=2 * prepared.shape[0] * prepared.shape[1] * chosen.shape[1],
            bytes_accessed=2 * prepared.size + 2 * chosen.size + 8 * total.size,
            transcendentals=0,
        ),
    )(prepared, chosen, total)


def precondition(queries, left_inv, right_inv):
    total = queries.shape[0]
    k_out = left_inv.shape[1]
    k_in = right_inv.shape[1]
    block_size = k_out * k_in
    pieces = []
    for layer_index in range(left_inv.shape[0]):
        block = queries[:, layer_index * block_size : (layer_index + 1) * block_size].reshape(
            total, k_out, k_in
        )
        middle = jnp.einsum(
            "qij,jk->qik", block, right_inv[layer_index], preferred_element_type=jnp.float32
        ).astype(jnp.bfloat16)
        result = jnp.einsum(
            "ai,qik->qak", left_inv[layer_index], middle, preferred_element_type=jnp.float32
        ).astype(jnp.bfloat16)
        pieces.append(result.reshape(total, block_size))
    return jnp.concatenate(pieces, axis=1)


def chunks_of(width):
    if width % 512:
        return [(0, width)]
    quarter = width // 4
    return [(0, quarter), (2 * quarter, 2 * quarter), (quarter, quarter)]


def on_device(doc_grads, query_grads, left_inv, right_inv, cand_owner, cand_row):
    devices = lax.axis_size("docs")
    doc_count = doc_grads.shape[0] // devices
    entries = cand_row.shape[0]
    width = doc_grads.shape[1]
    queries = query_grads.shape[0]
    own_ids = cand_owner[:, 0] * doc_count + cand_row
    ids = lax.all_to_all(
        jnp.broadcast_to(own_ids, (devices, 1, entries)), "docs", split_axis=0, concat_axis=0, tiled=True
    )
    table = doc_grads.T
    chosen = []
    for start, size in chunks_of(width):
        piece = gather_columns(ids, table[start : start + size])
        ids, _ = lax.optimization_barrier((ids, piece))
        chosen.append(
            lax.all_to_all(piece, "docs", split_axis=0, concat_axis=0, tiled=True).reshape(
                devices * size, entries
            )
        )
    prepared = precondition(query_grads, left_inv, right_inv).reshape(queries, devices, width)
    scores = jnp.zeros((queries, entries), jnp.float32)
    for i, (start, size) in enumerate(chunks_of(width)):
        block = prepared[:, :, start : start + size].reshape(queries, devices * size)
        last = i == len(chosen) - 1
        scores = add_scores(
            block, chosen[i], scores, query_grads.shape[1] ** (-0.5) if last else 1.0
        )
    return scores


def solution(mesh):
    placed = (
        P("parts", "docs"),
        P(("parts", "docs"), None),
        P(),
        P(),
        P(("parts", "docs"), None),
        P(("parts", "docs")),
    )
    return jax.shard_map(
        on_device, mesh=mesh, in_specs=placed, out_specs=P(("parts", "docs"), None), check_vma=False
    )
```

```python
import jax
import jax.numpy as jnp
from jax import lax
from jax.experimental import pallas as pl
from jax.experimental.pallas import tpu as pltpu
from jax.sharding import PartitionSpec as P

LANES = 128
VMEM_BYTES = 48 << 20


def gather_kernel(count, me_ref, *refs):
    ids_refs, table_ref, out_refs = refs[:count], refs[count], refs[count + 1 :]
    docs = table_ref.shape[1]
    for ids_ref, out_ref in zip(ids_refs, out_refs):
        ids = ids_ref[0]
        group, row = ids // LANES, ids % LANES
        in_group = (
            lax.broadcasted_iota(jnp.int32, (LANES, ids.shape[1]), 0) == row
        ).astype(jnp.bfloat16)
        one_hot = jnp.concatenate(
            [in_group * (group == g).astype(jnp.bfloat16) for g in range(docs // LANES)], axis=0
        )
        out_ref[...] = jnp.dot(
            table_ref[...], one_hot, preferred_element_type=jnp.float32
        ).astype(out_ref.dtype)


def gather_columns(me, ids, table, partners):
    entries = ids.shape[2]
    features, docs = table.shape
    count = len(partners)
    return pl.pallas_call(
        lambda *refs: gather_kernel(count, *refs),
        grid_spec=pltpu.PrefetchScalarGridSpec(
            num_scalar_prefetch=1,
            grid=(1,),
            in_specs=[
                pl.BlockSpec((1, 1, entries), lambda i, me, k=k: (me[0] ^ k, 0, 0)) for k in partners
            ]
            + [pl.BlockSpec((features, docs), lambda i, me: (0, 0))],
            out_specs=[pl.BlockSpec((features, entries), lambda i, me: (0, 0))] * count,
        ),
        out_shape=[jax.ShapeDtypeStruct((features, entries), table.dtype)] * count,
        compiler_params=pltpu.CompilerParams(vmem_limit_bytes=VMEM_BYTES),
        cost_estimate=pl.CostEstimate(
            flops=2 * count * features * docs * entries,
            bytes_accessed=2 * features * (docs + count * entries),
            transcendentals=0,
        ),
    )(me, *[ids] * count, table)


def score_kernel(count, scale, me_ref, *refs):
    prepared_refs, chosen_refs, totals, out_ref = (
        refs[:count],
        refs[count : 2 * count],
        refs[2 * count : -1],
        refs[-1],
    )
    total = sum(
        jnp.dot(p[...], c[...], preferred_element_type=jnp.float32)
        for p, c in zip(prepared_refs, chosen_refs)
    )
    for ref in totals:
        total = total + ref[...]
    out_ref[...] = total * scale


def add_scores(me, prepared, chosen, partners, total, scale):
    queries = prepared.shape[0]
    width, entries = chosen[0].shape
    count = len(partners)
    totals = [] if total is None else [total]
    whole = pl.BlockSpec((queries, entries), lambda i, me: (0, 0))
    return pl.pallas_call(
        lambda *refs: score_kernel(count, scale, *refs),
        grid_spec=pltpu.PrefetchScalarGridSpec(
            num_scalar_prefetch=1,
            grid=(1,),
            in_specs=[
                pl.BlockSpec((queries, width), lambda i, me, k=k: (0, me[0] ^ k)) for k in partners
            ]
            + [pl.BlockSpec((width, entries), lambda i, me: (0, 0))] * count
            + [whole] * len(totals),
            out_specs=whole,
        ),
        out_shape=jax.ShapeDtypeStruct((queries, entries), jnp.float32),
        compiler_params=pltpu.CompilerParams(vmem_limit_bytes=VMEM_BYTES),
        cost_estimate=pl.CostEstimate(
            flops=2 * count * queries * width * entries,
            bytes_accessed=2 * count * width * (queries + entries) + 8 * queries * entries,
            transcendentals=0,
        ),
    )(me, *[prepared] * count, *chosen, *totals)


def precondition(queries, left_inv, right_inv):
    total = queries.shape[0]
    k_out = left_inv.shape[1]
    k_in = right_inv.shape[1]
    block_size = k_out * k_in
    pieces = []
    for layer_index in range(left_inv.shape[0]):
        block = queries[:, layer_index * block_size : (layer_index + 1) * block_size].reshape(
            total, k_out, k_in
        )
        middle = jnp.einsum(
            "qij,jk->qik", block, right_inv[layer_index], preferred_element_type=jnp.float32
        ).astype(jnp.bfloat16)
        result = jnp.einsum(
            "ai,qik->qak", left_inv[layer_index], middle, preferred_element_type=jnp.float32
        ).astype(jnp.bfloat16)
        pieces.append(result.reshape(total, block_size))
    return jnp.concatenate(pieces, axis=1)


def on_device(doc_grads, query_grads, left_inv, right_inv, cand_owner, cand_row):
    devices = lax.axis_size("docs")
    me = lax.axis_index("docs").astype(jnp.int32).reshape(1)
    doc_count = doc_grads.shape[0] // devices
    entries = cand_row.shape[0]
    own_ids = cand_owner[:, 0] * doc_count + cand_row
    ids = lax.all_to_all(
        jnp.broadcast_to(own_ids, (devices, 1, entries)), "docs", split_axis=0, concat_axis=0, tiled=True
    )
    table = doc_grads.T
    half = devices // 2
    far, near = list(range(half, devices)), list(range(1, half))
    groups = [far[:1], far[1:3], far[3:] + near, [0]]
    chosen = {}
    for partners in groups:
        pieces = gather_columns(me, ids, table, partners)
        ids, pieces = lax.optimization_barrier((ids, pieces))
        for k, piece in zip(partners, pieces):
            chosen[k] = (
                piece
                if k == 0
                else lax.ppermute(piece, "docs", [(i, i ^ k) for i in range(devices)])
            )
    prepared = precondition(query_grads, left_inv, right_inv)
    scale = query_grads.shape[1] ** (-0.5)
    parts = [[0] + near, far[:-2], far[-2:]]
    scores = None
    for i, partners in enumerate(parts):
        scores = add_scores(
            me,
            prepared,
            [chosen[k] for k in partners],
            partners,
            scores,
            scale if i == len(parts) - 1 else 1.0,
        )
    return scores


def solution(mesh):
    placed = (
        P("parts", "docs"),
        P(("parts", "docs"), None),
        P(),
        P(),
        P(("parts", "docs"), None),
        P(("parts", "docs")),
    )
    return jax.shard_map(
        on_device, mesh=mesh, in_specs=placed, out_specs=P(("parts", "docs"), None), check_vma=False
    )
```

```python
import jax
import jax.numpy as jnp
from jax import lax
from jax.experimental import pallas as pl
from jax.experimental.pallas import tpu as pltpu
from jax.sharding import PartitionSpec as P

LANES = 128
VMEM_BYTES = 48 << 20


def one_hot(ids, docs):
    group, row = ids // LANES, ids % LANES
    in_group = (lax.broadcasted_iota(jnp.int32, (LANES, ids.shape[1]), 0) == row).astype(jnp.bfloat16)
    return jnp.concatenate(
        [in_group * (group == g).astype(jnp.bfloat16) for g in range(docs // LANES)], axis=0
    )


def gather_all_kernel(ids_ref, table_ref, out_ref):
    table = table_ref[...]
    out_ref[0] = jnp.dot(
        table, one_hot(ids_ref[0], table.shape[1]), preferred_element_type=jnp.float32
    ).astype(out_ref.dtype)


def gather_all(ids, table):
    batches, _, entries = ids.shape
    features, docs = table.shape
    return pl.pallas_call(
        gather_all_kernel,
        grid=(batches,),
        in_specs=[
            pl.BlockSpec((1, 1, entries), lambda b: (b, 0, 0)),
            pl.BlockSpec((features, docs), lambda b: (0, 0)),
        ],
        out_specs=pl.BlockSpec((1, features, entries), lambda b: (b, 0, 0)),
        out_shape=jax.ShapeDtypeStruct((batches, features, entries), table.dtype),
        compiler_params=pltpu.CompilerParams(vmem_limit_bytes=VMEM_BYTES),
        cost_estimate=pl.CostEstimate(
            flops=2 * batches * features * docs * entries,
            bytes_accessed=2 * features * (docs + batches * entries),
            transcendentals=0,
        ),
    )(ids, table)


def gather_near_kernel(count, me_ref, *refs):
    ids_refs, tables, out_refs = refs[:count], refs[count : count + 2], refs[count + 2 :]
    features, docs = tables[0].shape
    for ids_ref, out_ref in zip(ids_refs, out_refs):
        hot = one_hot(ids_ref[0], docs)
        for i, table_ref in enumerate(tables):
            out_ref[i * features : (i + 1) * features, :] = jnp.dot(
                table_ref[...], hot, preferred_element_type=jnp.float32
            ).astype(out_ref.dtype)


def gather_near(me, ids, own, far, partners):
    entries = ids.shape[2]
    features, docs = own.shape
    count = len(partners)
    return pl.pallas_call(
        lambda *refs: gather_near_kernel(count, *refs),
        grid_spec=pltpu.PrefetchScalarGridSpec(
            num_scalar_prefetch=1,
            grid=(1,),
            in_specs=[
                pl.BlockSpec((1, 1, entries), lambda i, me, k=k: (me[0] ^ k, 0, 0)) for k in partners
            ]
            + [pl.BlockSpec((features, docs), lambda i, me: (0, 0))] * 2,
            out_specs=[pl.BlockSpec((2 * features, entries), lambda i, me: (0, 0))] * count,
        ),
        out_shape=[jax.ShapeDtypeStruct((2 * features, entries), own.dtype)] * count,
        compiler_params=pltpu.CompilerParams(vmem_limit_bytes=VMEM_BYTES),
        cost_estimate=pl.CostEstimate(
            flops=4 * count * features * docs * entries,
            bytes_accessed=4 * features * (docs + count * entries),
            transcendentals=0,
        ),
    )(me, *[ids] * count, own, far)


def score_near_kernel(count, me_ref, *refs):
    own_refs, far_refs, chosen_refs, out_ref = (
        refs[:count],
        refs[count : 2 * count],
        refs[2 * count : 3 * count],
        refs[-1],
    )
    total = None
    for own, far, chosen in zip(own_refs, far_refs, chosen_refs):
        pair = jnp.concatenate([own[...], far[...]], axis=1)
        part = jnp.dot(pair, chosen[...], preferred_element_type=jnp.float32)
        total = part if total is None else total + part
    out_ref[...] = total


def score_near(me, prepared, chosen, partners, half, width):
    queries = prepared.shape[0]
    features, entries = chosen[0].shape
    size = features // 2
    stride = width // size
    count = len(partners)
    return pl.pallas_call(
        lambda *refs: score_near_kernel(count, *refs),
        grid_spec=pltpu.PrefetchScalarGridSpec(
            num_scalar_prefetch=1,
            grid=(1,),
            in_specs=[
                pl.BlockSpec((queries, size), lambda i, me, k=k: (0, (me[0] ^ k) * stride))
                for k in list(partners) + [k ^ half for k in partners]
            ]
            + [pl.BlockSpec((features, entries), lambda i, me: (0, 0))] * count,
            out_specs=pl.BlockSpec((queries, entries), lambda i, me: (0, 0)),
        ),
        out_shape=jax.ShapeDtypeStruct((queries, entries), jnp.float32),
        compiler_params=pltpu.CompilerParams(vmem_limit_bytes=VMEM_BYTES),
        cost_estimate=pl.CostEstimate(
            flops=2 * count * queries * features * entries,
            bytes_accessed=2 * count * features * (queries + entries) + 4 * queries * entries,
            transcendentals=0,
        ),
    )(me, *[prepared] * (2 * count), *chosen)


def score_all_kernel(width, scale, prepared_ref, chosen_ref, total_ref, out_ref):
    sources, features, _ = chosen_ref.shape
    step = pl.program_id(0)
    part = sum(
        jnp.dot(
            prepared_ref[:, s * width + width - features : (s + 1) * width],
            chosen_ref[s],
            preferred_element_type=jnp.float32,
        )
        for s in range(sources)
    )

    @pl.when(step == 0)
    def _():
        out_ref[...] = total_ref[...] + part

    @pl.when(step > 0)
    def _():
        out_ref[...] += part

    @pl.when(step == pl.num_programs(0) - 1)
    def _():
        out_ref[...] *= scale


def score_all(prepared, chosen, total, width, scale):
    queries = prepared.shape[0]
    devices, features, entries = chosen.shape
    steps = 4
    whole = pl.BlockSpec((queries, entries), lambda i: (0, 0))
    return pl.pallas_call(
        lambda *refs: score_all_kernel(width, scale, *refs),
        grid=(steps,),
        in_specs=[
            pl.BlockSpec((queries, devices // steps * width), lambda i: (0, i)),
            pl.BlockSpec((devices // steps, features, entries), lambda i: (i, 0, 0)),
            whole,
        ],
        out_specs=whole,
        out_shape=jax.ShapeDtypeStruct((queries, entries), jnp.float32),
        compiler_params=pltpu.CompilerParams(vmem_limit_bytes=VMEM_BYTES),
        cost_estimate=pl.CostEstimate(
            flops=2 * devices * features * queries * entries,
            bytes_accessed=2 * devices * features * (queries + entries) + 8 * queries * entries,
            transcendentals=0,
        ),
    )(prepared, chosen, total)


def precondition(queries, left_inv, right_inv):
    total = queries.shape[0]
    k_out = left_inv.shape[1]
    k_in = right_inv.shape[1]
    block_size = k_out * k_in
    pieces = []
    for layer_index in range(left_inv.shape[0]):
        block = queries[:, layer_index * block_size : (layer_index + 1) * block_size].reshape(
            total, k_out, k_in
        )
        middle = jnp.einsum(
            "qij,jk->qik", block, right_inv[layer_index], preferred_element_type=jnp.float32
        ).astype(jnp.bfloat16)
        result = jnp.einsum(
            "ai,qik->qak", left_inv[layer_index], middle, preferred_element_type=jnp.float32
        ).astype(jnp.bfloat16)
        pieces.append(result.reshape(total, block_size))
    return jnp.concatenate(pieces, axis=1)


def on_device(doc_grads, query_grads, left_inv, right_inv, cand_owner, cand_row):
    devices = lax.axis_size("docs")
    half = devices // 2
    doc_count = doc_grads.shape[0] // devices
    entries = cand_row.shape[0]
    width = doc_grads.shape[1]
    queries, features = query_grads.shape

    def swap(values, k):
        return lax.ppermute(values, "docs", [(i, i ^ k) for i in range(devices)])

    head = width // 4 if width % (4 * LANES) == 0 else 0
    if head:
        own = doc_grads[:, :head].T
        far = swap(own, half)
    own_ids = cand_owner[:, 0] * doc_count + cand_row
    ids = lax.all_to_all(
        jnp.broadcast_to(own_ids, (devices, 1, entries)), "docs", split_axis=0, concat_axis=0, tiled=True
    )
    picked = gather_all(ids, doc_grads[:, head:].T)
    ids, query_grads, picked = lax.optimization_barrier((ids, query_grads, picked))
    chosen = lax.all_to_all(picked, "docs", split_axis=0, concat_axis=0, tiled=True)
    if head:
        me = lax.axis_index("docs").astype(jnp.int32).reshape(1)
        partners = list(range(half))
        pieces = gather_near(me, ids, own, far, partners)
        query_grads, pieces = lax.optimization_barrier((query_grads, pieces))
        near = [piece if k == 0 else swap(piece, k) for k, piece in zip(partners, pieces)]
    prepared = precondition(query_grads, left_inv, right_inv)
    if head:
        total = score_near(me, prepared, near, partners, half, width)
    else:
        total = jnp.zeros((queries, entries), jnp.float32)
    return score_all(prepared, chosen, total, width, features ** (-0.5))


def solution(mesh):
    placed = (
        P("parts", "docs"),
        P(("parts", "docs"), None),
        P(),
        P(),
        P(("parts", "docs"), None),
        P(("parts", "docs")),
    )
    return jax.shard_map(
        on_device, mesh=mesh, in_specs=placed, out_specs=P(("parts", "docs"), None), check_vma=False
    )
```

```python
import jax
import jax.numpy as jnp
from jax import lax
from jax.experimental import pallas as pl
from jax.experimental.pallas import tpu as pltpu
from jax.sharding import PartitionSpec as P

LANES = 128
SUBLANES = 8
MXU = 256
VMEM_BYTES = 48 << 20


def call(kernel, out_shape, grid, in_specs, out_specs, flops, bytes_accessed, scratch=(), prefetch=0):
    return pl.pallas_call(
        kernel,
        grid_spec=pltpu.PrefetchScalarGridSpec(
            num_scalar_prefetch=prefetch,
            grid=grid,
            in_specs=in_specs,
            out_specs=out_specs,
            scratch_shapes=scratch,
        ),
        out_shape=out_shape,
        compiler_params=pltpu.CompilerParams(vmem_limit_bytes=VMEM_BYTES),
        cost_estimate=pl.CostEstimate(flops=flops, bytes_accessed=bytes_accessed, transcendentals=0),
    )


def dot(a, b):
    return jnp.dot(a, b, preferred_element_type=jnp.float32)


def one_hot(ids, docs):
    group, row = ids // LANES, ids % LANES
    in_group = (lax.broadcasted_iota(jnp.int32, (LANES, ids.shape[1]), 0) == row).astype(jnp.bfloat16)
    return jnp.concatenate(
        [in_group * (group == g).astype(jnp.bfloat16) for g in range(docs // LANES)], axis=0
    )


def gather_rows(base, ids, tables, count):
    entries = ids.shape[2]
    docs = tables[0].shape[1]
    features = sum(t.shape[0] for t in tables)

    def kernel(base_ref, ids_ref, *refs):
        out_ref = refs[-1]
        hot = one_hot(ids_ref[0], docs)
        start = 0
        for table_ref in refs[:-1]:
            stop = start + table_ref.shape[0]
            out_ref[0, start:stop, :] = dot(table_ref[...], hot).astype(out_ref.dtype)
            start = stop

    return call(
        kernel,
        jax.ShapeDtypeStruct((count, features, entries), tables[0].dtype),
        (count,),
        [pl.BlockSpec((1, 1, entries), lambda b, base: (base[0] + b, 0, 0))]
        + [pl.BlockSpec(t.shape, lambda b, base: (0, 0)) for t in tables],
        pl.BlockSpec((1, features, entries), lambda b, base: (b, 0, 0)),
        1000,
        1000,
        prefetch=1,
    )(base, ids, *tables)


def gather_pieces(me, ids, table, partners):
    entries = ids.shape[2]
    features, docs = table.shape
    count = len(partners)

    def kernel(me_ref, *refs):
        table_ref = refs[count]
        for ids_ref, out_ref in zip(refs[:count], refs[count + 1 :]):
            out_ref[...] = dot(table_ref[...], one_hot(ids_ref[0], docs)).astype(out_ref.dtype)

    return call(
        kernel,
        [jax.ShapeDtypeStruct((features, entries), table.dtype)] * count,
        (1,),
        [pl.BlockSpec((1, 1, entries), lambda i, me, k=k: (me[0] ^ k, 0, 0)) for k in partners]
        + [pl.BlockSpec((features, docs), lambda i, me: (0, 0))],
        [pl.BlockSpec((features, entries), lambda i, me: (0, 0))] * count,
        1000,
        1000,
        prefetch=1,
    )(me, *[ids] * count, table)


def score_near(base, prepared, chosen, width, half):
    queries = prepared.shape[0]
    count, features, entries = chosen.shape
    head = features - width
    stride = width // head

    def kernel(base_ref, own_ref, far_ref, chosen_ref, out_ref):
        part = dot(own_ref[...], chosen_ref[0, :width, :]) + dot(far_ref[...], chosen_ref[0, width:, :])

        @pl.when(pl.program_id(0) == 0)
        def _():
            out_ref[...] = part

        @pl.when(pl.program_id(0) > 0)
        def _():
            out_ref[...] += part

    return call(
        kernel,
        jax.ShapeDtypeStruct((queries, entries), jnp.float32),
        (count,),
        [
            pl.BlockSpec((queries, width), lambda j, base: (0, base[0] + j)),
            pl.BlockSpec((queries, head), lambda j, base: (0, ((base[0] + j) ^ half) * stride)),
            pl.BlockSpec((1, features, entries), lambda j, base: (j, 0, 0)),
        ],
        pl.BlockSpec((queries, entries), lambda j, base: (0, 0)),
        2 * count * features * queries * entries,
        2 * count * features * (queries + entries) + 4 * queries * entries,
        prefetch=1,
    )(base, prepared, prepared, chosen)


def score_pieces(me, prepared, chosen, partners, total, width, scale):
    queries = prepared.shape[0]
    features, entries = chosen[0].shape
    count = len(partners)
    whole = pl.BlockSpec((queries, entries), lambda i, me: (0, 0))

    def kernel(me_ref, *refs):
        out = refs[-2][...]
        for prepared_ref, chosen_ref in zip(refs[:count], refs[count : 2 * count]):
            out = out + dot(prepared_ref[:, width - features :], chosen_ref[...])
        refs[-1][...] = out * scale

    return call(
        kernel,
        jax.ShapeDtypeStruct((queries, entries), jnp.float32),
        (1,),
        [pl.BlockSpec((queries, width), lambda i, me, k=k: (0, me[0] ^ k)) for k in partners]
        + [pl.BlockSpec((features, entries), lambda i, me: (0, 0))] * count
        + [whole],
        whole,
        2 * count * features * queries * entries,
        2 * count * features * (queries + entries) + 8 * queries * entries,
        prefetch=1,
    )(me, *[prepared] * count, *chosen, total)


def score_all(prepared, chosen, scale):
    queries = prepared.shape[0]
    devices, width, entries = chosen.shape

    def kernel(prepared_ref, chosen_ref, out_ref):
        part = dot(prepared_ref[...], chosen_ref[...]) * scale

        @pl.when(pl.program_id(0) == 0)
        def _():
            out_ref[...] = part

        @pl.when(pl.program_id(0) > 0)
        def _():
            out_ref[...] += part

    steps = 4
    block = devices * width // steps
    return call(
        kernel,
        jax.ShapeDtypeStruct((queries, entries), jnp.float32),
        (steps,),
        [
            pl.BlockSpec((queries, block), lambda i: (0, i)),
            pl.BlockSpec((block, entries), lambda i: (i, 0)),
        ],
        pl.BlockSpec((queries, entries), lambda i: (0, 0)),
        2 * devices * width * queries * entries,
        2 * devices * width * (queries + entries) + 4 * queries * entries,
    )(prepared, chosen.reshape(devices * width, entries))


def precondition(queries, left_inv, right_inv):
    total, features = queries.shape
    layers, k_out, _ = left_inv.shape
    k_in = right_inv.shape[1]
    group = MXU // k_out
    pair = MXU // k_in
    left = jnp.einsum("lai,rs->laris", left_inv, jnp.eye(group, dtype=left_inv.dtype)).reshape(
        layers, MXU, MXU
    )
    right = jnp.einsum("rs,ljk->lrjsk", jnp.eye(pair, dtype=right_inv.dtype), right_inv).reshape(
        layers, MXU, MXU
    )
    rows = 64
    wide = k_out // pair
    both = 2 * group

    def kernel(queries_ref, left_ref, right_ref, out_ref, middle_ref):
        for layer in range(layers):
            first = layer * k_out * k_in
            stack = jnp.concatenate(
                [queries_ref[:, first + p * MXU : first + (p + 1) * MXU] for p in range(wide)], axis=0
            )
            middle_ref[...] = dot(stack, right_ref[layer])
            for q in range(0, rows, both):
                halves = []
                for start in (q, q + group):
                    tiles = []
                    for p in range(wide):
                        at = p * rows + start
                        for s in range(pair):
                            tiles.append(middle_ref[at : at + group, s * k_in : (s + 1) * k_in])
                    halves.append(jnp.concatenate(tiles, axis=0))
                middle = jnp.concatenate(halves, axis=1).astype(queries_ref.dtype)
                result = dot(left_ref[layer], middle)
                for a in range(k_out):
                    at = a * group
                    tile = jnp.concatenate(
                        [result[at : at + group, :k_in], result[at : at + group, k_in:]], axis=0
                    )
                    lanes = first + a * k_in
                    out_ref[q : q + both, lanes : lanes + k_in] = tile.astype(out_ref.dtype)

    square = pl.BlockSpec((layers, MXU, MXU), lambda i: (0, 0, 0))
    return call(
        kernel,
        jax.ShapeDtypeStruct(queries.shape, queries.dtype),
        (total // rows,),
        [pl.BlockSpec((rows, features), lambda i: (i, 0)), square, square],
        pl.BlockSpec((rows, features), lambda i: (i, 0)),
        4 * total * features * MXU,
        4 * total * features,
        scratch=[pltpu.VMEM((wide * rows, MXU), jnp.float32)],
    )(queries, left, right)


def on_device(doc_grads, query_grads, left_inv, right_inv, cand_owner, cand_row):
    devices = lax.axis_size("docs")
    half = devices // 2
    me = lax.axis_index("docs").astype(jnp.int32).reshape(1)
    base = me & -half
    doc_count = doc_grads.shape[0] // devices
    entries = cand_row.shape[0]
    width = doc_grads.shape[1]
    scale = query_grads.shape[1] ** (-0.5)

    def swap(values, k):
        return lax.ppermute(values, "docs", [(i, i ^ k) for i in range(devices)])

    head = width // 4 if width % (4 * LANES) == 0 else 0
    if head:
        across = swap(doc_grads[:, :head], half)
    own_ids = cand_owner[:, 0] * doc_count + cand_row
    ids = lax.all_to_all(
        jnp.broadcast_to(own_ids, (devices, 1, entries)), "docs", split_axis=0, concat_axis=0, tiled=True
    )
    table = doc_grads.T
    if not head:
        picked = gather_rows(jnp.zeros((1,), jnp.int32), ids, [table], devices)
        chosen = lax.all_to_all(picked, "docs", split_axis=0, concat_axis=0, tiled=True)
        return score_all(precondition(query_grads, left_inv, right_inv), chosen, scale)

    partners = list(range(half, devices))
    body = table[head:]
    first = gather_pieces(me, ids, body, partners[:2])
    ids, first = lax.optimization_barrier((ids, first))
    rest = gather_pieces(me, ids, body, partners[2:])
    ids, rest = lax.optimization_barrier((ids, rest))
    far = [swap(piece, k) for piece, k in zip([*first, *rest], partners)]
    picked = gather_rows(base, ids, [table, across.T], half)
    query_grads, picked = lax.optimization_barrier((query_grads, picked))
    groups = [list(range(half)), list(range(half, devices))]
    near = lax.all_to_all(
        picked, "docs", split_axis=0, concat_axis=0, axis_index_groups=groups, tiled=True
    )
    prepared = precondition(query_grads, left_inv, right_inv)
    total = score_near(base, prepared, near, width, half)
    last = half - 2
    total = score_pieces(me, prepared, far[:last], partners[:last], total, width, 1.0)
    return score_pieces(me, prepared, far[last:], partners[last:], total, width, scale)


def solution(mesh):
    placed = (
        P("parts", "docs"),
        P(("parts", "docs"), None),
        P(),
        P(),
        P(("parts", "docs"), None),
        P(("parts", "docs")),
    )
    return jax.shard_map(
        on_device, mesh=mesh, in_specs=placed, out_specs=P(("parts", "docs"), None), check_vma=False
    )
```

```python
import jax
import jax.numpy as jnp
from jax import lax
from jax.experimental import pallas as pl
from jax.experimental.pallas import tpu as pltpu
from jax.sharding import PartitionSpec as P

LANES = 128
SUBLANES = 8
MXU = 256
VMEM_BYTES = 48 << 20


def call(kernel, out_shape, grid, in_specs, out_specs, flops, bytes_accessed, scratch=(), prefetch=0):
    return pl.pallas_call(
        kernel,
        grid_spec=pltpu.PrefetchScalarGridSpec(
            num_scalar_prefetch=prefetch,
            grid=grid,
            in_specs=in_specs,
            out_specs=out_specs,
            scratch_shapes=scratch,
        ),
        out_shape=out_shape,
        compiler_params=pltpu.CompilerParams(vmem_limit_bytes=VMEM_BYTES),
        cost_estimate=pl.CostEstimate(flops=flops, bytes_accessed=bytes_accessed, transcendentals=0),
    )


def dot(a, b):
    return jnp.dot(a, b, preferred_element_type=jnp.float32)


def one_hot(ids, docs):
    group, row = ids // LANES, ids % LANES
    in_group = (lax.broadcasted_iota(jnp.int32, (LANES, ids.shape[1]), 0) == row).astype(jnp.bfloat16)
    return jnp.concatenate(
        [in_group * (group == g).astype(jnp.bfloat16) for g in range(docs // LANES)], axis=0
    )


def gather_rows(base, ids, tables, count):
    entries = ids.shape[2]
    docs = tables[0].shape[1]
    features = sum(t.shape[0] for t in tables)

    def kernel(base_ref, ids_ref, *refs):
        out_ref = refs[-1]
        hot = one_hot(ids_ref[0], docs)
        start = 0
        for table_ref in refs[:-1]:
            stop = start + table_ref.shape[0]
            out_ref[0, start:stop, :] = dot(table_ref[...], hot).astype(out_ref.dtype)
            start = stop

    return call(
        kernel,
        pltpu.HBM((count, features, entries), tables[0].dtype),
        (count,),
        [pl.BlockSpec((1, 1, entries), lambda b, base: (base[0] + b, 0, 0))]
        + [pl.BlockSpec(t.shape, lambda b, base: (0, 0)) for t in tables],
        pl.BlockSpec((1, features, entries), lambda b, base: (b, 0, 0)),
        1000,
        1000,
        prefetch=1,
    )(base, ids, *tables)


def gather_pieces(me, ids, table, partners):
    entries = ids.shape[2]
    features, docs = table.shape
    count = len(partners)

    def kernel(me_ref, *refs):
        table_ref = refs[count]
        for ids_ref, out_ref in zip(refs[:count], refs[count + 1 :]):
            out_ref[...] = dot(table_ref[...], one_hot(ids_ref[0], docs)).astype(out_ref.dtype)

    return call(
        kernel,
        [pltpu.HBM((features, entries), table.dtype)] * count,
        (1,),
        [pl.BlockSpec((1, 1, entries), lambda i, me, k=k: (me[0] ^ k, 0, 0)) for k in partners]
        + [pl.BlockSpec((features, docs), lambda i, me: (0, 0))],
        [pl.BlockSpec((features, entries), lambda i, me: (0, 0))] * count,
        1000,
        1000,
        prefetch=1,
    )(me, *[ids] * count, table)


def score_near(base, prepared, chosen):
    queries = prepared.shape[0]
    count, width, entries = chosen.shape

    def kernel(base_ref, prepared_ref, chosen_ref, out_ref):
        part = dot(prepared_ref[...], chosen_ref[0])

        @pl.when(pl.program_id(0) == 0)
        def _():
            out_ref[...] = part

        @pl.when(pl.program_id(0) > 0)
        def _():
            out_ref[...] += part

    return call(
        kernel,
        jax.ShapeDtypeStruct((queries, entries), jnp.float32),
        (count,),
        [
            pl.BlockSpec((queries, width), lambda j, base: (0, base[0] + j)),
            pl.BlockSpec((1, width, entries), lambda j, base: (j, 0, 0)),
        ],
        pl.BlockSpec((queries, entries), lambda j, base: (0, 0)),
        2 * count * width * queries * entries,
        2 * count * width * (queries + entries) + 4 * queries * entries,
        prefetch=1,
    )(base, prepared, chosen)


def score_pieces(me, prepared, chosen, partners, total, scale):
    queries = prepared.shape[0]
    width, entries = chosen[0].shape
    count = len(partners)
    whole = pl.BlockSpec((queries, entries), lambda i, me: (0, 0))

    def kernel(me_ref, *refs):
        out = refs[-2][...]
        for prepared_ref, chosen_ref in zip(refs[:count], refs[count : 2 * count]):
            out = out + dot(prepared_ref[...], chosen_ref[...])
        refs[-1][...] = out * scale

    return call(
        kernel,
        jax.ShapeDtypeStruct((queries, entries), jnp.float32),
        (1,),
        [pl.BlockSpec((queries, width), lambda i, me, k=k: (0, me[0] ^ k)) for k in partners]
        + [pl.BlockSpec((width, entries), lambda i, me: (0, 0))] * count
        + [whole],
        whole,
        2 * count * width * queries * entries,
        2 * count * width * (queries + entries) + 8 * queries * entries,
        prefetch=1,
    )(me, *[prepared] * count, *chosen, total)


def score_all(prepared, chosen, scale):
    queries = prepared.shape[0]
    devices, width, entries = chosen.shape

    def kernel(prepared_ref, chosen_ref, out_ref):
        part = dot(prepared_ref[...], chosen_ref[...]) * scale

        @pl.when(pl.program_id(0) == 0)
        def _():
            out_ref[...] = part

        @pl.when(pl.program_id(0) > 0)
        def _():
            out_ref[...] += part

    steps = 4
    block = devices * width // steps
    return call(
        kernel,
        jax.ShapeDtypeStruct((queries, entries), jnp.float32),
        (steps,),
        [
            pl.BlockSpec((queries, block), lambda i: (0, i)),
            pl.BlockSpec((block, entries), lambda i: (i, 0)),
        ],
        pl.BlockSpec((queries, entries), lambda i: (0, 0)),
        2 * devices * width * queries * entries,
        2 * devices * width * (queries + entries) + 4 * queries * entries,
    )(prepared, chosen.reshape(devices * width, entries))


def precondition(queries, left_inv, right_inv):
    total, features = queries.shape
    layers, k_out, _ = left_inv.shape
    k_in = right_inv.shape[1]
    group = MXU // k_out
    pair = MXU // k_in
    rows = 64
    wide = k_out // pair
    both = 2 * group

    def spread(values, times):
        size = values.shape[0]
        rows = lax.broadcasted_iota(jnp.int32, (MXU, size), 0) // times
        picks = (rows == lax.broadcasted_iota(jnp.int32, (MXU, size), 1)).astype(values.dtype)
        wide = dot(picks, values).astype(values.dtype)
        wide = lax.dot_general(
            wide, picks, (((1,), (1,)), ((), ())), preferred_element_type=jnp.float32
        )
        row = lax.broadcasted_iota(jnp.int32, (MXU, MXU), 0) % times
        column = lax.broadcasted_iota(jnp.int32, (MXU, MXU), 1) % times
        return jnp.where(row == column, wide, 0.0).astype(values.dtype)

    def repeat(values, times):
        empty = jnp.zeros_like(values)
        return jnp.concatenate(
            [
                jnp.concatenate([values if i == j else empty for j in range(times)], axis=1)
                for i in range(times)
            ],
            axis=0,
        )

    def kernel(queries_ref, left_inv_ref, right_inv_ref, out_ref, middle_ref, left_ref, right_ref):
        @pl.when(pl.program_id(0) == 0)
        def _():
            for layer in range(layers):
                left_ref[layer] = spread(left_inv_ref[layer], group)
                right_ref[layer] = repeat(right_inv_ref[layer], pair)

        for layer in range(layers):
            first = layer * k_out * k_in
            stack = jnp.concatenate(
                [queries_ref[:, first + p * MXU : first + (p + 1) * MXU] for p in range(wide)], axis=0
            )
            middle_ref[...] = dot(stack, right_ref[layer])
            for q in range(0, rows, both):
                halves = []
                for start in (q, q + group):
                    tiles = []
                    for p in range(wide):
                        at = p * rows + start
                        for s in range(pair):
                            tiles.append(middle_ref[at : at + group, s * k_in : (s + 1) * k_in])
                    halves.append(jnp.concatenate(tiles, axis=0))
                middle = jnp.concatenate(halves, axis=1).astype(queries_ref.dtype)
                result = dot(left_ref[layer], middle)
                for a in range(k_out):
                    at = a * group
                    tile = jnp.concatenate(
                        [result[at : at + group, :k_in], result[at : at + group, k_in:]], axis=0
                    )
                    lanes = first + a * k_in
                    out_ref[q : q + both, lanes : lanes + k_in] = tile.astype(out_ref.dtype)

    return call(
        kernel,
        jax.ShapeDtypeStruct(queries.shape, queries.dtype),
        (total // rows,),
        [
            pl.BlockSpec((rows, features), lambda i: (i, 0)),
            pl.BlockSpec(left_inv.shape, lambda i: (0, 0, 0)),
            pl.BlockSpec(right_inv.shape, lambda i: (0, 0, 0)),
        ],
        pl.BlockSpec((rows, features), lambda i: (i, 0)),
        4 * total * features * MXU,
        4 * total * features,
        scratch=[
            pltpu.VMEM((wide * rows, MXU), jnp.float32),
            pltpu.VMEM((layers, MXU, MXU), left_inv.dtype),
            pltpu.VMEM((layers, MXU, MXU), right_inv.dtype),
        ],
    )(queries, left_inv, right_inv)


def after(value, *earlier):
    return lax.optimization_barrier((value, *earlier))[0]


def on_device(doc_grads, query_grads, left_inv, right_inv, cand_owner, cand_row):
    devices = lax.axis_size("docs")
    half = devices // 2
    me = lax.axis_index("docs").astype(jnp.int32).reshape(1)
    base = me & -half
    doc_count = doc_grads.shape[0] // devices
    entries = cand_row.shape[0]
    width = doc_grads.shape[1]
    scale = query_grads.shape[1] ** (-0.5)

    def swap(values, k):
        return lax.ppermute(values, "docs", [(i, i ^ k) for i in range(devices)])

    own_ids = cand_owner[:, 0] * doc_count + cand_row
    ids = lax.all_to_all(
        jnp.broadcast_to(own_ids, (devices, 1, entries)), "docs", split_axis=0, concat_axis=0, tiled=True
    )
    table = doc_grads.T
    if width % (4 * LANES):
        picked = gather_rows(jnp.zeros((1,), jnp.int32), ids, [table], devices)
        chosen = lax.all_to_all(picked, "docs", split_axis=0, concat_axis=0, tiled=True)
        return score_all(precondition(query_grads, left_inv, right_inv), chosen, scale)

    partners = list(range(half, devices))
    far = [
        swap(piece, k)
        for piece, k in zip(gather_pieces(me, ids, table, partners[:2]), partners[:2])
    ]
    ids = after(ids, far[0])
    far += [
        swap(piece, k)
        for piece, k in zip(gather_pieces(me, ids, table, partners[2:]), partners[2:])
    ]
    ids = after(ids, far[1])
    picked = gather_rows(base, ids, [table], half)
    near = lax.all_to_all(
        picked,
        "docs",
        split_axis=0,
        concat_axis=0,
        axis_index_groups=[list(range(half)), list(range(half, devices))],
        tiled=True,
    )
    prepared = precondition(after(query_grads, picked, far[2]), left_inv, right_inv)
    total = score_near(base, prepared, near)
    middle = half // 2
    total = score_pieces(me, prepared, far[:middle], partners[:middle], total, 1.0)
    return score_pieces(me, prepared, far[middle:], partners[middle:], total, scale)


def solution(mesh):
    placed = (
        P("parts", "docs"),
        P(("parts", "docs"), None),
        P(),
        P(),
        P(("parts", "docs"), None),
        P(("parts", "docs")),
    )
    return jax.shard_map(
        on_device, mesh=mesh, in_specs=placed, out_specs=P(("parts", "docs"), None), check_vma=False
    )
```

```python
import jax
import jax.numpy as jnp
from jax import lax
from jax.experimental import pallas as pl
from jax.experimental.pallas import tpu as pltpu
from jax.sharding import PartitionSpec as P

LANES = 128
SUBLANES = 8
MXU = 256
VMEM_BYTES = 48 << 20


def call(kernel, out_shape, grid, in_specs, out_specs, flops, bytes_accessed, scratch=(), prefetch=0):
    return pl.pallas_call(
        kernel,
        grid_spec=pltpu.PrefetchScalarGridSpec(
            num_scalar_prefetch=prefetch,
            grid=grid,
            in_specs=in_specs,
            out_specs=out_specs,
            scratch_shapes=scratch,
        ),
        out_shape=out_shape,
        compiler_params=pltpu.CompilerParams(vmem_limit_bytes=VMEM_BYTES),
        cost_estimate=pl.CostEstimate(flops=flops, bytes_accessed=bytes_accessed, transcendentals=0),
    )


def dot(a, b):
    return jnp.dot(a, b, preferred_element_type=jnp.float32)


def one_hot(ids, docs):
    group, row = ids // LANES, ids % LANES
    in_group = (lax.broadcasted_iota(jnp.int32, (LANES, ids.shape[1]), 0) == row).astype(jnp.bfloat16)
    return jnp.concatenate(
        [in_group * (group == g).astype(jnp.bfloat16) for g in range(docs // LANES)], axis=0
    )


def gather_rows(base, ids, tables, count):
    entries = ids.shape[2]
    docs = tables[0].shape[1]
    features = sum(t.shape[0] for t in tables)

    def kernel(base_ref, ids_ref, *refs):
        out_ref = refs[-1]
        hot = one_hot(ids_ref[0], docs)
        start = 0
        for table_ref in refs[:-1]:
            stop = start + table_ref.shape[0]
            out_ref[0, start:stop, :] = dot(table_ref[...], hot).astype(out_ref.dtype)
            start = stop

    return call(
        kernel,
        pltpu.HBM((count, features, entries), tables[0].dtype),
        (count,),
        [pl.BlockSpec((1, 1, entries), lambda b, base: (base[0] + b, 0, 0))]
        + [pl.BlockSpec(t.shape, lambda b, base: (0, 0)) for t in tables],
        pl.BlockSpec((1, features, entries), lambda b, base: (b, 0, 0)),
        1000,
        1000,
        prefetch=1,
    )(base, ids, *tables)


def gather_pieces(me, ids, table, partners):
    entries = ids.shape[2]
    features, docs = table.shape
    count = len(partners)

    def kernel(me_ref, *refs):
        table_ref = refs[count]
        for ids_ref, out_ref in zip(refs[:count], refs[count + 1 :]):
            out_ref[...] = dot(table_ref[...], one_hot(ids_ref[0], docs)).astype(out_ref.dtype)

    return call(
        kernel,
        [pltpu.HBM((features, entries), table.dtype)] * count,
        (1,),
        [pl.BlockSpec((1, 1, entries), lambda i, me, k=k: (me[0] ^ k, 0, 0)) for k in partners]
        + [pl.BlockSpec((features, docs), lambda i, me: (0, 0))],
        [pl.BlockSpec((features, entries), lambda i, me: (0, 0))] * count,
        1000,
        1000,
        prefetch=1,
    )(me, *[ids] * count, table)


def padded(values, above, below):
    zeros = lambda rows: [jnp.zeros((rows, values.shape[1]), values.dtype)] if rows else []
    return jnp.concatenate([*zeros(above), values, *zeros(below)], axis=0)


def score_near(base, prepared, chosen, width, half):
    queries = prepared.shape[0]
    count, features, entries = chosen.shape
    tail = features - width
    block = max(tail, LANES)
    stride = width // block

    def kernel(base_ref, own_ref, far_ref, chosen_ref, out_ref):
        part = dot(own_ref[...], chosen_ref[0, :width, :])
        part += dot(far_ref[...], padded(chosen_ref[0, width:, :], block - tail, 0))

        @pl.when(pl.program_id(0) == 0)
        def _():
            out_ref[...] = part

        @pl.when(pl.program_id(0) > 0)
        def _():
            out_ref[...] += part

    return call(
        kernel,
        jax.ShapeDtypeStruct((queries, entries), jnp.float32),
        (count,),
        [
            pl.BlockSpec((queries, width), lambda j, base: (0, base[0] + j)),
            pl.BlockSpec(
                (queries, block), lambda j, base: (0, ((base[0] + j) ^ half) * stride + stride - 1)
            ),
            pl.BlockSpec((1, features, entries), lambda j, base: (j, 0, 0)),
        ],
        pl.BlockSpec((queries, entries), lambda j, base: (0, 0)),
        2 * count * features * queries * entries,
        2 * count * features * (queries + entries) + 4 * queries * entries,
        prefetch=1,
    )(base, prepared, prepared, chosen)


def score_pieces(me, prepared, chosen, partners, total, width, scale):
    queries = prepared.shape[0]
    features, entries = chosen[0].shape
    count = len(partners)
    whole = pl.BlockSpec((queries, entries), lambda i, me: (0, 0))

    def kernel(me_ref, *refs):
        out = refs[-2][...]
        for prepared_ref, chosen_ref in zip(refs[:count], refs[count : 2 * count]):
            out = out + dot(prepared_ref[...], padded(chosen_ref[...], 0, width - features))
        refs[-1][...] = out * scale

    return call(
        kernel,
        jax.ShapeDtypeStruct((queries, entries), jnp.float32),
        (1,),
        [pl.BlockSpec((queries, width), lambda i, me, k=k: (0, me[0] ^ k)) for k in partners]
        + [pl.BlockSpec((features, entries), lambda i, me: (0, 0))] * count
        + [whole],
        whole,
        2 * count * width * queries * entries,
        2 * count * width * (queries + entries) + 8 * queries * entries,
        prefetch=1,
    )(me, *[prepared] * count, *chosen, total)


def score_all(prepared, chosen, scale):
    queries = prepared.shape[0]
    devices, width, entries = chosen.shape

    def kernel(prepared_ref, chosen_ref, out_ref):
        part = dot(prepared_ref[...], chosen_ref[...]) * scale

        @pl.when(pl.program_id(0) == 0)
        def _():
            out_ref[...] = part

        @pl.when(pl.program_id(0) > 0)
        def _():
            out_ref[...] += part

    steps = 4
    block = devices * width // steps
    return call(
        kernel,
        jax.ShapeDtypeStruct((queries, entries), jnp.float32),
        (steps,),
        [
            pl.BlockSpec((queries, block), lambda i: (0, i)),
            pl.BlockSpec((block, entries), lambda i: (i, 0)),
        ],
        pl.BlockSpec((queries, entries), lambda i: (0, 0)),
        2 * devices * width * queries * entries,
        2 * devices * width * (queries + entries) + 4 * queries * entries,
    )(prepared, chosen.reshape(devices * width, entries))


def precondition(queries, left_inv, right_inv):
    total, features = queries.shape
    layers, k_out, _ = left_inv.shape
    k_in = right_inv.shape[1]
    group = MXU // k_out
    pair = MXU // k_in
    rows = 64
    wide = k_out // pair
    both = 2 * group

    def spread(values, times):
        size = values.shape[0]
        rows = lax.broadcasted_iota(jnp.int32, (MXU, size), 0) // times
        picks = (rows == lax.broadcasted_iota(jnp.int32, (MXU, size), 1)).astype(values.dtype)
        wide = dot(picks, values).astype(values.dtype)
        wide = lax.dot_general(
            wide, picks, (((1,), (1,)), ((), ())), preferred_element_type=jnp.float32
        )
        row = lax.broadcasted_iota(jnp.int32, (MXU, MXU), 0) % times
        column = lax.broadcasted_iota(jnp.int32, (MXU, MXU), 1) % times
        return jnp.where(row == column, wide, 0.0).astype(values.dtype)

    def repeat(values, times):
        empty = jnp.zeros_like(values)
        return jnp.concatenate(
            [
                jnp.concatenate([values if i == j else empty for j in range(times)], axis=1)
                for i in range(times)
            ],
            axis=0,
        )

    def kernel(queries_ref, left_inv_ref, right_inv_ref, out_ref, middle_ref, left_ref, right_ref):
        @pl.when(pl.program_id(0) == 0)
        def _():
            for layer in range(layers):
                left_ref[layer] = spread(left_inv_ref[layer], group)
                right_ref[layer] = repeat(right_inv_ref[layer], pair)

        for layer in range(layers):
            first = layer * k_out * k_in
            stack = jnp.concatenate(
                [queries_ref[:, first + p * MXU : first + (p + 1) * MXU] for p in range(wide)], axis=0
            )
            middle_ref[...] = dot(stack, right_ref[layer])
            for q in range(0, rows, both):
                halves = []
                for start in (q, q + group):
                    tiles = []
                    for p in range(wide):
                        at = p * rows + start
                        for s in range(pair):
                            tiles.append(middle_ref[at : at + group, s * k_in : (s + 1) * k_in])
                    halves.append(jnp.concatenate(tiles, axis=0))
                middle = jnp.concatenate(halves, axis=1).astype(queries_ref.dtype)
                result = dot(left_ref[layer], middle)
                for a in range(k_out):
                    at = a * group
                    tile = jnp.concatenate(
                        [result[at : at + group, :k_in], result[at : at + group, k_in:]], axis=0
                    )
                    lanes = first + a * k_in
                    out_ref[q : q + both, lanes : lanes + k_in] = tile.astype(out_ref.dtype)

    return call(
        kernel,
        jax.ShapeDtypeStruct(queries.shape, queries.dtype),
        (total // rows,),
        [
            pl.BlockSpec((rows, features), lambda i: (i, 0)),
            pl.BlockSpec(left_inv.shape, lambda i: (0, 0, 0)),
            pl.BlockSpec(right_inv.shape, lambda i: (0, 0, 0)),
        ],
        pl.BlockSpec((rows, features), lambda i: (i, 0)),
        4 * total * features * MXU,
        4 * total * features,
        scratch=[
            pltpu.VMEM((wide * rows, MXU), jnp.float32),
            pltpu.VMEM((layers, MXU, MXU), left_inv.dtype),
            pltpu.VMEM((layers, MXU, MXU), right_inv.dtype),
        ],
    )(queries, left_inv, right_inv)


def after(value, *earlier):
    return lax.optimization_barrier((value, *earlier))[0]


def on_device(doc_grads, query_grads, left_inv, right_inv, cand_owner, cand_row):
    devices = lax.axis_size("docs")
    half = devices // 2
    me = lax.axis_index("docs").astype(jnp.int32).reshape(1)
    base = me & -half
    doc_count = doc_grads.shape[0] // devices
    entries = cand_row.shape[0]
    width = doc_grads.shape[1]
    scale = query_grads.shape[1] ** (-0.5)

    def swap(values, k):
        return lax.ppermute(values, "docs", [(i, i ^ k) for i in range(devices)])

    tail = width // 8 if width % (4 * LANES) == 0 else 0
    table = doc_grads.T
    if tail:
        across = swap(table[width - tail :], half)
    own_ids = cand_owner[:, 0] * doc_count + cand_row
    ids = lax.all_to_all(
        jnp.broadcast_to(own_ids, (devices, 1, entries)), "docs", split_axis=0, concat_axis=0, tiled=True
    )
    if not tail:
        picked = gather_rows(jnp.zeros((1,), jnp.int32), ids, [table], devices)
        chosen = lax.all_to_all(picked, "docs", split_axis=0, concat_axis=0, tiled=True)
        return score_all(precondition(query_grads, left_inv, right_inv), chosen, scale)

    ids = after(ids, across)
    partners = list(range(half, devices))
    pieces = gather_pieces(me, ids, table[: width - tail], partners)
    far = [swap(piece, k) for piece, k in zip(pieces, partners)]
    picked = gather_rows(base, after(ids, far[0]), [table, across], half)
    near = lax.all_to_all(
        picked,
        "docs",
        split_axis=0,
        concat_axis=0,
        axis_index_groups=[list(range(half)), list(range(half, devices))],
        tiled=True,
    )
    prepared = precondition(after(query_grads, picked), left_inv, right_inv)
    total = score_near(base, prepared, near, width, half)
    return score_pieces(me, prepared, far, partners, total, width, scale)


def solution(mesh):
    placed = (
        P("parts", "docs"),
        P(("parts", "docs"), None),
        P(),
        P(),
        P(("parts", "docs"), None),
        P(("parts", "docs")),
    )
    return jax.shard_map(
        on_device, mesh=mesh, in_specs=placed, out_specs=P(("parts", "docs"), None), check_vma=False
    )
```

```python
import jax
import jax.numpy as jnp
from jax import lax
from jax.experimental import pallas as pl
from jax.experimental.pallas import tpu as pltpu
from jax.sharding import PartitionSpec as P

LANES = 128
SUBLANES = 8
MXU = 256
VMEM_BYTES = 48 << 20


def call(kernel, out_shape, grid, in_specs, out_specs, flops, bytes_accessed, scratch=(), prefetch=0):
    return pl.pallas_call(
        kernel,
        grid_spec=pltpu.PrefetchScalarGridSpec(
            num_scalar_prefetch=prefetch,
            grid=grid,
            in_specs=in_specs,
            out_specs=out_specs,
            scratch_shapes=scratch,
        ),
        out_shape=out_shape,
        compiler_params=pltpu.CompilerParams(vmem_limit_bytes=VMEM_BYTES),
        cost_estimate=pl.CostEstimate(flops=flops, bytes_accessed=bytes_accessed, transcendentals=0),
    )


def dot(a, b):
    return jnp.dot(a, b, preferred_element_type=jnp.float32)


def one_hot(ids, docs):
    group, row = ids // LANES, ids % LANES
    in_group = (lax.broadcasted_iota(jnp.int32, (LANES, ids.shape[1]), 0) == row).astype(jnp.bfloat16)
    return jnp.concatenate(
        [in_group * (group == g).astype(jnp.bfloat16) for g in range(docs // LANES)], axis=0
    )


def gather_rows(base, ids, tables, count):
    entries = ids.shape[2]
    docs = tables[0].shape[1]
    features = sum(t.shape[0] for t in tables)

    def kernel(base_ref, ids_ref, *refs):
        out_ref = refs[-1]
        hot = one_hot(ids_ref[0], docs)
        start = 0
        for table_ref in refs[:-1]:
            stop = start + table_ref.shape[0]
            out_ref[0, start:stop, :] = dot(table_ref[...], hot).astype(out_ref.dtype)
            start = stop

    return call(
        kernel,
        pltpu.HBM((count, features, entries), tables[0].dtype),
        (count,),
        [pl.BlockSpec((1, 1, entries), lambda b, base: (base[0] + b, 0, 0))]
        + [pl.BlockSpec(t.shape, lambda b, base: (0, 0)) for t in tables],
        pl.BlockSpec((1, features, entries), lambda b, base: (b, 0, 0)),
        1000,
        1000,
        prefetch=1,
    )(base, ids, *tables)


def gather_pieces(me, ids, tables, partners):
    entries = ids.shape[2]
    docs = tables[0][0].shape[1]
    features = sum(rows for _, rows in tables)
    count = len(partners)

    def kernel(me_ref, *refs):
        table_refs = refs[count : count + len(tables)]
        for ids_ref, out_ref in zip(refs[:count], refs[count + len(tables) :]):
            hot = one_hot(ids_ref[0], docs)
            start = 0
            for table_ref in table_refs:
                stop = start + table_ref.shape[0]
                out_ref[start:stop, :] = dot(table_ref[...], hot).astype(out_ref.dtype)
                start = stop

    return call(
        kernel,
        [pltpu.HBM((features, entries), tables[0][0].dtype)] * count,
        (1,),
        [pl.BlockSpec((1, 1, entries), lambda i, me, k=k: (me[0] ^ k, 0, 0)) for k in partners]
        + [pl.BlockSpec((rows, docs), lambda i, me: (0, 0)) for _, rows in tables],
        [pl.BlockSpec((features, entries), lambda i, me: (0, 0))] * count,
        2 * count * features * docs * entries,
        2 * features * (docs + count * entries),
        prefetch=1,
    )(me, *[ids] * count, *[table for table, _ in tables])


def padded(values, above, below):
    zeros = lambda rows: [jnp.zeros((rows, values.shape[1]), values.dtype)] if rows else []
    return jnp.concatenate([*zeros(above), values, *zeros(below)], axis=0)


def score_pieces(me, prepared, far, near, total, width, half, scale):
    queries = prepared.shape[0]
    entries = next(iter({**far, **near}.values())).shape[1]
    prepared_specs, chosen, depth = [], [], 0
    for k, piece in far.items():
        prepared_specs.append(pl.BlockSpec((queries, width), lambda i, me, k=k: (0, me[0] ^ k)))
        chosen.append(piece)
        depth += piece.shape[0]
    for k, piece in near.items():
        tail = piece.shape[0] - width
        block = max(tail, LANES)
        stride = width // block
        prepared_specs.append(pl.BlockSpec((queries, width), lambda i, me, k=k: (0, me[0] ^ k)))
        prepared_specs.append(
            pl.BlockSpec(
                (queries, block), lambda i, me, k=k: (0, (me[0] ^ k ^ half) * stride + stride - 1)
            )
        )
        chosen.append(piece)
        depth += piece.shape[0]
    totals = [] if total is None else [total]
    whole = pl.BlockSpec((queries, entries), lambda i, me: (0, 0))

    def kernel(me_ref, *refs):
        prepared_refs = iter(refs[: len(prepared_specs)])
        chosen_refs = iter(refs[len(prepared_specs) : len(prepared_specs) + len(chosen)])
        parts = [ref[...] for ref in refs[len(prepared_specs) + len(chosen) : -1]]
        for _ in far:
            piece = next(chosen_refs)[...]
            parts.append(dot(next(prepared_refs)[...], padded(piece, 0, width - piece.shape[0])))
        for _ in near:
            piece = next(chosen_refs)[...]
            parts.append(dot(next(prepared_refs)[...], piece[:width]))
            rest = next(prepared_refs)[...]
            parts.append(dot(rest, padded(piece[width:], rest.shape[1] - piece.shape[0] + width, 0)))
        refs[-1][...] = sum(parts[1:], parts[0]) * scale

    return call(
        kernel,
        jax.ShapeDtypeStruct((queries, entries), jnp.float32),
        (1,),
        prepared_specs
        + [pl.BlockSpec(piece.shape, lambda i, me: (0, 0)) for piece in chosen]
        + [whole] * len(totals),
        whole,
        2 * queries * depth * entries,
        2 * depth * (queries + entries) + 8 * queries * entries,
        prefetch=1,
    )(me, *[prepared] * len(prepared_specs), *chosen, *totals)


def score_all(prepared, chosen, scale):
    queries = prepared.shape[0]
    devices, width, entries = chosen.shape

    def kernel(prepared_ref, chosen_ref, out_ref):
        part = dot(prepared_ref[...], chosen_ref[...]) * scale

        @pl.when(pl.program_id(0) == 0)
        def _():
            out_ref[...] = part

        @pl.when(pl.program_id(0) > 0)
        def _():
            out_ref[...] += part

    steps = 4
    block = devices * width // steps
    return call(
        kernel,
        jax.ShapeDtypeStruct((queries, entries), jnp.float32),
        (steps,),
        [
            pl.BlockSpec((queries, block), lambda i: (0, i)),
            pl.BlockSpec((block, entries), lambda i: (i, 0)),
        ],
        pl.BlockSpec((queries, entries), lambda i: (0, 0)),
        2 * devices * width * queries * entries,
        2 * devices * width * (queries + entries) + 4 * queries * entries,
    )(prepared, chosen.reshape(devices * width, entries))


def precondition(queries, left_inv, right_inv):
    total, features = queries.shape
    layers, k_out, _ = left_inv.shape
    k_in = right_inv.shape[1]
    group = MXU // k_out
    pair = MXU // k_in
    rows = 64
    wide = k_out // pair
    both = 2 * group

    def spread(values, times):
        size = values.shape[0]
        rows = lax.broadcasted_iota(jnp.int32, (MXU, size), 0) // times
        picks = (rows == lax.broadcasted_iota(jnp.int32, (MXU, size), 1)).astype(values.dtype)
        wide = dot(picks, values).astype(values.dtype)
        wide = lax.dot_general(
            wide, picks, (((1,), (1,)), ((), ())), preferred_element_type=jnp.float32
        )
        row = lax.broadcasted_iota(jnp.int32, (MXU, MXU), 0) % times
        column = lax.broadcasted_iota(jnp.int32, (MXU, MXU), 1) % times
        return jnp.where(row == column, wide, 0.0).astype(values.dtype)

    def repeat(values, times):
        empty = jnp.zeros_like(values)
        return jnp.concatenate(
            [
                jnp.concatenate([values if i == j else empty for j in range(times)], axis=1)
                for i in range(times)
            ],
            axis=0,
        )

    def kernel(queries_ref, left_inv_ref, right_inv_ref, out_ref, middle_ref, left_ref, right_ref):
        @pl.when(pl.program_id(0) == 0)
        def _():
            for layer in range(layers):
                left_ref[layer] = spread(left_inv_ref[layer], group)
                right_ref[layer] = repeat(right_inv_ref[layer], pair)

        for layer in range(layers):
            first = layer * k_out * k_in
            stack = jnp.concatenate(
                [queries_ref[:, first + p * MXU : first + (p + 1) * MXU] for p in range(wide)], axis=0
            )
            middle_ref[...] = dot(stack, right_ref[layer])
            for q in range(0, rows, both):
                halves = []
                for start in (q, q + group):
                    tiles = []
                    for p in range(wide):
                        at = p * rows + start
                        for s in range(pair):
                            tiles.append(middle_ref[at : at + group, s * k_in : (s + 1) * k_in])
                    halves.append(jnp.concatenate(tiles, axis=0))
                middle = jnp.concatenate(halves, axis=1).astype(queries_ref.dtype)
                result = dot(left_ref[layer], middle)
                for a in range(k_out):
                    at = a * group
                    tile = jnp.concatenate(
                        [result[at : at + group, :k_in], result[at : at + group, k_in:]], axis=0
                    )
                    lanes = first + a * k_in
                    out_ref[q : q + both, lanes : lanes + k_in] = tile.astype(out_ref.dtype)

    return call(
        kernel,
        jax.ShapeDtypeStruct(queries.shape, queries.dtype),
        (total // rows,),
        [
            pl.BlockSpec((rows, features), lambda i: (i, 0)),
            pl.BlockSpec(left_inv.shape, lambda i: (0, 0, 0)),
            pl.BlockSpec(right_inv.shape, lambda i: (0, 0, 0)),
        ],
        pl.BlockSpec((rows, features), lambda i: (i, 0)),
        4 * total * features * MXU,
        4 * total * features,
        scratch=[
            pltpu.VMEM((wide * rows, MXU), jnp.float32),
            pltpu.VMEM((layers, MXU, MXU), left_inv.dtype),
            pltpu.VMEM((layers, MXU, MXU), right_inv.dtype),
        ],
    )(queries, left_inv, right_inv)


def after(value, *earlier):
    return lax.optimization_barrier((value, *earlier))[0]


def on_device(doc_grads, query_grads, left_inv, right_inv, cand_owner, cand_row):
    devices = lax.axis_size("docs")
    half = devices // 2
    me = lax.axis_index("docs").astype(jnp.int32).reshape(1)
    base = me & -half
    doc_count = doc_grads.shape[0] // devices
    entries = cand_row.shape[0]
    width = doc_grads.shape[1]
    scale = query_grads.shape[1] ** (-0.5)

    def swap(values, k):
        return lax.ppermute(values, "docs", [(i, i ^ k) for i in range(devices)])

    tail = width // 8 if width % (4 * LANES) == 0 else 0
    table = doc_grads.T
    if tail:
        across = swap(table[width - tail :], half)
    own_ids = cand_owner[:, 0] * doc_count + cand_row
    ids = lax.all_to_all(
        jnp.broadcast_to(own_ids, (devices, 1, entries)), "docs", split_axis=0, concat_axis=0, tiled=True
    )
    if not tail:
        picked = gather_rows(jnp.zeros((1,), jnp.int32), ids, [table], devices)
        chosen = lax.all_to_all(picked, "docs", split_axis=0, concat_axis=0, tiled=True)
        return score_all(precondition(query_grads, left_inv, right_inv), chosen, scale)

    first, flight = 2, 5
    far = list(range(half, devices))
    near = [*range(half // 2, half), *range(half // 2 - 1, 0, -1)]
    inside = [0, *near]
    body = [(table, width - tail)]
    order = far[:first]
    rest = [far[first:-1], list(near)]
    while any(rest):
        order += [part.pop(0) for part in rest if part]
    order.append(far[-1])
    ids = after(ids, across)
    pieces = dict(zip(far, gather_pieces(me, ids, body, far[:first])))
    ids = after(ids, pieces[order[0]])
    pieces.update(zip(inside, gather_pieces(me, ids, [(table, width), (across, tail)], inside)))
    ids = after(ids, pieces[0])
    pieces.update(zip(far[first:], gather_pieces(me, ids, body, far[first:])))
    came = {0: pieces[0]}
    for position, k in enumerate(order):
        piece = pieces[k]
        if position >= first:
            before = [came[j] for j in order[:first]]
            if position >= flight + first:
                before = [came[order[position - flight]]]
            piece = after(piece, *before)
        came[k] = swap(piece, k)
    prepared = precondition(after(query_grads, came[order[first - 1]]), left_inv, right_inv)

    total = None
    stops = [0, len(order) - 5, len(order) - 1, len(order)]
    for start, stop in zip(stops, stops[1:]):
        keys = [*([0] if start == 0 else []), *order[start:stop]]
        total = score_pieces(
            me,
            prepared,
            {k: came[k] for k in keys if k >= half},
            {k: came[k] for k in keys if k < half},
            total,
            width,
            half,
            scale if stop == len(order) else 1.0,
        )
    return total


def solution(mesh):
    placed = (
        P("parts", "docs"),
        P(("parts", "docs"), None),
        P(),
        P(),
        P(("parts", "docs"), None),
        P(("parts", "docs")),
    )
    return jax.shard_map(
        on_device, mesh=mesh, in_specs=placed, out_specs=P(("parts", "docs"), None), check_vma=False
    )
```

```python
import jax
import jax.numpy as jnp
from jax import lax
from jax.experimental import pallas as pl
from jax.experimental.pallas import tpu as pltpu
from jax.sharding import PartitionSpec as P

LANES = 128
SUBLANES = 8
MXU = 256
VMEM_BYTES = 48 << 20


def call(kernel, out_shape, grid, in_specs, out_specs, flops, bytes_accessed, scratch=(), prefetch=0):
    return pl.pallas_call(
        kernel,
        grid_spec=pltpu.PrefetchScalarGridSpec(
            num_scalar_prefetch=prefetch,
            grid=grid,
            in_specs=in_specs,
            out_specs=out_specs,
            scratch_shapes=scratch,
        ),
        out_shape=out_shape,
        compiler_params=pltpu.CompilerParams(vmem_limit_bytes=VMEM_BYTES),
        cost_estimate=pl.CostEstimate(flops=flops, bytes_accessed=bytes_accessed, transcendentals=0),
    )


def dot(a, b):
    return jnp.dot(a, b, preferred_element_type=jnp.float32)


def one_hot(ids, docs):
    group, row = ids // LANES, ids % LANES
    in_group = (lax.broadcasted_iota(jnp.int32, (LANES, ids.shape[1]), 0) == row).astype(jnp.bfloat16)
    return jnp.concatenate(
        [in_group * (group == g).astype(jnp.bfloat16) for g in range(docs // LANES)], axis=0
    )


def prepare(doc_grads, owners, rows, devices, tail):
    docs, width = doc_grads.shape
    entries = rows.shape[0]
    doc_count = docs // devices
    block = max(tail, LANES)

    def kernel(docs_ref, owners_ref, rows_ref, tail_ref, ids_ref):
        tail_ref[...] = docs_ref[...].T[block - tail :, :]
        ids = owners_ref[...] * doc_count + rows_ref[...]
        ids_ref[...] = jnp.broadcast_to(ids[None], ids_ref.shape)

    return call(
        kernel,
        [
            pltpu.HBM((tail, docs), doc_grads.dtype),
            pltpu.HBM((devices, 1, entries), jnp.int32),
        ],
        (1,),
        [
            pl.BlockSpec((docs, block), lambda i: (0, width // block - 1)),
            pl.BlockSpec((1, entries), lambda i: (0, 0)),
            pl.BlockSpec((1, entries), lambda i: (0, 0)),
        ],
        [
            pl.BlockSpec((tail, docs), lambda i: (0, 0)),
            pl.BlockSpec((devices, 1, entries), lambda i: (0, 0, 0)),
        ],
        0,
        2 * docs * (block + tail),
    )(doc_grads, owners.reshape(1, entries), rows.reshape(1, entries))


def gather_rows(base, ids, tables, count):
    entries = ids.shape[2]
    docs = tables[0].shape[1]
    features = sum(t.shape[0] for t in tables)

    def kernel(base_ref, ids_ref, *refs):
        out_ref = refs[-1]
        hot = one_hot(ids_ref[0], docs)
        start = 0
        for table_ref in refs[:-1]:
            stop = start + table_ref.shape[0]
            out_ref[0, start:stop, :] = dot(table_ref[...], hot).astype(out_ref.dtype)
            start = stop

    return call(
        kernel,
        pltpu.HBM((count, features, entries), tables[0].dtype),
        (count,),
        [pl.BlockSpec((1, 1, entries), lambda b, base: (base[0] + b, 0, 0))]
        + [pl.BlockSpec(t.shape, lambda b, base: (0, 0)) for t in tables],
        pl.BlockSpec((1, features, entries), lambda b, base: (b, 0, 0)),
        1000,
        1000,
        prefetch=1,
    )(base, ids, *tables)


def gather_pieces(me, ids, tables, partners):
    entries = ids.shape[2]
    docs = tables[0][0].shape[1]
    features = sum(rows for _, rows in tables)
    count = len(partners)

    def kernel(me_ref, *refs):
        table_refs = refs[count : count + len(tables)]
        for ids_ref, out_ref in zip(refs[:count], refs[count + len(tables) :]):
            hot = one_hot(ids_ref[0], docs)
            start = 0
            for table_ref in table_refs:
                stop = start + table_ref.shape[0]
                out_ref[start:stop, :] = dot(table_ref[...], hot).astype(out_ref.dtype)
                start = stop

    return call(
        kernel,
        [pltpu.HBM((features, entries), tables[0][0].dtype)] * count,
        (1,),
        [pl.BlockSpec((1, 1, entries), lambda i, me, k=k: (me[0] ^ k, 0, 0)) for k in partners]
        + [pl.BlockSpec((rows, docs), lambda i, me: (0, 0)) for _, rows in tables],
        [pl.BlockSpec((features, entries), lambda i, me: (0, 0))] * count,
        2 * count * features * docs * entries,
        2 * features * (docs + count * entries),
        prefetch=1,
    )(me, *[ids] * count, *[table for table, _ in tables])


def padded(values, above, below):
    zeros = lambda rows: [jnp.zeros((rows, values.shape[1]), values.dtype)] if rows else []
    return jnp.concatenate([*zeros(above), values, *zeros(below)], axis=0)


def score_pieces(me, prepared, far, near, total, width, half, scale):
    queries = prepared.shape[0]
    entries = next(iter({**far, **near}.values())).shape[1]
    prepared_specs, chosen, depth = [], [], 0
    for k, piece in far.items():
        prepared_specs.append(pl.BlockSpec((queries, width), lambda i, me, k=k: (0, me[0] ^ k)))
        chosen.append(piece)
        depth += piece.shape[0]
    for k, piece in near.items():
        tail = piece.shape[0] - width
        block = max(tail, LANES)
        stride = width // block
        prepared_specs.append(pl.BlockSpec((queries, width), lambda i, me, k=k: (0, me[0] ^ k)))
        prepared_specs.append(
            pl.BlockSpec(
                (queries, block), lambda i, me, k=k: (0, (me[0] ^ k ^ half) * stride + stride - 1)
            )
        )
        chosen.append(piece)
        depth += piece.shape[0]
    totals = [] if total is None else [total]
    whole = pl.BlockSpec((queries, entries), lambda i, me: (0, 0))

    def kernel(me_ref, *refs):
        prepared_refs = iter(refs[: len(prepared_specs)])
        chosen_refs = iter(refs[len(prepared_specs) : len(prepared_specs) + len(chosen)])
        parts = [ref[...] for ref in refs[len(prepared_specs) + len(chosen) : -1]]
        for _ in far:
            piece = next(chosen_refs)[...]
            parts.append(dot(next(prepared_refs)[...], padded(piece, 0, width - piece.shape[0])))
        for _ in near:
            piece = next(chosen_refs)[...]
            parts.append(dot(next(prepared_refs)[...], piece[:width]))
            rest = next(prepared_refs)[...]
            parts.append(dot(rest, padded(piece[width:], rest.shape[1] - piece.shape[0] + width, 0)))
        refs[-1][...] = sum(parts[1:], parts[0]) * scale

    return call(
        kernel,
        jax.ShapeDtypeStruct((queries, entries), jnp.float32),
        (1,),
        prepared_specs
        + [pl.BlockSpec(piece.shape, lambda i, me: (0, 0)) for piece in chosen]
        + [whole] * len(totals),
        whole,
        2 * queries * depth * entries,
        2 * depth * (queries + entries) + 8 * queries * entries,
        prefetch=1,
    )(me, *[prepared] * len(prepared_specs), *chosen, *totals)


def score_all(prepared, chosen, scale):
    queries = prepared.shape[0]
    devices, width, entries = chosen.shape

    def kernel(prepared_ref, chosen_ref, out_ref):
        part = dot(prepared_ref[...], chosen_ref[...]) * scale

        @pl.when(pl.program_id(0) == 0)
        def _():
            out_ref[...] = part

        @pl.when(pl.program_id(0) > 0)
        def _():
            out_ref[...] += part

    steps = 4
    block = devices * width // steps
    return call(
        kernel,
        jax.ShapeDtypeStruct((queries, entries), jnp.float32),
        (steps,),
        [
            pl.BlockSpec((queries, block), lambda i: (0, i)),
            pl.BlockSpec((block, entries), lambda i: (i, 0)),
        ],
        pl.BlockSpec((queries, entries), lambda i: (0, 0)),
        2 * devices * width * queries * entries,
        2 * devices * width * (queries + entries) + 4 * queries * entries,
    )(prepared, chosen.reshape(devices * width, entries))


def precondition(queries, left_inv, right_inv):
    total, features = queries.shape
    layers, k_out, _ = left_inv.shape
    k_in = right_inv.shape[1]
    group = MXU // k_out
    pair = MXU // k_in
    rows = 64
    wide = k_out // pair
    both = 2 * group

    def spread(values, times):
        size = values.shape[0]
        rows = lax.broadcasted_iota(jnp.int32, (MXU, size), 0) // times
        picks = (rows == lax.broadcasted_iota(jnp.int32, (MXU, size), 1)).astype(values.dtype)
        wide = dot(picks, values).astype(values.dtype)
        wide = lax.dot_general(
            wide, picks, (((1,), (1,)), ((), ())), preferred_element_type=jnp.float32
        )
        row = lax.broadcasted_iota(jnp.int32, (MXU, MXU), 0) % times
        column = lax.broadcasted_iota(jnp.int32, (MXU, MXU), 1) % times
        return jnp.where(row == column, wide, 0.0).astype(values.dtype)

    def repeat(values, times):
        empty = jnp.zeros_like(values)
        return jnp.concatenate(
            [
                jnp.concatenate([values if i == j else empty for j in range(times)], axis=1)
                for i in range(times)
            ],
            axis=0,
        )

    def kernel(queries_ref, left_inv_ref, right_inv_ref, out_ref, middle_ref, left_ref, right_ref):
        @pl.when(pl.program_id(0) == 0)
        def _():
            for layer in range(layers):
                left_ref[layer] = spread(left_inv_ref[layer], group)
                right_ref[layer] = repeat(right_inv_ref[layer], pair)

        for layer in range(layers):
            first = layer * k_out * k_in
            stack = jnp.concatenate(
                [queries_ref[:, first + p * MXU : first + (p + 1) * MXU] for p in range(wide)], axis=0
            )
            middle_ref[...] = dot(stack, right_ref[layer])
            for q in range(0, rows, both):
                halves = []
                for start in (q, q + group):
                    tiles = []
                    for p in range(wide):
                        at = p * rows + start
                        for s in range(pair):
                            tiles.append(middle_ref[at : at + group, s * k_in : (s + 1) * k_in])
                    halves.append(jnp.concatenate(tiles, axis=0))
                middle = jnp.concatenate(halves, axis=1).astype(queries_ref.dtype)
                result = dot(left_ref[layer], middle)
                for a in range(k_out):
                    at = a * group
                    tile = jnp.concatenate(
                        [result[at : at + group, :k_in], result[at : at + group, k_in:]], axis=0
                    )
                    lanes = first + a * k_in
                    out_ref[q : q + both, lanes : lanes + k_in] = tile.astype(out_ref.dtype)

    return call(
        kernel,
        jax.ShapeDtypeStruct(queries.shape, queries.dtype),
        (total // rows,),
        [
            pl.BlockSpec((rows, features), lambda i: (i, 0)),
            pl.BlockSpec(left_inv.shape, lambda i: (0, 0, 0)),
            pl.BlockSpec(right_inv.shape, lambda i: (0, 0, 0)),
        ],
        pl.BlockSpec((rows, features), lambda i: (i, 0)),
        4 * total * features * MXU,
        4 * total * features,
        scratch=[
            pltpu.VMEM((wide * rows, MXU), jnp.float32),
            pltpu.VMEM((layers, MXU, MXU), left_inv.dtype),
            pltpu.VMEM((layers, MXU, MXU), right_inv.dtype),
        ],
    )(queries, left_inv, right_inv)


def after(value, *earlier):
    return lax.optimization_barrier((value, *earlier))[0]


def on_device(doc_grads, query_grads, left_inv, right_inv, cand_owner, cand_row):
    devices = lax.axis_size("docs")
    half = devices // 2
    me = lax.axis_index("docs").astype(jnp.int32).reshape(1)
    base = me & -half
    doc_count = doc_grads.shape[0] // devices
    entries = cand_row.shape[0]
    width = doc_grads.shape[1]
    scale = query_grads.shape[1] ** (-0.5)

    def swap(values, k):
        return lax.ppermute(values, "docs", [(i, i ^ k) for i in range(devices)])

    def exchange(values):
        return lax.all_to_all(values, "docs", split_axis=0, concat_axis=0, tiled=True)

    tail = width // 8 if width % (4 * LANES) == 0 else 0
    if not tail:
        own_ids = cand_owner[:, 0] * doc_count + cand_row
        ids = exchange(jnp.broadcast_to(own_ids, (devices, 1, entries)))
        picked = gather_rows(jnp.zeros((1,), jnp.int32), ids, [doc_grads.T], devices)
        return score_all(precondition(query_grads, left_inv, right_inv), exchange(picked), scale)

    own_tail, own_ids = prepare(doc_grads, cand_owner, cand_row, devices, tail)
    across = swap(own_tail, half)
    ids = exchange(own_ids)
    table = after(doc_grads, own_ids).T
    far, near = list(range(half, devices)), list(range(1, half))
    inside = [0, *near]
    body = [(table, width - tail)]
    ids = after(ids, across)
    pieces = dict(zip(far, gather_pieces(me, ids, body, far[:2])))
    ids = after(ids, pieces[far[0]])
    pieces.update(zip(inside, gather_pieces(me, ids, [(table, width), (across, tail)], inside)))
    ids = after(ids, pieces[0])
    pieces.update(zip(far[2:], gather_pieces(me, ids, body, far[2:])))
    near = [half // 2, *near[1 : half // 2 - 1], *near[half // 2 :], 1]
    counts = [(2, 0), (2, 3)]
    phases = []
    while far or near:
        fars, nears = counts.pop(0) if counts else (3, 2)
        phases.append(far[:fars] + near[:nears])
        far, near = far[fars:], near[nears:]

    prepared = total = None
    came, ready, waiting = {0: pieces[0]}, [], [0]
    for number, phase in enumerate(phases):
        for k in phase:
            came[k] = swap(after(pieces[k], *ready) if ready else pieces[k], k)
        ready = [came[k] for k in phase]
        if number == 0:
            prepared = precondition(after(query_grads, *ready), left_inv, right_inv)
        if number == 1:
            ready.append(prepared)
        waiting += phase
        last = number == len(phases) - 1
        if last or number == len(phases) - 2:
            total = score_pieces(
                me,
                prepared,
                {k: came[k] for k in waiting if k >= half},
                {k: came[k] for k in waiting if k < half},
                total,
                width,
                half,
                scale if last else 1.0,
            )
            waiting = []
    return total


def solution(mesh):
    placed = (
        P("parts", "docs"),
        P(("parts", "docs"), None),
        P(),
        P(),
        P(("parts", "docs"), None),
        P(("parts", "docs")),
    )
    return jax.shard_map(
        on_device, mesh=mesh, in_specs=placed, out_specs=P(("parts", "docs"), None), check_vma=False
    )
```

```python
import jax
import jax.numpy as jnp
from jax import lax
from jax.experimental import pallas as pl
from jax.experimental.pallas import tpu as pltpu
from jax.sharding import PartitionSpec as P

LANES = 128
SUBLANES = 8
MXU = 256
VMEM_BYTES = 48 << 20
ALL_VMEM_BYTES = 63 << 20


def call(kernel, out_shape, grid, in_specs, out_specs, flops, bytes_accessed, scratch=(), prefetch=0, vmem=VMEM_BYTES):
    return pl.pallas_call(
        kernel,
        grid_spec=pltpu.PrefetchScalarGridSpec(
            num_scalar_prefetch=prefetch,
            grid=grid,
            in_specs=in_specs,
            out_specs=out_specs,
            scratch_shapes=scratch,
        ),
        out_shape=out_shape,
        compiler_params=pltpu.CompilerParams(vmem_limit_bytes=vmem),
        cost_estimate=pl.CostEstimate(flops=flops, bytes_accessed=bytes_accessed, transcendentals=0),
    )


def dot(a, b):
    return jnp.dot(a, b, preferred_element_type=jnp.float32)


def one_hot(ids, docs):
    group, row = ids // LANES, ids % LANES
    in_group = (lax.broadcasted_iota(jnp.int32, (LANES, ids.shape[1]), 0) == row).astype(jnp.bfloat16)
    return jnp.concatenate(
        [in_group * (group == g).astype(jnp.bfloat16) for g in range(docs // LANES)], axis=0
    )


def prepare(doc_grads, owners, rows, devices, tail):
    docs, width = doc_grads.shape
    entries = rows.shape[0]
    doc_count = docs // devices
    block = max(tail, LANES)

    def kernel(docs_hbm, owners_hbm, rows_hbm, tail_ref, ids_ref, docs_ref, owners_ref, rows_ref, sems):
        copies = [
            pltpu.make_async_copy(docs_hbm.at[:, width - block :], docs_ref, sems.at[0]),
            pltpu.make_async_copy(owners_hbm, owners_ref, sems.at[1]),
            pltpu.make_async_copy(rows_hbm, rows_ref, sems.at[2]),
        ]
        for copy in copies:
            copy.start()
        for copy in copies:
            copy.wait()
        tail_ref[...] = docs_ref[...].T[block - tail :, :]
        ids = owners_ref[...] * doc_count + rows_ref[...]
        ids_ref[...] = jnp.broadcast_to(ids[None], ids_ref.shape)

    return call(
        kernel,
        [
            pltpu.HBM((tail, docs), doc_grads.dtype),
            pltpu.HBM((devices, 1, entries), jnp.int32),
        ],
        (1,),
        [pl.BlockSpec(memory_space=pltpu.HBM)] * 3,
        [
            pl.BlockSpec((tail, docs), lambda i: (0, 0)),
            pl.BlockSpec((devices, 1, entries), lambda i: (0, 0, 0)),
        ],
        0,
        2 * docs * (block + tail),
        scratch=[
            pltpu.VMEM((docs, block), doc_grads.dtype),
            pltpu.VMEM((1, entries), jnp.int32),
            pltpu.VMEM((1, entries), jnp.int32),
            pltpu.SemaphoreType.DMA((3,)),
        ],
        vmem=ALL_VMEM_BYTES,
    )(doc_grads, owners.reshape(1, entries), rows.reshape(1, entries))


def gather_rows(base, ids, tables, count):
    entries = ids.shape[2]
    docs = tables[0].shape[1]
    features = sum(t.shape[0] for t in tables)

    def kernel(base_ref, ids_ref, *refs):
        out_ref = refs[-1]
        hot = one_hot(ids_ref[0], docs)
        start = 0
        for table_ref in refs[:-1]:
            stop = start + table_ref.shape[0]
            out_ref[0, start:stop, :] = dot(table_ref[...], hot).astype(out_ref.dtype)
            start = stop

    return call(
        kernel,
        pltpu.HBM((count, features, entries), tables[0].dtype),
        (count,),
        [pl.BlockSpec((1, 1, entries), lambda b, base: (base[0] + b, 0, 0))]
        + [pl.BlockSpec(t.shape, lambda b, base: (0, 0)) for t in tables],
        pl.BlockSpec((1, features, entries), lambda b, base: (b, 0, 0)),
        2 * count * features * docs * entries,
        2 * features * (docs + count * entries),
        prefetch=1,
    )(base, ids, *tables)


def gather_pieces(me, ids, tables, partners):
    entries = ids.shape[2]
    docs = tables[0][0].shape[1]
    features = sum(rows for _, rows in tables)
    count = len(partners)

    def kernel(me_ref, *refs):
        table_refs = refs[count : count + len(tables)]
        for ids_ref, out_ref in zip(refs[:count], refs[count + len(tables) :]):
            hot = one_hot(ids_ref[0], docs)
            start = 0
            for table_ref in table_refs:
                stop = start + table_ref.shape[0]
                out_ref[start:stop, :] = dot(table_ref[...], hot).astype(out_ref.dtype)
                start = stop

    return call(
        kernel,
        [pltpu.HBM((features, entries), tables[0][0].dtype)] * count,
        (1,),
        [pl.BlockSpec((1, 1, entries), lambda i, me, k=k: (me[0] ^ k, 0, 0)) for k in partners]
        + [pl.BlockSpec((rows, docs), lambda i, me: (0, 0)) for _, rows in tables],
        [pl.BlockSpec((features, entries), lambda i, me: (0, 0))] * count,
        2 * count * features * docs * entries,
        2 * features * (docs + count * entries),
        prefetch=1,
    )(me, *[ids] * count, *[table for table, _ in tables])


def padded(values, above, below):
    zeros = lambda rows: [jnp.zeros((rows, values.shape[1]), values.dtype)] if rows else []
    return jnp.concatenate([*zeros(above), values, *zeros(below)], axis=0)


def score_pieces(me, prepared, chosen, total, width, scale):
    queries = prepared.shape[0]
    features, entries = next(iter(chosen.values())).shape
    count = len(chosen)
    whole = pl.BlockSpec((queries, entries), lambda i, me: (0, 0))

    def kernel(me_ref, *refs):
        out = refs[-2][...]
        for prepared_ref, chosen_ref in zip(refs[:count], refs[count : 2 * count]):
            out = out + dot(prepared_ref[...], padded(chosen_ref[...], 0, width - features))
        refs[-1][...] = out * scale

    return call(
        kernel,
        jax.ShapeDtypeStruct((queries, entries), jnp.float32),
        (1,),
        [pl.BlockSpec((queries, width), lambda i, me, k=k: (0, me[0] ^ k)) for k in chosen]
        + [pl.BlockSpec((features, entries), lambda i, me: (0, 0))] * count
        + [whole],
        whole,
        2 * count * features * queries * entries,
        2 * count * features * (queries + entries) + 8 * queries * entries,
        prefetch=1,
    )(me, *[prepared] * count, *chosen.values(), total)


def score_near(base, prepared, chosen, width, half):
    queries = prepared.shape[0]
    count, features, entries = chosen.shape
    tail = features - width
    block = max(tail, LANES)
    stride = width // block

    def kernel(base_ref, own_ref, far_ref, chosen_ref, out_ref):
        part = dot(own_ref[...], chosen_ref[0, :width, :])
        part += dot(far_ref[...], padded(chosen_ref[0, width:, :], block - tail, 0))

        @pl.when(pl.program_id(0) == 0)
        def _():
            out_ref[...] = part

        @pl.when(pl.program_id(0) > 0)
        def _():
            out_ref[...] += part

    return call(
        kernel,
        jax.ShapeDtypeStruct((queries, entries), jnp.float32),
        (count,),
        [
            pl.BlockSpec((queries, width), lambda j, base: (0, base[0] + j)),
            pl.BlockSpec(
                (queries, block), lambda j, base: (0, ((base[0] + j) ^ half) * stride + stride - 1)
            ),
            pl.BlockSpec((1, features, entries), lambda j, base: (j, 0, 0)),
        ],
        pl.BlockSpec((queries, entries), lambda j, base: (0, 0)),
        2 * count * features * queries * entries,
        2 * count * features * (queries + entries) + 4 * queries * entries,
        prefetch=1,
    )(base, prepared, prepared, chosen)


def score_all(prepared, chosen, scale):
    queries = prepared.shape[0]
    devices, width, entries = chosen.shape

    def kernel(prepared_ref, chosen_ref, out_ref):
        part = dot(prepared_ref[...], chosen_ref[...]) * scale

        @pl.when(pl.program_id(0) == 0)
        def _():
            out_ref[...] = part

        @pl.when(pl.program_id(0) > 0)
        def _():
            out_ref[...] += part

    steps = 4
    block = devices * width // steps
    return call(
        kernel,
        jax.ShapeDtypeStruct((queries, entries), jnp.float32),
        (steps,),
        [
            pl.BlockSpec((queries, block), lambda i: (0, i)),
            pl.BlockSpec((block, entries), lambda i: (i, 0)),
        ],
        pl.BlockSpec((queries, entries), lambda i: (0, 0)),
        2 * devices * width * queries * entries,
        2 * devices * width * (queries + entries) + 4 * queries * entries,
    )(prepared, chosen.reshape(devices * width, entries))


def precondition(queries, left_inv, right_inv):
    total, features = queries.shape
    layers, k_out, _ = left_inv.shape
    k_in = right_inv.shape[1]
    group = MXU // k_out
    pair = MXU // k_in
    rows = 64
    wide = k_out // pair
    both = 2 * group

    def spread(values, times):
        size = values.shape[0]
        rows = lax.broadcasted_iota(jnp.int32, (MXU, size), 0) // times
        picks = (rows == lax.broadcasted_iota(jnp.int32, (MXU, size), 1)).astype(values.dtype)
        wide = dot(picks, values).astype(values.dtype)
        wide = lax.dot_general(
            wide, picks, (((1,), (1,)), ((), ())), preferred_element_type=jnp.float32
        )
        row = lax.broadcasted_iota(jnp.int32, (MXU, MXU), 0) % times
        column = lax.broadcasted_iota(jnp.int32, (MXU, MXU), 1) % times
        return jnp.where(row == column, wide, 0.0).astype(values.dtype)

    def repeat(values, times):
        empty = jnp.zeros_like(values)
        return jnp.concatenate(
            [
                jnp.concatenate([values if i == j else empty for j in range(times)], axis=1)
                for i in range(times)
            ],
            axis=0,
        )

    def kernel(queries_ref, left_inv_ref, right_inv_ref, out_ref, middle_ref, left_ref, right_ref):
        @pl.when(pl.program_id(0) == 0)
        def _():
            for layer in range(layers):
                left_ref[layer] = spread(left_inv_ref[layer], group)
                right_ref[layer] = repeat(right_inv_ref[layer], pair)

        for layer in range(layers):
            first = layer * k_out * k_in
            stack = jnp.concatenate(
                [queries_ref[:, first + p * MXU : first + (p + 1) * MXU] for p in range(wide)], axis=0
            )
            middle_ref[...] = dot(stack, right_ref[layer])
            for q in range(0, rows, both):
                halves = []
                for start in (q, q + group):
                    tiles = []
                    for p in range(wide):
                        at = p * rows + start
                        for s in range(pair):
                            tiles.append(middle_ref[at : at + group, s * k_in : (s + 1) * k_in])
                    halves.append(jnp.concatenate(tiles, axis=0))
                middle = jnp.concatenate(halves, axis=1).astype(queries_ref.dtype)
                result = dot(left_ref[layer], middle)
                for a in range(k_out):
                    at = a * group
                    tile = jnp.concatenate(
                        [result[at : at + group, :k_in], result[at : at + group, k_in:]], axis=0
                    )
                    lanes = first + a * k_in
                    out_ref[q : q + both, lanes : lanes + k_in] = tile.astype(out_ref.dtype)

    return call(
        kernel,
        jax.ShapeDtypeStruct(queries.shape, queries.dtype),
        (total // rows,),
        [
            pl.BlockSpec((rows, features), lambda i: (i, 0)),
            pl.BlockSpec(left_inv.shape, lambda i: (0, 0, 0)),
            pl.BlockSpec(right_inv.shape, lambda i: (0, 0, 0)),
        ],
        pl.BlockSpec((rows, features), lambda i: (i, 0)),
        40000 * total * features,
        4 * total * features,
        scratch=[
            pltpu.VMEM((wide * rows, MXU), jnp.float32),
            pltpu.VMEM((layers, MXU, MXU), left_inv.dtype),
            pltpu.VMEM((layers, MXU, MXU), right_inv.dtype),
        ],
    )(queries, left_inv, right_inv)


def after(value, *earlier):
    return lax.optimization_barrier((value, *earlier))[0]


def on_device(doc_grads, query_grads, left_inv, right_inv, cand_owner, cand_row):
    devices = lax.axis_size("docs")
    half = devices // 2
    me = lax.axis_index("docs").astype(jnp.int32).reshape(1)
    base = me & -half
    doc_count = doc_grads.shape[0] // devices
    entries = cand_row.shape[0]
    width = doc_grads.shape[1]
    scale = query_grads.shape[1] ** (-0.5)

    def swap(values, k):
        return lax.ppermute(values, "docs", [(i, i ^ k) for i in range(devices)])

    def exchange(values):
        return lax.all_to_all(values, "docs", split_axis=0, concat_axis=0, tiled=True)

    tail = width // 8 if width % (4 * LANES) == 0 else 0
    if not tail:
        own_ids = cand_owner[:, 0] * doc_count + cand_row
        ids = exchange(jnp.broadcast_to(own_ids, (devices, 1, entries)))
        picked = gather_rows(jnp.zeros((1,), jnp.int32), ids, [doc_grads.T], devices)
        return score_all(precondition(query_grads, left_inv, right_inv), exchange(picked), scale)

    own_tail, own_ids = prepare(doc_grads, cand_owner, cand_row, devices, tail)
    across = swap(own_tail, half)
    ids = exchange(own_ids)
    table = after(doc_grads, own_ids).T
    far = list(range(half, devices))
    first, flight = far[:2], 5
    body = [(table, width - tail)]
    ids = after(ids, across)
    pieces = dict(zip(far, gather_pieces(me, ids, body, first)))
    came = {k: swap(pieces[k], k) for k in first}
    ids = after(ids, pieces[far[0]])
    picked = gather_rows(base, ids, [table, across], half)
    near = lax.all_to_all(
        picked,
        "docs",
        split_axis=0,
        concat_axis=0,
        axis_index_groups=[list(range(half)), list(range(half, devices))],
        tiled=True,
    )
    ids = after(ids, picked)
    pieces.update(zip(far[2:], gather_pieces(me, ids, body, far[2:])))
    ready = [came[k] for k in first]
    prepared = precondition(after(query_grads, *ready), left_inv, right_inv)
    for i, k in enumerate(far[2:]):
        before = ready if i < flight else [came[far[2 + i - flight]], prepared]
        came[k] = swap(after(pieces[k], *before), k)
    total = score_near(base, prepared, near, width, half)
    return score_pieces(me, prepared, came, total, width, scale)


def solution(mesh):
    placed = (
        P("parts", "docs"),
        P(("parts", "docs"), None),
        P(),
        P(),
        P(("parts", "docs"), None),
        P(("parts", "docs")),
    )
    return jax.shard_map(
        on_device, mesh=mesh, in_specs=placed, out_specs=P(("parts", "docs"), None), check_vma=False
    )
```

```python
import jax
import jax.numpy as jnp
from jax import lax
from jax.experimental import pallas as pl
from jax.experimental.pallas import tpu as pltpu
from jax.sharding import PartitionSpec as P

LANES = 128
SUBLANES = 8
MXU = 256
VMEM_BYTES = 48 << 20
ALL_VMEM_BYTES = 63 << 20


def call(kernel, out_shape, grid, in_specs, out_specs, flops, bytes_accessed, scratch=(), prefetch=0, vmem=VMEM_BYTES):
    return pl.pallas_call(
        kernel,
        grid_spec=pltpu.PrefetchScalarGridSpec(
            num_scalar_prefetch=prefetch,
            grid=grid,
            in_specs=in_specs,
            out_specs=out_specs,
            scratch_shapes=scratch,
        ),
        out_shape=out_shape,
        compiler_params=pltpu.CompilerParams(vmem_limit_bytes=vmem),
        cost_estimate=pl.CostEstimate(flops=flops, bytes_accessed=bytes_accessed, transcendentals=0),
    )


def dot(a, b):
    return jnp.dot(a, b, preferred_element_type=jnp.float32)


def one_hot(ids, docs):
    group, row = ids // LANES, ids % LANES
    in_group = (lax.broadcasted_iota(jnp.int32, (LANES, ids.shape[1]), 0) == row).astype(jnp.bfloat16)
    return jnp.concatenate(
        [in_group * (group == g).astype(jnp.bfloat16) for g in range(docs // LANES)], axis=0
    )


def prepare(doc_grads, owners, rows, devices, first, size):
    docs = doc_grads.shape[0]
    entries = rows.shape[0]
    doc_count = docs // devices
    block = -(-size // LANES) * LANES
    skip = first % LANES

    def kernel(docs_hbm, owners_hbm, rows_hbm, some_ref, ids_ref, docs_ref, owners_ref, rows_ref, sems):
        copies = [
            pltpu.make_async_copy(docs_hbm.at[:, pl.ds(first - skip, block)], docs_ref, sems.at[0]),
            pltpu.make_async_copy(owners_hbm, owners_ref, sems.at[1]),
            pltpu.make_async_copy(rows_hbm, rows_ref, sems.at[2]),
        ]
        for copy in copies:
            copy.start()
        for copy in copies:
            copy.wait()
        some_ref[...] = docs_ref[...].T[skip : skip + size, :]
        ids = owners_ref[...] * doc_count + rows_ref[...]
        ids_ref[...] = jnp.broadcast_to(ids[None], ids_ref.shape)

    return call(
        kernel,
        [
            pltpu.HBM((size, docs), doc_grads.dtype),
            pltpu.HBM((devices, 1, entries), jnp.int32),
        ],
        (1,),
        [pl.BlockSpec(memory_space=pltpu.HBM)] * 3,
        [
            pl.BlockSpec((size, docs), lambda i: (0, 0)),
            pl.BlockSpec((devices, 1, entries), lambda i: (0, 0, 0)),
        ],
        0,
        2 * docs * (block + size),
        scratch=[
            pltpu.VMEM((docs, block), doc_grads.dtype),
            pltpu.VMEM((1, entries), jnp.int32),
            pltpu.VMEM((1, entries), jnp.int32),
            pltpu.SemaphoreType.DMA((3,)),
        ],
        vmem=ALL_VMEM_BYTES,
    )(doc_grads, owners.reshape(1, entries), rows.reshape(1, entries))


def gather_rows(base, ids, tables, count):
    entries = ids.shape[2]
    docs = tables[0].shape[1]
    features = sum(t.shape[0] for t in tables)

    def kernel(base_ref, ids_ref, *refs):
        out_ref = refs[-1]
        hot = one_hot(ids_ref[0], docs)
        start = 0
        for table_ref in refs[:-1]:
            stop = start + table_ref.shape[0]
            out_ref[0, start:stop, :] = dot(table_ref[...], hot).astype(out_ref.dtype)
            start = stop

    return call(
        kernel,
        pltpu.HBM((count, features, entries), tables[0].dtype),
        (count,),
        [pl.BlockSpec((1, 1, entries), lambda b, base: (base[0] + b, 0, 0))]
        + [pl.BlockSpec(t.shape, lambda b, base: (0, 0)) for t in tables],
        pl.BlockSpec((1, features, entries), lambda b, base: (b, 0, 0)),
        1000,
        1000,
        prefetch=1,
    )(base, ids, *tables)


def gather_pieces(me, ids, tables, partners):
    entries = ids.shape[2]
    docs = tables[0][0].shape[1]
    features = sum(rows for _, rows in tables)
    count = len(partners)

    def kernel(me_ref, *refs):
        table_refs = refs[count : count + len(tables)]
        for ids_ref, out_ref in zip(refs[:count], refs[count + len(tables) :]):
            hot = one_hot(ids_ref[0], docs)
            start = 0
            for table_ref in table_refs:
                stop = start + table_ref.shape[0]
                out_ref[start:stop, :] = dot(table_ref[...], hot).astype(out_ref.dtype)
                start = stop

    return call(
        kernel,
        [pltpu.HBM((features, entries), tables[0][0].dtype)] * count,
        (1,),
        [pl.BlockSpec((1, 1, entries), lambda i, me, k=k: (me[0] ^ k, 0, 0)) for k in partners]
        + [pl.BlockSpec((rows, docs), lambda i, me: (0, 0)) for _, rows in tables],
        [pl.BlockSpec((features, entries), lambda i, me: (0, 0))] * count,
        1000,
        1000,
        prefetch=1,
    )(me, *[ids] * count, *[table for table, _ in tables])


def padded(values, above, below):
    zeros = lambda rows: [jnp.zeros((rows, values.shape[1]), values.dtype)] if rows else []
    return jnp.concatenate([*zeros(above), values, *zeros(below)], axis=0)


def score_pieces(me, prepared, chosen, total, width, scale):
    queries = prepared.shape[0]
    features, entries = next(iter(chosen.values())).shape
    count = len(chosen)
    whole = pl.BlockSpec((queries, entries), lambda i, me: (0, 0))

    def kernel(me_ref, *refs):
        out = refs[-2][...]
        for prepared_ref, chosen_ref in zip(refs[:count], refs[count : 2 * count]):
            out = out + dot(prepared_ref[...], padded(chosen_ref[...], 0, width - features))
        refs[-1][...] = out * scale

    return call(
        kernel,
        jax.ShapeDtypeStruct((queries, entries), jnp.float32),
        (1,),
        [pl.BlockSpec((queries, width), lambda i, me, k=k: (0, me[0] ^ k)) for k in chosen]
        + [pl.BlockSpec((features, entries), lambda i, me: (0, 0))] * count
        + [whole],
        whole,
        2 * count * features * queries * entries,
        2 * count * features * (queries + entries) + 8 * queries * entries,
        prefetch=1,
    )(me, *[prepared] * count, *chosen.values(), total)


def score_near(base, prepared, chosen, width, first, half):
    queries = prepared.shape[0]
    count, features, entries = chosen.shape
    size = features - width
    stride = width // LANES

    def kernel(base_ref, own_ref, far_ref, chosen_ref, out_ref):
        above = first % LANES
        part = dot(own_ref[...], chosen_ref[0, :width, :])
        part += dot(far_ref[...], padded(chosen_ref[0, width:, :], above, LANES - above - size))

        @pl.when(pl.program_id(0) == 0)
        def _():
            out_ref[...] = part

        @pl.when(pl.program_id(0) > 0)
        def _():
            out_ref[...] += part

    return call(
        kernel,
        jax.ShapeDtypeStruct((queries, entries), jnp.float32),
        (count,),
        [
            pl.BlockSpec((queries, width), lambda j, base: (0, base[0] + j)),
            pl.BlockSpec(
                (queries, LANES),
                lambda j, base: (0, ((base[0] + j) ^ half) * stride + first // LANES),
            ),
            pl.BlockSpec((1, features, entries), lambda j, base: (j, 0, 0)),
        ],
        pl.BlockSpec((queries, entries), lambda j, base: (0, 0)),
        2 * count * features * queries * entries,
        2 * count * features * (queries + entries) + 4 * queries * entries,
        prefetch=1,
    )(base, prepared, prepared, chosen)


def score_across(base, prepared, chosen, total, width, first, half):
    queries = prepared.shape[0]
    count, features, entries = chosen.shape
    whole = pl.BlockSpec((queries, entries), lambda i, base: (0, 0))

    def kernel(base_ref, *refs):
        chosen_ref, total_ref, out_ref = refs[count:]
        out = total_ref[...]
        for j in range(count):
            out = out + dot(refs[j][...], chosen_ref[j])
        out_ref[...] = out

    return call(
        kernel,
        jax.ShapeDtypeStruct((queries, entries), jnp.float32),
        (1,),
        [
            pl.BlockSpec(
                (queries, features),
                lambda i, base, j=j: (0, (((base[0] + j) ^ half) * width + first) // features),
            )
            for j in range(count)
        ]
        + [pl.BlockSpec(chosen.shape, lambda i, base: (0, 0, 0)), whole],
        whole,
        2 * count * features * queries * entries,
        2 * count * features * (queries + entries) + 8 * queries * entries,
        prefetch=1,
    )(base, *[prepared] * count, chosen, total)


def score_all(prepared, chosen, scale):
    queries = prepared.shape[0]
    devices, width, entries = chosen.shape

    def kernel(prepared_ref, chosen_ref, out_ref):
        part = dot(prepared_ref[...], chosen_ref[...]) * scale

        @pl.when(pl.program_id(0) == 0)
        def _():
            out_ref[...] = part

        @pl.when(pl.program_id(0) > 0)
        def _():
            out_ref[...] += part

    steps = 4
    block = devices * width // steps
    return call(
        kernel,
        jax.ShapeDtypeStruct((queries, entries), jnp.float32),
        (steps,),
        [
            pl.BlockSpec((queries, block), lambda i: (0, i)),
            pl.BlockSpec((block, entries), lambda i: (i, 0)),
        ],
        pl.BlockSpec((queries, entries), lambda i: (0, 0)),
        2 * devices * width * queries * entries,
        2 * devices * width * (queries + entries) + 4 * queries * entries,
    )(prepared, chosen.reshape(devices * width, entries))


def precondition(queries, left_inv, right_inv):
    total, features = queries.shape
    layers, k_out, _ = left_inv.shape
    k_in = right_inv.shape[1]
    group = MXU // k_out
    pair = MXU // k_in
    rows = 64
    wide = k_out // pair
    both = 2 * group

    def spread(values, times):
        size = values.shape[0]
        rows = lax.broadcasted_iota(jnp.int32, (MXU, size), 0) // times
        picks = (rows == lax.broadcasted_iota(jnp.int32, (MXU, size), 1)).astype(values.dtype)
        wide = dot(picks, values).astype(values.dtype)
        wide = lax.dot_general(
            wide, picks, (((1,), (1,)), ((), ())), preferred_element_type=jnp.float32
        )
        row = lax.broadcasted_iota(jnp.int32, (MXU, MXU), 0) % times
        column = lax.broadcasted_iota(jnp.int32, (MXU, MXU), 1) % times
        return jnp.where(row == column, wide, 0.0).astype(values.dtype)

    def repeat(values, times):
        empty = jnp.zeros_like(values)
        return jnp.concatenate(
            [
                jnp.concatenate([values if i == j else empty for j in range(times)], axis=1)
                for i in range(times)
            ],
            axis=0,
        )

    def kernel(queries_ref, left_inv_ref, right_inv_ref, out_ref, middle_ref, left_ref, right_ref):
        @pl.when(pl.program_id(0) == 0)
        def _():
            for layer in range(layers):
                left_ref[layer] = spread(left_inv_ref[layer], group)
                right_ref[layer] = repeat(right_inv_ref[layer], pair)

        for layer in range(layers):
            first = layer * k_out * k_in
            stack = jnp.concatenate(
                [queries_ref[:, first + p * MXU : first + (p + 1) * MXU] for p in range(wide)], axis=0
            )
            middle_ref[...] = dot(stack, right_ref[layer])
            for q in range(0, rows, both):
                halves = []
                for start in (q, q + group):
                    tiles = []
                    for p in range(wide):
                        at = p * rows + start
                        for s in range(pair):
                            tiles.append(middle_ref[at : at + group, s * k_in : (s + 1) * k_in])
                    halves.append(jnp.concatenate(tiles, axis=0))
                middle = jnp.concatenate(halves, axis=1).astype(queries_ref.dtype)
                result = dot(left_ref[layer], middle)
                for a in range(k_out):
                    at = a * group
                    tile = jnp.concatenate(
                        [result[at : at + group, :k_in], result[at : at + group, k_in:]], axis=0
                    )
                    lanes = first + a * k_in
                    out_ref[q : q + both, lanes : lanes + k_in] = tile.astype(out_ref.dtype)

    return call(
        kernel,
        jax.ShapeDtypeStruct(queries.shape, queries.dtype),
        (total // rows,),
        [
            pl.BlockSpec((rows, features), lambda i: (i, 0)),
            pl.BlockSpec(left_inv.shape, lambda i: (0, 0, 0)),
            pl.BlockSpec(right_inv.shape, lambda i: (0, 0, 0)),
        ],
        pl.BlockSpec((rows, features), lambda i: (i, 0)),
        40000 * total * features,
        4 * total * features,
        scratch=[
            pltpu.VMEM((wide * rows, MXU), jnp.float32),
            pltpu.VMEM((layers, MXU, MXU), left_inv.dtype),
            pltpu.VMEM((layers, MXU, MXU), right_inv.dtype),
        ],
    )(queries, left_inv, right_inv)


def after(value, *earlier):
    return lax.optimization_barrier((value, *earlier))[0]


def on_device(doc_grads, query_grads, left_inv, right_inv, cand_owner, cand_row):
    devices = lax.axis_size("docs")
    half = devices // 2
    me = lax.axis_index("docs").astype(jnp.int32).reshape(1)
    base = me & -half
    doc_count = doc_grads.shape[0] // devices
    entries = cand_row.shape[0]
    width = doc_grads.shape[1]
    scale = query_grads.shape[1] ** (-0.5)

    def swap(values, k):
        return lax.ppermute(values, "docs", [(i, i ^ k) for i in range(devices)])

    def exchange(values):
        return lax.all_to_all(values, "docs", split_axis=0, concat_axis=0, tiled=True)

    if width % (4 * LANES):
        own_ids = cand_owner[:, 0] * doc_count + cand_row
        ids = exchange(jnp.broadcast_to(own_ids, (devices, 1, entries)))
        picked = gather_rows(jnp.zeros((1,), jnp.int32), ids, [doc_grads.T], devices)
        return score_all(precondition(query_grads, left_inv, right_inv), exchange(picked), scale)

    def exchange_inside(values):
        return lax.all_to_all(
            values,
            "docs",
            split_axis=0,
            concat_axis=0,
            axis_index_groups=[list(range(half)), list(range(half, devices))],
            tiled=True,
        )

    direct, first, second = width // 8 * 5, width // 8, width // 4
    own_first, own_ids = prepare(doc_grads, cand_owner, cand_row, devices, direct, first)
    across_first = swap(own_first, half)
    ids = exchange(own_ids)
    table = after(doc_grads, own_ids).T
    across_second = swap(after(table[direct + first :], across_first), half)
    ids = after(ids, across_first)
    far = list(range(half, devices))
    pieces = dict(zip(far, gather_pieces(me, ids, [(table, direct)], far)))
    picked = gather_rows(base, after(ids, pieces[far[0]]), [table, across_first], half)
    near = exchange_inside(picked)
    prepared = precondition(after(query_grads, across_second), left_inv, right_inv)
    flight = 5
    came = {}
    for i, k in enumerate(far):
        before = [across_second] if i < flight else [came[far[i - flight]], prepared]
        came[k] = swap(after(pieces[k], *before), k)
    picked = gather_rows(base, after(ids, came[far[2]]), [across_second], half)
    near_second = exchange_inside(picked)
    total = score_near(base, prepared, after(near, came[far[2]]), width, direct, half)
    total = score_across(base, prepared, near_second, total, width, direct + first, half)
    return score_pieces(me, prepared, came, total, width, scale)


def solution(mesh):
    placed = (
        P("parts", "docs"),
        P(("parts", "docs"), None),
        P(),
        P(),
        P(("parts", "docs"), None),
        P(("parts", "docs")),
    )
    return jax.shard_map(
        on_device, mesh=mesh, in_specs=placed, out_specs=P(("parts", "docs"), None), check_vma=False
    )
```

```python
import jax
import jax.numpy as jnp
from jax import lax
from jax.experimental import pallas as pl
from jax.experimental.pallas import tpu as pltpu
from jax.sharding import PartitionSpec as P

LANES = 128
SUBLANES = 8
MXU = 256
VMEM_BYTES = 48 << 20
ALL_VMEM_BYTES = 63 << 20


def call(kernel, out_shape, grid, in_specs, out_specs, flops, bytes_accessed, scratch=(), prefetch=0, vmem=VMEM_BYTES):
    return pl.pallas_call(
        kernel,
        grid_spec=pltpu.PrefetchScalarGridSpec(
            num_scalar_prefetch=prefetch,
            grid=grid,
            in_specs=in_specs,
            out_specs=out_specs,
            scratch_shapes=scratch,
        ),
        out_shape=out_shape,
        compiler_params=pltpu.CompilerParams(vmem_limit_bytes=vmem),
        cost_estimate=pl.CostEstimate(flops=flops, bytes_accessed=bytes_accessed, transcendentals=0),
    )


def dot(a, b):
    return jnp.dot(a, b, preferred_element_type=jnp.float32)


def one_hot(ids, docs):
    group, row = ids // LANES, ids % LANES
    in_group = (lax.broadcasted_iota(jnp.int32, (LANES, ids.shape[1]), 0) == row).astype(jnp.bfloat16)
    return jnp.concatenate(
        [in_group * (group == g).astype(jnp.bfloat16) for g in range(docs // LANES)], axis=0
    )


def prepare(doc_grads, owners, rows, devices, tail):
    docs, width = doc_grads.shape
    entries = rows.shape[0]
    doc_count = docs // devices
    block = max(tail, LANES)

    def kernel(docs_hbm, owners_hbm, rows_hbm, tail_ref, ids_ref, docs_ref, owners_ref, rows_ref, sems):
        copies = [
            pltpu.make_async_copy(docs_hbm.at[:, width - block :], docs_ref, sems.at[0]),
            pltpu.make_async_copy(owners_hbm, owners_ref, sems.at[1]),
            pltpu.make_async_copy(rows_hbm, rows_ref, sems.at[2]),
        ]
        for copy in copies:
            copy.start()
        for copy in copies:
            copy.wait()
        tail_ref[...] = docs_ref[...].T[block - tail :, :]
        ids = owners_ref[...] * doc_count + rows_ref[...]
        ids_ref[...] = jnp.broadcast_to(ids[None], ids_ref.shape)

    return call(
        kernel,
        [
            pltpu.HBM((tail, docs), doc_grads.dtype),
            pltpu.HBM((devices, 1, entries), jnp.int32),
        ],
        (1,),
        [pl.BlockSpec(memory_space=pltpu.HBM)] * 3,
        [
            pl.BlockSpec((tail, docs), lambda i: (0, 0)),
            pl.BlockSpec((devices, 1, entries), lambda i: (0, 0, 0)),
        ],
        0,
        2 * docs * (block + tail),
        scratch=[
            pltpu.VMEM((docs, block), doc_grads.dtype),
            pltpu.VMEM((1, entries), jnp.int32),
            pltpu.VMEM((1, entries), jnp.int32),
            pltpu.SemaphoreType.DMA((3,)),
        ],
        vmem=ALL_VMEM_BYTES,
    )(doc_grads, owners.reshape(1, entries), rows.reshape(1, entries))


def gather_rows(base, ids, tables, count):
    entries = ids.shape[2]
    docs = tables[0].shape[1]
    features = sum(t.shape[0] for t in tables)

    def kernel(base_ref, ids_ref, *refs):
        out_ref = refs[-1]
        hot = one_hot(ids_ref[0], docs)
        start = 0
        for table_ref in refs[:-1]:
            stop = start + table_ref.shape[0]
            out_ref[0, start:stop, :] = dot(table_ref[...], hot).astype(out_ref.dtype)
            start = stop

    return call(
        kernel,
        pltpu.HBM((count, features, entries), tables[0].dtype),
        (count,),
        [pl.BlockSpec((1, 1, entries), lambda b, base: (base[0] + b, 0, 0))]
        + [pl.BlockSpec(t.shape, lambda b, base: (0, 0)) for t in tables],
        pl.BlockSpec((1, features, entries), lambda b, base: (b, 0, 0)),
        2 * count * features * docs * entries,
        2 * features * (docs + count * entries),
        prefetch=1,
    )(base, ids, *tables)


def gather_pieces(me, ids, tables, partners):
    entries = ids.shape[2]
    docs = tables[0][0].shape[1]
    features = sum(rows for _, rows in tables)
    count = len(partners)

    def kernel(me_ref, *refs):
        table_refs = refs[count : count + len(tables)]
        for ids_ref, out_ref in zip(refs[:count], refs[count + len(tables) :]):
            hot = one_hot(ids_ref[0], docs)
            start = 0
            for table_ref in table_refs:
                stop = start + table_ref.shape[0]
                out_ref[start:stop, :] = dot(table_ref[...], hot).astype(out_ref.dtype)
                start = stop

    return call(
        kernel,
        [pltpu.HBM((features, entries), tables[0][0].dtype)] * count,
        (1,),
        [pl.BlockSpec((1, 1, entries), lambda i, me, k=k: (me[0] ^ k, 0, 0)) for k in partners]
        + [pl.BlockSpec((rows, docs), lambda i, me: (0, 0)) for _, rows in tables],
        [pl.BlockSpec((features, entries), lambda i, me: (0, 0))] * count,
        2 * count * features * docs * entries,
        2 * features * (docs + count * entries),
        prefetch=1,
    )(me, *[ids] * count, *[table for table, _ in tables])


def padded(values, above, below):
    zeros = lambda rows: [jnp.zeros((rows, values.shape[1]), values.dtype)] if rows else []
    return jnp.concatenate([*zeros(above), values, *zeros(below)], axis=0)


def score_pieces(me, prepared, chosen, total, width, scale):
    queries = prepared.shape[0]
    features, entries = next(iter(chosen.values())).shape
    count = len(chosen)
    whole = pl.BlockSpec((queries, entries), lambda i, me: (0, 0))

    def kernel(me_ref, *refs):
        out = refs[-2][...]
        for prepared_ref, chosen_ref in zip(refs[:count], refs[count : 2 * count]):
            out = out + dot(prepared_ref[...], padded(chosen_ref[...], 0, width - features))
        refs[-1][...] = out * scale

    return call(
        kernel,
        jax.ShapeDtypeStruct((queries, entries), jnp.float32),
        (1,),
        [pl.BlockSpec((queries, width), lambda i, me, k=k: (0, me[0] ^ k)) for k in chosen]
        + [pl.BlockSpec((features, entries), lambda i, me: (0, 0))] * count
        + [whole],
        whole,
        2 * count * features * queries * entries,
        2 * count * features * (queries + entries) + 8 * queries * entries,
        prefetch=1,
    )(me, *[prepared] * count, *chosen.values(), total)


def score_near(base, prepared, chosen, width, half):
    queries = prepared.shape[0]
    count, features, entries = chosen.shape
    tail = features - width
    block = max(tail, LANES)
    stride = width // block

    def kernel(base_ref, own_ref, far_ref, chosen_ref, out_ref):
        part = dot(own_ref[...], chosen_ref[0, :width, :])
        part += dot(far_ref[...], padded(chosen_ref[0, width:, :], block - tail, 0))

        @pl.when(pl.program_id(0) == 0)
        def _():
            out_ref[...] = part

        @pl.when(pl.program_id(0) > 0)
        def _():
            out_ref[...] += part

    return call(
        kernel,
        jax.ShapeDtypeStruct((queries, entries), jnp.float32),
        (count,),
        [
            pl.BlockSpec((queries, width), lambda j, base: (0, base[0] + j)),
            pl.BlockSpec(
                (queries, block), lambda j, base: (0, ((base[0] + j) ^ half) * stride + stride - 1)
            ),
            pl.BlockSpec((1, features, entries), lambda j, base: (j, 0, 0)),
        ],
        pl.BlockSpec((queries, entries), lambda j, base: (0, 0)),
        2 * count * features * queries * entries,
        2 * count * features * (queries + entries) + 4 * queries * entries,
        prefetch=1,
    )(base, prepared, prepared, chosen)


def score_all(prepared, chosen, scale):
    queries = prepared.shape[0]
    devices, width, entries = chosen.shape

    def kernel(prepared_ref, chosen_ref, out_ref):
        part = dot(prepared_ref[...], chosen_ref[...]) * scale

        @pl.when(pl.program_id(0) == 0)
        def _():
            out_ref[...] = part

        @pl.when(pl.program_id(0) > 0)
        def _():
            out_ref[...] += part

    steps = 4
    block = devices * width // steps
    return call(
        kernel,
        jax.ShapeDtypeStruct((queries, entries), jnp.float32),
        (steps,),
        [
            pl.BlockSpec((queries, block), lambda i: (0, i)),
            pl.BlockSpec((block, entries), lambda i: (i, 0)),
        ],
        pl.BlockSpec((queries, entries), lambda i: (0, 0)),
        2 * devices * width * queries * entries,
        2 * devices * width * (queries + entries) + 4 * queries * entries,
    )(prepared, chosen.reshape(devices * width, entries))


def precondition(queries, left_inv, right_inv):
    total, features = queries.shape
    layers, k_out, _ = left_inv.shape
    k_in = right_inv.shape[1]
    group = MXU // k_out
    pair = MXU // k_in
    rows = 64
    wide = k_out // pair
    both = 2 * group

    def spread(values, times):
        size = values.shape[0]
        rows = lax.broadcasted_iota(jnp.int32, (MXU, size), 0) // times
        picks = (rows == lax.broadcasted_iota(jnp.int32, (MXU, size), 1)).astype(values.dtype)
        wide = dot(picks, values).astype(values.dtype)
        wide = lax.dot_general(
            wide, picks, (((1,), (1,)), ((), ())), preferred_element_type=jnp.float32
        )
        row = lax.broadcasted_iota(jnp.int32, (MXU, MXU), 0) % times
        column = lax.broadcasted_iota(jnp.int32, (MXU, MXU), 1) % times
        return jnp.where(row == column, wide, 0.0).astype(values.dtype)

    def repeat(values, times):
        empty = jnp.zeros_like(values)
        return jnp.concatenate(
            [
                jnp.concatenate([values if i == j else empty for j in range(times)], axis=1)
                for i in range(times)
            ],
            axis=0,
        )

    def kernel(queries_ref, left_inv_ref, right_inv_ref, out_ref, middle_ref, left_ref, right_ref):
        @pl.when(pl.program_id(0) == 0)
        def _():
            for layer in range(layers):
                left_ref[layer] = spread(left_inv_ref[layer], group)
                right_ref[layer] = repeat(right_inv_ref[layer], pair)

        for layer in range(layers):
            first = layer * k_out * k_in
            stack = jnp.concatenate(
                [queries_ref[:, first + p * MXU : first + (p + 1) * MXU] for p in range(wide)], axis=0
            )
            middle_ref[...] = dot(stack, right_ref[layer])
            for q in range(0, rows, both):
                halves = []
                for start in (q, q + group):
                    tiles = []
                    for p in range(wide):
                        at = p * rows + start
                        for s in range(pair):
                            tiles.append(middle_ref[at : at + group, s * k_in : (s + 1) * k_in])
                    halves.append(jnp.concatenate(tiles, axis=0))
                middle = jnp.concatenate(halves, axis=1).astype(queries_ref.dtype)
                result = dot(left_ref[layer], middle)
                for a in range(k_out):
                    at = a * group
                    tile = jnp.concatenate(
                        [result[at : at + group, :k_in], result[at : at + group, k_in:]], axis=0
                    )
                    lanes = first + a * k_in
                    out_ref[q : q + both, lanes : lanes + k_in] = tile.astype(out_ref.dtype)

    return call(
        kernel,
        jax.ShapeDtypeStruct(queries.shape, queries.dtype),
        (total // rows,),
        [
            pl.BlockSpec((rows, features), lambda i: (i, 0)),
            pl.BlockSpec(left_inv.shape, lambda i: (0, 0, 0)),
            pl.BlockSpec(right_inv.shape, lambda i: (0, 0, 0)),
        ],
        pl.BlockSpec((rows, features), lambda i: (i, 0)),
        40000 * total * features,
        4 * total * features,
        scratch=[
            pltpu.VMEM((wide * rows, MXU), jnp.float32),
            pltpu.VMEM((layers, MXU, MXU), left_inv.dtype),
            pltpu.VMEM((layers, MXU, MXU), right_inv.dtype),
        ],
    )(queries, left_inv, right_inv)


def after(value, *earlier):
    return lax.optimization_barrier((value, *earlier))[0]


def on_device(doc_grads, query_grads, left_inv, right_inv, cand_owner, cand_row):
    devices = lax.axis_size("docs")
    half = devices // 2
    me = lax.axis_index("docs").astype(jnp.int32).reshape(1)
    base = me & -half
    doc_count = doc_grads.shape[0] // devices
    entries = cand_row.shape[0]
    width = doc_grads.shape[1]
    scale = query_grads.shape[1] ** (-0.5)

    def swap(values, k):
        return lax.ppermute(values, "docs", [(i, i ^ k) for i in range(devices)])

    def exchange(values):
        return lax.all_to_all(values, "docs", split_axis=0, concat_axis=0, tiled=True)

    tail = width // 8 if width % (4 * LANES) == 0 else 0
    if not tail:
        own_ids = cand_owner[:, 0] * doc_count + cand_row
        ids = exchange(jnp.broadcast_to(own_ids, (devices, 1, entries)))
        picked = gather_rows(jnp.zeros((1,), jnp.int32), ids, [doc_grads.T], devices)
        return score_all(precondition(query_grads, left_inv, right_inv), exchange(picked), scale)

    own_tail, own_ids = prepare(doc_grads, cand_owner, cand_row, devices, tail)
    across = swap(own_tail, half)
    ids = exchange(own_ids)
    table = after(doc_grads, own_ids).T
    quarter = half // 2
    far = [half, half + 1, *range(half + quarter, devices), *range(half + 2, half + quarter)]
    first, flight = far[:2], 5
    body = [(table, width - tail)]
    ids = after(ids, across)
    pieces = dict(zip(far, gather_pieces(me, ids, body, first)))
    came = {k: swap(pieces[k], k) for k in first}
    ids = after(ids, pieces[far[0]])
    picked = gather_rows(base, ids, [table, across], half)
    ids = after(ids, picked)
    pieces.update(zip(far[2:], gather_pieces(me, ids, body, far[2:])))
    ready = [came[k] for k in first]
    near = lax.all_to_all(
        after(picked, *ready),
        "docs",
        split_axis=0,
        concat_axis=0,
        axis_index_groups=[list(range(half)), list(range(half, devices))],
        tiled=True,
    )
    prepared = precondition(after(query_grads, *ready), left_inv, right_inv)
    for i, k in enumerate(far[2:]):
        before = ready if i < flight else [*ready, prepared]
        came[k] = swap(after(pieces[k], *before), k)
    total = score_near(base, prepared, near, width, half)
    total = score_pieces(me, prepared, {k: came[k] for k in far[:2]}, total, width, 1.0)
    return score_pieces(me, prepared, {k: came[k] for k in far[2:]}, total, width, scale)


def solution(mesh):
    placed = (
        P("parts", "docs"),
        P(("parts", "docs"), None),
        P(),
        P(),
        P(("parts", "docs"), None),
        P(("parts", "docs")),
    )
    return jax.shard_map(
        on_device, mesh=mesh, in_specs=placed, out_specs=P(("parts", "docs"), None), check_vma=False
    )
```

```python
import jax
import jax.numpy as jnp
from jax import lax
from jax.experimental import pallas as pl
from jax.experimental.pallas import tpu as pltpu
from jax.sharding import PartitionSpec as P

LANES = 128
SUBLANES = 8
MXU = 256
VMEM_BYTES = 48 << 20
ALL_VMEM_BYTES = 63 << 20


def call(kernel, out_shape, grid, in_specs, out_specs, flops, bytes_accessed, scratch=(), prefetch=0, vmem=VMEM_BYTES):
    return pl.pallas_call(
        kernel,
        grid_spec=pltpu.PrefetchScalarGridSpec(
            num_scalar_prefetch=prefetch,
            grid=grid,
            in_specs=in_specs,
            out_specs=out_specs,
            scratch_shapes=scratch,
        ),
        out_shape=out_shape,
        compiler_params=pltpu.CompilerParams(vmem_limit_bytes=vmem),
        cost_estimate=pl.CostEstimate(flops=flops, bytes_accessed=bytes_accessed, transcendentals=0),
    )


def dot(a, b):
    return jnp.dot(a, b, preferred_element_type=jnp.float32)


def one_hot(ids, docs):
    group, row = ids // LANES, ids % LANES
    in_group = (lax.broadcasted_iota(jnp.int32, (LANES, ids.shape[1]), 0) == row).astype(jnp.bfloat16)
    return jnp.concatenate(
        [in_group * (group == g).astype(jnp.bfloat16) for g in range(docs // LANES)], axis=0
    )


def prepare(doc_grads, owners, rows, devices, tail):
    docs, width = doc_grads.shape
    entries = rows.shape[0]
    doc_count = docs // devices
    block = max(tail, LANES)

    def kernel(docs_hbm, owners_hbm, rows_hbm, tail_ref, ids_ref, docs_ref, owners_ref, rows_ref, sems):
        copies = [
            pltpu.make_async_copy(docs_hbm.at[:, width - block :], docs_ref, sems.at[0]),
            pltpu.make_async_copy(owners_hbm, owners_ref, sems.at[1]),
            pltpu.make_async_copy(rows_hbm, rows_ref, sems.at[2]),
        ]
        for copy in copies:
            copy.start()
        for copy in copies:
            copy.wait()
        tail_ref[...] = docs_ref[...].T[block - tail :, :]
        ids = owners_ref[...] * doc_count + rows_ref[...]
        ids_ref[...] = jnp.broadcast_to(ids[None], ids_ref.shape)

    return call(
        kernel,
        [
            pltpu.HBM((tail, docs), doc_grads.dtype),
            pltpu.HBM((devices, 1, entries), jnp.int32),
        ],
        (1,),
        [pl.BlockSpec(memory_space=pltpu.HBM)] * 3,
        [
            pl.BlockSpec((tail, docs), lambda i: (0, 0)),
            pl.BlockSpec((devices, 1, entries), lambda i: (0, 0, 0)),
        ],
        0,
        2 * docs * (block + tail),
        scratch=[
            pltpu.VMEM((docs, block), doc_grads.dtype),
            pltpu.VMEM((1, entries), jnp.int32),
            pltpu.VMEM((1, entries), jnp.int32),
            pltpu.SemaphoreType.DMA((3,)),
        ],
        vmem=ALL_VMEM_BYTES,
    )(doc_grads, owners.reshape(1, entries), rows.reshape(1, entries))


def gather_rows(base, ids, tables, count):
    entries = ids.shape[2]
    docs = tables[0].shape[1]
    features = sum(t.shape[0] for t in tables)

    def kernel(base_ref, ids_ref, *refs):
        out_ref = refs[-1]
        hot = one_hot(ids_ref[0], docs)
        start = 0
        for table_ref in refs[:-1]:
            stop = start + table_ref.shape[0]
            out_ref[0, start:stop, :] = dot(table_ref[...], hot).astype(out_ref.dtype)
            start = stop

    return call(
        kernel,
        pltpu.HBM((count, features, entries), tables[0].dtype),
        (count,),
        [pl.BlockSpec((1, 1, entries), lambda b, base: (base[0] + b, 0, 0))]
        + [pl.BlockSpec(t.shape, lambda b, base: (0, 0)) for t in tables],
        pl.BlockSpec((1, features, entries), lambda b, base: (b, 0, 0)),
        1000,
        1000,
        prefetch=1,
    )(base, ids, *tables)


def gather_pieces(me, ids, tables, partners):
    entries = ids.shape[2]
    docs = tables[0][0].shape[1]
    features = sum(rows for _, rows in tables)
    count = len(partners)

    def kernel(me_ref, *refs):
        table_refs = refs[count : count + len(tables)]
        for ids_ref, out_ref in zip(refs[:count], refs[count + len(tables) :]):
            hot = one_hot(ids_ref[0], docs)
            start = 0
            for table_ref in table_refs:
                stop = start + table_ref.shape[0]
                out_ref[start:stop, :] = dot(table_ref[...], hot).astype(out_ref.dtype)
                start = stop

    return call(
        kernel,
        [pltpu.HBM((features, entries), tables[0][0].dtype)] * count,
        (1,),
        [pl.BlockSpec((1, 1, entries), lambda i, me, k=k: (me[0] ^ k, 0, 0)) for k in partners]
        + [pl.BlockSpec((rows, docs), lambda i, me: (0, 0)) for _, rows in tables],
        [pl.BlockSpec((features, entries), lambda i, me: (0, 0))] * count,
        1000,
        1000,
        prefetch=1,
    )(me, *[ids] * count, *[table for table, _ in tables])


def padded(values, above, below):
    zeros = lambda rows: [jnp.zeros((rows, values.shape[1]), values.dtype)] if rows else []
    return jnp.concatenate([*zeros(above), values, *zeros(below)], axis=0)


def score_pieces(me, prepared, chosen, total, width, scale):
    queries = prepared.shape[0]
    features, entries = next(iter(chosen.values())).shape
    count = len(chosen)
    whole = pl.BlockSpec((queries, entries), lambda i, me: (0, 0))

    def kernel(me_ref, *refs):
        out = refs[-2][...]
        for prepared_ref, chosen_ref in zip(refs[:count], refs[count : 2 * count]):
            out = out + dot(prepared_ref[...], padded(chosen_ref[...], 0, width - features))
        refs[-1][...] = out * scale

    return call(
        kernel,
        jax.ShapeDtypeStruct((queries, entries), jnp.float32),
        (1,),
        [pl.BlockSpec((queries, width), lambda i, me, k=k: (0, me[0] ^ k)) for k in chosen]
        + [pl.BlockSpec((features, entries), lambda i, me: (0, 0))] * count
        + [whole],
        whole,
        2 * count * features * queries * entries,
        2 * count * features * (queries + entries) + 8 * queries * entries,
        prefetch=1,
    )(me, *[prepared] * count, *chosen.values(), total)


def score_near(base, prepared, chosen, width, half):
    queries = prepared.shape[0]
    count, features, entries = chosen.shape
    tail = features - width
    block = max(tail, LANES)
    stride = width // block

    def kernel(base_ref, own_ref, far_ref, chosen_ref, out_ref):
        part = dot(own_ref[...], chosen_ref[0, :width, :])
        part += dot(far_ref[...], padded(chosen_ref[0, width:, :], block - tail, 0))

        @pl.when(pl.program_id(0) == 0)
        def _():
            out_ref[...] = part

        @pl.when(pl.program_id(0) > 0)
        def _():
            out_ref[...] += part

    return call(
        kernel,
        jax.ShapeDtypeStruct((queries, entries), jnp.float32),
        (count,),
        [
            pl.BlockSpec((queries, width), lambda j, base: (0, base[0] + j)),
            pl.BlockSpec(
                (queries, block), lambda j, base: (0, ((base[0] + j) ^ half) * stride + stride - 1)
            ),
            pl.BlockSpec((1, features, entries), lambda j, base: (j, 0, 0)),
        ],
        pl.BlockSpec((queries, entries), lambda j, base: (0, 0)),
        2 * count * features * queries * entries,
        2 * count * features * (queries + entries) + 4 * queries * entries,
        prefetch=1,
    )(base, prepared, prepared, chosen)


def score_all(prepared, chosen, scale):
    queries = prepared.shape[0]
    devices, width, entries = chosen.shape

    def kernel(prepared_ref, chosen_ref, out_ref):
        part = dot(prepared_ref[...], chosen_ref[...]) * scale

        @pl.when(pl.program_id(0) == 0)
        def _():
            out_ref[...] = part

        @pl.when(pl.program_id(0) > 0)
        def _():
            out_ref[...] += part

    steps = 4
    block = devices * width // steps
    return call(
        kernel,
        jax.ShapeDtypeStruct((queries, entries), jnp.float32),
        (steps,),
        [
            pl.BlockSpec((queries, block), lambda i: (0, i)),
            pl.BlockSpec((block, entries), lambda i: (i, 0)),
        ],
        pl.BlockSpec((queries, entries), lambda i: (0, 0)),
        2 * devices * width * queries * entries,
        2 * devices * width * (queries + entries) + 4 * queries * entries,
    )(prepared, chosen.reshape(devices * width, entries))


def precondition(queries, left_inv, right_inv):
    total, features = queries.shape
    layers, k_out, _ = left_inv.shape
    k_in = right_inv.shape[1]
    group = MXU // k_out
    pair = MXU // k_in
    rows = 64
    wide = k_out // pair
    both = 2 * group

    def spread(values, times):
        size = values.shape[0]
        rows = lax.broadcasted_iota(jnp.int32, (MXU, size), 0) // times
        picks = (rows == lax.broadcasted_iota(jnp.int32, (MXU, size), 1)).astype(values.dtype)
        wide = dot(picks, values).astype(values.dtype)
        wide = lax.dot_general(
            wide, picks, (((1,), (1,)), ((), ())), preferred_element_type=jnp.float32
        )
        row = lax.broadcasted_iota(jnp.int32, (MXU, MXU), 0) % times
        column = lax.broadcasted_iota(jnp.int32, (MXU, MXU), 1) % times
        return jnp.where(row == column, wide, 0.0).astype(values.dtype)

    def repeat(values, times):
        empty = jnp.zeros_like(values)
        return jnp.concatenate(
            [
                jnp.concatenate([values if i == j else empty for j in range(times)], axis=1)
                for i in range(times)
            ],
            axis=0,
        )

    def kernel(queries_ref, left_inv_ref, right_inv_ref, out_ref, middle_ref, left_ref, right_ref):
        @pl.when(pl.program_id(0) == 0)
        def _():
            for layer in range(layers):
                left_ref[layer] = spread(left_inv_ref[layer], group)
                right_ref[layer] = repeat(right_inv_ref[layer], pair)

        for layer in range(layers):
            first = layer * k_out * k_in
            stack = jnp.concatenate(
                [queries_ref[:, first + p * MXU : first + (p + 1) * MXU] for p in range(wide)], axis=0
            )
            middle_ref[...] = dot(stack, right_ref[layer])
            for q in range(0, rows, both):
                halves = []
                for start in (q, q + group):
                    tiles = []
                    for p in range(wide):
                        at = p * rows + start
                        for s in range(pair):
                            tiles.append(middle_ref[at : at + group, s * k_in : (s + 1) * k_in])
                    halves.append(jnp.concatenate(tiles, axis=0))
                middle = jnp.concatenate(halves, axis=1).astype(queries_ref.dtype)
                result = dot(left_ref[layer], middle)
                for a in range(k_out):
                    at = a * group
                    tile = jnp.concatenate(
                        [result[at : at + group, :k_in], result[at : at + group, k_in:]], axis=0
                    )
                    lanes = first + a * k_in
                    out_ref[q : q + both, lanes : lanes + k_in] = tile.astype(out_ref.dtype)

    return call(
        kernel,
        jax.ShapeDtypeStruct(queries.shape, queries.dtype),
        (total // rows,),
        [
            pl.BlockSpec((rows, features), lambda i: (i, 0)),
            pl.BlockSpec(left_inv.shape, lambda i: (0, 0, 0)),
            pl.BlockSpec(right_inv.shape, lambda i: (0, 0, 0)),
        ],
        pl.BlockSpec((rows, features), lambda i: (i, 0)),
        40000 * total * features,
        4 * total * features,
        scratch=[
            pltpu.VMEM((wide * rows, MXU), jnp.float32),
            pltpu.VMEM((layers, MXU, MXU), left_inv.dtype),
            pltpu.VMEM((layers, MXU, MXU), right_inv.dtype),
        ],
    )(queries, left_inv, right_inv)


def after(value, *earlier):
    return lax.optimization_barrier((value, *earlier))[0]


def on_device(doc_grads, query_grads, left_inv, right_inv, cand_owner, cand_row):
    devices = lax.axis_size("docs")
    half = devices // 2
    me = lax.axis_index("docs").astype(jnp.int32).reshape(1)
    base = me & -half
    doc_count = doc_grads.shape[0] // devices
    entries = cand_row.shape[0]
    width = doc_grads.shape[1]
    scale = query_grads.shape[1] ** (-0.5)

    def swap(values, k):
        return lax.ppermute(values, "docs", [(i, i ^ k) for i in range(devices)])

    def exchange(values):
        return lax.all_to_all(values, "docs", split_axis=0, concat_axis=0, tiled=True)

    tail = width // 8 if width % (4 * LANES) == 0 else 0
    if not tail:
        own_ids = cand_owner[:, 0] * doc_count + cand_row
        ids = exchange(jnp.broadcast_to(own_ids, (devices, 1, entries)))
        picked = gather_rows(jnp.zeros((1,), jnp.int32), ids, [doc_grads.T], devices)
        return score_all(precondition(query_grads, left_inv, right_inv), exchange(picked), scale)

    own_tail, own_ids = prepare(doc_grads, cand_owner, cand_row, devices, tail)
    across = swap(own_tail, half)
    ids = exchange(own_ids)
    table = after(doc_grads, own_ids).T
    quarter = half // 2
    far = [half, half + 1, *range(half + quarter, devices), *range(half + 2, half + quarter)]
    first, second, third = far[:2], far[2 : 2 + quarter], far[2 + quarter :]
    body = [(table, width - tail)]
    ids = after(ids, across)
    pieces = dict(zip(far, gather_pieces(me, ids, body, first)))
    came = {k: swap(pieces[k], k) for k in first}
    ids = after(ids, pieces[first[0]])
    pieces.update(zip(far[2:], gather_pieces(me, ids, body, far[2:])))
    ids = after(ids, pieces[second[0]])
    picked = gather_rows(base, ids, [table, across], half)
    near = lax.all_to_all(
        picked,
        "docs",
        split_axis=0,
        concat_axis=0,
        axis_index_groups=[list(range(half)), list(range(half, devices))],
        tiled=True,
    )
    ready = [came[k] for k in first]
    prepared = precondition(after(query_grads, *ready), left_inv, right_inv)
    for k in second:
        came[k] = swap(after(pieces[k], *ready), k)
    for k, earlier in zip(third, second[::-1]):
        came[k] = swap(after(pieces[k], came[earlier], prepared), k)
    total = score_near(base, prepared, near, width, half)
    total = score_pieces(me, prepared, {k: came[k] for k in first}, total, width, 1.0)
    return score_pieces(me, prepared, {k: came[k] for k in second + third}, total, width, scale)


def solution(mesh):
    placed = (
        P("parts", "docs"),
        P(("parts", "docs"), None),
        P(),
        P(),
        P(("parts", "docs"), None),
        P(("parts", "docs")),
    )
    return jax.shard_map(
        on_device, mesh=mesh, in_specs=placed, out_specs=P(("parts", "docs"), None), check_vma=False
    )
```

```python
import jax
import jax.numpy as jnp
from jax import lax
from jax.experimental import pallas as pl
from jax.experimental.pallas import tpu as pltpu
from jax.sharding import PartitionSpec as P

LANES = 128
SUBLANES = 8
MXU = 256
VMEM_BYTES = 48 << 20
ALL_VMEM_BYTES = 63 << 20


def call(kernel, out_shape, grid, in_specs, out_specs, flops, bytes_accessed, scratch=(), prefetch=0, vmem=VMEM_BYTES):
    return pl.pallas_call(
        kernel,
        grid_spec=pltpu.PrefetchScalarGridSpec(
            num_scalar_prefetch=prefetch,
            grid=grid,
            in_specs=in_specs,
            out_specs=out_specs,
            scratch_shapes=scratch,
        ),
        out_shape=out_shape,
        compiler_params=pltpu.CompilerParams(vmem_limit_bytes=vmem),
        cost_estimate=pl.CostEstimate(flops=flops, bytes_accessed=bytes_accessed, transcendentals=0),
    )


def dot(a, b):
    return jnp.dot(a, b, preferred_element_type=jnp.float32)


def one_hot(ids, docs):
    group, row = ids // LANES, ids % LANES
    in_group = (lax.broadcasted_iota(jnp.int32, (LANES, ids.shape[1]), 0) == row).astype(jnp.bfloat16)
    return jnp.concatenate(
        [in_group * (group == g).astype(jnp.bfloat16) for g in range(docs // LANES)], axis=0
    )


def prepare(doc_grads, owners, rows, devices, tail):
    docs, width = doc_grads.shape
    entries = rows.shape[0]
    doc_count = docs // devices
    block = max(tail, LANES)

    def kernel(docs_hbm, owners_hbm, rows_hbm, tail_ref, ids_ref, docs_ref, owners_ref, rows_ref, sems):
        copies = [
            pltpu.make_async_copy(docs_hbm.at[:, width - block :], docs_ref, sems.at[0]),
            pltpu.make_async_copy(owners_hbm, owners_ref, sems.at[1]),
            pltpu.make_async_copy(rows_hbm, rows_ref, sems.at[2]),
        ]
        for copy in copies:
            copy.start()
        for copy in copies:
            copy.wait()
        tail_ref[...] = docs_ref[...].T[block - tail :, :]
        ids = owners_ref[...] * doc_count + rows_ref[...]
        ids_ref[...] = jnp.broadcast_to(ids[None], ids_ref.shape)

    return call(
        kernel,
        [
            pltpu.HBM((tail, docs), doc_grads.dtype),
            pltpu.HBM((devices, 1, entries), jnp.int32),
        ],
        (1,),
        [pl.BlockSpec(memory_space=pltpu.HBM)] * 3,
        [
            pl.BlockSpec((tail, docs), lambda i: (0, 0)),
            pl.BlockSpec((devices, 1, entries), lambda i: (0, 0, 0)),
        ],
        0,
        2 * docs * (block + tail),
        scratch=[
            pltpu.VMEM((docs, block), doc_grads.dtype),
            pltpu.VMEM((1, entries), jnp.int32),
            pltpu.VMEM((1, entries), jnp.int32),
            pltpu.SemaphoreType.DMA((3,)),
        ],
        vmem=ALL_VMEM_BYTES,
    )(doc_grads, owners.reshape(1, entries), rows.reshape(1, entries))


def gather_rows(base, ids, tables, count):
    entries = ids.shape[2]
    docs = tables[0].shape[1]
    features = sum(t.shape[0] for t in tables)

    def kernel(base_ref, ids_ref, *refs):
        out_ref = refs[-1]
        hot = one_hot(ids_ref[0], docs)
        start = 0
        for table_ref in refs[:-1]:
            stop = start + table_ref.shape[0]
            out_ref[0, start:stop, :] = dot(table_ref[...], hot).astype(out_ref.dtype)
            start = stop

    return call(
        kernel,
        pltpu.HBM((count, features, entries), tables[0].dtype),
        (count,),
        [pl.BlockSpec((1, 1, entries), lambda b, base: (base[0] + b, 0, 0))]
        + [pl.BlockSpec(t.shape, lambda b, base: (0, 0)) for t in tables],
        pl.BlockSpec((1, features, entries), lambda b, base: (b, 0, 0)),
        1000,
        1000,
        prefetch=1,
    )(base, ids, *tables)


def gather_pieces(me, ids, tables, partners):
    entries = ids.shape[2]
    docs = tables[0][0].shape[1]
    features = sum(rows for _, rows in tables)
    count = len(partners)

    def kernel(me_ref, *refs):
        table_refs = refs[count : count + len(tables)]
        for ids_ref, out_ref in zip(refs[:count], refs[count + len(tables) :]):
            hot = one_hot(ids_ref[0], docs)
            start = 0
            for table_ref in table_refs:
                stop = start + table_ref.shape[0]
                out_ref[start:stop, :] = dot(table_ref[...], hot).astype(out_ref.dtype)
                start = stop

    return call(
        kernel,
        [pltpu.HBM((features, entries), tables[0][0].dtype)] * count,
        (1,),
        [pl.BlockSpec((1, 1, entries), lambda i, me, k=k: (me[0] ^ k, 0, 0)) for k in partners]
        + [pl.BlockSpec((rows, docs), lambda i, me: (0, 0)) for _, rows in tables],
        [pl.BlockSpec((features, entries), lambda i, me: (0, 0))] * count,
        1000,
        1000,
        prefetch=1,
    )(me, *[ids] * count, *[table for table, _ in tables])


def padded(values, above, below):
    zeros = lambda rows: [jnp.zeros((rows, values.shape[1]), values.dtype)] if rows else []
    return jnp.concatenate([*zeros(above), values, *zeros(below)], axis=0)


def score_pieces(me, prepared, chosen, total, width, scale):
    queries = prepared.shape[0]
    features, entries = next(iter(chosen.values())).shape
    count = len(chosen)
    whole = pl.BlockSpec((queries, entries), lambda i, me: (0, 0))

    def kernel(me_ref, *refs):
        out = refs[-2][...]
        for prepared_ref, chosen_ref in zip(refs[:count], refs[count : 2 * count]):
            out = out + dot(prepared_ref[...], padded(chosen_ref[...], 0, width - features))
        refs[-1][...] = out * scale

    return call(
        kernel,
        jax.ShapeDtypeStruct((queries, entries), jnp.float32),
        (1,),
        [pl.BlockSpec((queries, width), lambda i, me, k=k: (0, me[0] ^ k)) for k in chosen]
        + [pl.BlockSpec((features, entries), lambda i, me: (0, 0))] * count
        + [whole],
        whole,
        2 * count * features * queries * entries,
        2 * count * features * (queries + entries) + 8 * queries * entries,
        prefetch=1,
    )(me, *[prepared] * count, *chosen.values(), total)


def score_near(base, prepared, chosen, width, half):
    queries = prepared.shape[0]
    count, features, entries = chosen.shape
    tail = features - width
    block = max(tail, LANES)
    stride = width // block

    def kernel(base_ref, own_ref, far_ref, chosen_ref, out_ref):
        part = dot(own_ref[...], chosen_ref[0, :width, :])
        part += dot(far_ref[...], padded(chosen_ref[0, width:, :], block - tail, 0))

        @pl.when(pl.program_id(0) == 0)
        def _():
            out_ref[...] = part

        @pl.when(pl.program_id(0) > 0)
        def _():
            out_ref[...] += part

    return call(
        kernel,
        jax.ShapeDtypeStruct((queries, entries), jnp.float32),
        (count,),
        [
            pl.BlockSpec((queries, width), lambda j, base: (0, base[0] + j)),
            pl.BlockSpec(
                (queries, block), lambda j, base: (0, ((base[0] + j) ^ half) * stride + stride - 1)
            ),
            pl.BlockSpec((1, features, entries), lambda j, base: (j, 0, 0)),
        ],
        pl.BlockSpec((queries, entries), lambda j, base: (0, 0)),
        2 * count * features * queries * entries,
        2 * count * features * (queries + entries) + 4 * queries * entries,
        prefetch=1,
    )(base, prepared, prepared, chosen)


def score_all(prepared, chosen, scale):
    queries = prepared.shape[0]
    devices, width, entries = chosen.shape

    def kernel(prepared_ref, chosen_ref, out_ref):
        part = dot(prepared_ref[...], chosen_ref[...]) * scale

        @pl.when(pl.program_id(0) == 0)
        def _():
            out_ref[...] = part

        @pl.when(pl.program_id(0) > 0)
        def _():
            out_ref[...] += part

    steps = 4
    block = devices * width // steps
    return call(
        kernel,
        jax.ShapeDtypeStruct((queries, entries), jnp.float32),
        (steps,),
        [
            pl.BlockSpec((queries, block), lambda i: (0, i)),
            pl.BlockSpec((block, entries), lambda i: (i, 0)),
        ],
        pl.BlockSpec((queries, entries), lambda i: (0, 0)),
        2 * devices * width * queries * entries,
        2 * devices * width * (queries + entries) + 4 * queries * entries,
    )(prepared, chosen.reshape(devices * width, entries))


def precondition(queries, left_inv, right_inv):
    total, features = queries.shape
    layers, k_out, _ = left_inv.shape
    k_in = right_inv.shape[1]
    group = MXU // k_out
    pair = MXU // k_in
    rows = 64
    wide = k_out // pair
    both = 2 * group

    def spread(values, times):
        size = values.shape[0]
        rows = lax.broadcasted_iota(jnp.int32, (MXU, size), 0) // times
        picks = (rows == lax.broadcasted_iota(jnp.int32, (MXU, size), 1)).astype(values.dtype)
        wide = dot(picks, values).astype(values.dtype)
        wide = lax.dot_general(
            wide, picks, (((1,), (1,)), ((), ())), preferred_element_type=jnp.float32
        )
        row = lax.broadcasted_iota(jnp.int32, (MXU, MXU), 0) % times
        column = lax.broadcasted_iota(jnp.int32, (MXU, MXU), 1) % times
        return jnp.where(row == column, wide, 0.0).astype(values.dtype)

    def repeat(values, times):
        empty = jnp.zeros_like(values)
        return jnp.concatenate(
            [
                jnp.concatenate([values if i == j else empty for j in range(times)], axis=1)
                for i in range(times)
            ],
            axis=0,
        )

    def kernel(queries_ref, left_inv_ref, right_inv_ref, out_ref, middle_ref, left_ref, right_ref):
        @pl.when(pl.program_id(0) == 0)
        def _():
            for layer in range(layers):
                left_ref[layer] = spread(left_inv_ref[layer], group)
                right_ref[layer] = repeat(right_inv_ref[layer], pair)

        for layer in range(layers):
            first = layer * k_out * k_in
            stack = jnp.concatenate(
                [queries_ref[:, first + p * MXU : first + (p + 1) * MXU] for p in range(wide)], axis=0
            )
            middle_ref[...] = dot(stack, right_ref[layer])
            for q in range(0, rows, both):
                halves = []
                for start in (q, q + group):
                    tiles = []
                    for p in range(wide):
                        at = p * rows + start
                        for s in range(pair):
                            tiles.append(middle_ref[at : at + group, s * k_in : (s + 1) * k_in])
                    halves.append(jnp.concatenate(tiles, axis=0))
                middle = jnp.concatenate(halves, axis=1).astype(queries_ref.dtype)
                result = dot(left_ref[layer], middle)
                for a in range(k_out):
                    at = a * group
                    tile = jnp.concatenate(
                        [result[at : at + group, :k_in], result[at : at + group, k_in:]], axis=0
                    )
                    lanes = first + a * k_in
                    out_ref[q : q + both, lanes : lanes + k_in] = tile.astype(out_ref.dtype)

    return call(
        kernel,
        jax.ShapeDtypeStruct(queries.shape, queries.dtype),
        (total // rows,),
        [
            pl.BlockSpec((rows, features), lambda i: (i, 0)),
            pl.BlockSpec(left_inv.shape, lambda i: (0, 0, 0)),
            pl.BlockSpec(right_inv.shape, lambda i: (0, 0, 0)),
        ],
        pl.BlockSpec((rows, features), lambda i: (i, 0)),
        40000 * total * features,
        4 * total * features,
        scratch=[
            pltpu.VMEM((wide * rows, MXU), jnp.float32),
            pltpu.VMEM((layers, MXU, MXU), left_inv.dtype),
            pltpu.VMEM((layers, MXU, MXU), right_inv.dtype),
        ],
    )(queries, left_inv, right_inv)


def after(value, *earlier):
    return lax.optimization_barrier((value, *earlier))[0]


def on_device(doc_grads, query_grads, left_inv, right_inv, cand_owner, cand_row):
    devices = lax.axis_size("docs")
    half = devices // 2
    me = lax.axis_index("docs").astype(jnp.int32).reshape(1)
    base = me & -half
    doc_count = doc_grads.shape[0] // devices
    entries = cand_row.shape[0]
    width = doc_grads.shape[1]
    scale = query_grads.shape[1] ** (-0.5)

    def swap(values, k):
        return lax.ppermute(values, "docs", [(i, i ^ k) for i in range(devices)])

    def exchange(values):
        return lax.all_to_all(values, "docs", split_axis=0, concat_axis=0, tiled=True)

    tail = width // 8 if width % (4 * LANES) == 0 else 0
    if not tail:
        own_ids = cand_owner[:, 0] * doc_count + cand_row
        ids = exchange(jnp.broadcast_to(own_ids, (devices, 1, entries)))
        picked = gather_rows(jnp.zeros((1,), jnp.int32), ids, [doc_grads.T], devices)
        return score_all(precondition(query_grads, left_inv, right_inv), exchange(picked), scale)

    own_tail, own_ids = prepare(doc_grads, cand_owner, cand_row, devices, tail)
    across = swap(own_tail, half)
    ids = exchange(own_ids)
    table = after(doc_grads, own_ids).T
    quarter = half // 2
    first, second = list(range(half + quarter, devices)), list(range(half, half + quarter))
    body = [(table, width - tail)]
    ids = after(ids, across)
    pieces = dict(zip(first, gather_pieces(me, ids, body, first)))
    came = {k: swap(pieces[k], k) for k in first}
    ids = after(ids, pieces[first[0]])
    picked = gather_rows(base, ids, [table, across], half)
    near = lax.all_to_all(
        picked,
        "docs",
        split_axis=0,
        concat_axis=0,
        axis_index_groups=[list(range(half)), list(range(half, devices))],
        tiled=True,
    )
    ids = after(ids, picked)
    pieces.update(zip(second, gather_pieces(me, ids, body, second)))
    prepared = precondition(after(query_grads, *[came[k] for k in first[:2]]), left_inv, right_inv)
    for i, (k, earlier) in enumerate(zip(second, first)):
        before = [came[earlier], prepared] if i == quarter - 1 else [came[earlier]]
        came[k] = swap(after(pieces[k], *before), k)
    total = score_near(base, prepared, near, width, half)
    last = second[quarter // 2 :]
    others = [k for k in came if k not in last]
    total = score_pieces(me, prepared, {k: came[k] for k in others}, total, width, 1.0)
    return score_pieces(me, prepared, {k: came[k] for k in last}, total, width, scale)


def solution(mesh):
    placed = (
        P("parts", "docs"),
        P(("parts", "docs"), None),
        P(),
        P(),
        P(("parts", "docs"), None),
        P(("parts", "docs")),
    )
    return jax.shard_map(
        on_device, mesh=mesh, in_specs=placed, out_specs=P(("parts", "docs"), None), check_vma=False
    )
```

```python
import jax
import jax.numpy as jnp
from jax import lax
from jax.experimental import pallas as pl
from jax.experimental.pallas import tpu as pltpu
from jax.sharding import PartitionSpec as P

LANES = 128
SUBLANES = 8
MXU = 256
VMEM_BYTES = 48 << 20
ALL_VMEM_BYTES = 63 << 20


def call(kernel, out_shape, grid, in_specs, out_specs, flops, bytes_accessed, scratch=(), prefetch=0, vmem=VMEM_BYTES):
    return pl.pallas_call(
        kernel,
        grid_spec=pltpu.PrefetchScalarGridSpec(
            num_scalar_prefetch=prefetch,
            grid=grid,
            in_specs=in_specs,
            out_specs=out_specs,
            scratch_shapes=scratch,
        ),
        out_shape=out_shape,
        compiler_params=pltpu.CompilerParams(vmem_limit_bytes=vmem),
        cost_estimate=pl.CostEstimate(flops=flops, bytes_accessed=bytes_accessed, transcendentals=0),
    )


def dot(a, b):
    return jnp.dot(a, b, preferred_element_type=jnp.float32)


def one_hot(ids, docs):
    group, row = ids // LANES, ids % LANES
    in_group = (lax.broadcasted_iota(jnp.int32, (LANES, ids.shape[1]), 0) == row).astype(jnp.bfloat16)
    return jnp.concatenate(
        [in_group * (group == g).astype(jnp.bfloat16) for g in range(docs // LANES)], axis=0
    )


def prepare(doc_grads, owners, rows, devices, tail):
    docs, width = doc_grads.shape
    entries = rows.shape[0]
    doc_count = docs // devices
    block = max(tail, LANES)

    def kernel(docs_hbm, owners_hbm, rows_hbm, tail_ref, ids_ref, docs_ref, owners_ref, rows_ref, sems):
        copies = [
            pltpu.make_async_copy(docs_hbm.at[:, width - block :], docs_ref, sems.at[0]),
            pltpu.make_async_copy(owners_hbm, owners_ref, sems.at[1]),
            pltpu.make_async_copy(rows_hbm, rows_ref, sems.at[2]),
        ]
        for copy in copies:
            copy.start()
        for copy in copies:
            copy.wait()
        tail_ref[...] = docs_ref[...].T[block - tail :, :]
        ids = owners_ref[...] * doc_count + rows_ref[...]
        ids_ref[...] = jnp.broadcast_to(ids[None], ids_ref.shape)

    return call(
        kernel,
        [
            pltpu.HBM((tail, docs), doc_grads.dtype),
            pltpu.HBM((devices, 1, entries), jnp.int32),
        ],
        (1,),
        [pl.BlockSpec(memory_space=pltpu.HBM)] * 3,
        [
            pl.BlockSpec((tail, docs), lambda i: (0, 0)),
            pl.BlockSpec((devices, 1, entries), lambda i: (0, 0, 0)),
        ],
        0,
        2 * docs * (block + tail),
        scratch=[
            pltpu.VMEM((docs, block), doc_grads.dtype),
            pltpu.VMEM((1, entries), jnp.int32),
            pltpu.VMEM((1, entries), jnp.int32),
            pltpu.SemaphoreType.DMA((3,)),
        ],
        vmem=ALL_VMEM_BYTES,
    )(doc_grads, owners.reshape(1, entries), rows.reshape(1, entries))


def gather_rows(base, ids, tables, count):
    entries = ids.shape[2]
    docs = tables[0].shape[1]
    features = sum(t.shape[0] for t in tables)

    def kernel(base_ref, ids_ref, *refs):
        out_ref = refs[-1]
        hot = one_hot(ids_ref[0], docs)
        start = 0
        for table_ref in refs[:-1]:
            stop = start + table_ref.shape[0]
            out_ref[0, start:stop, :] = dot(table_ref[...], hot).astype(out_ref.dtype)
            start = stop

    return call(
        kernel,
        pltpu.HBM((count, features, entries), tables[0].dtype),
        (count,),
        [pl.BlockSpec((1, 1, entries), lambda b, base: (base[0] + b, 0, 0))]
        + [pl.BlockSpec(t.shape, lambda b, base: (0, 0)) for t in tables],
        pl.BlockSpec((1, features, entries), lambda b, base: (b, 0, 0)),
        1000,
        1000,
        prefetch=1,
    )(base, ids, *tables)


def gather_pieces(me, ids, tables, partners):
    entries = ids.shape[2]
    docs = tables[0][0].shape[1]
    features = sum(rows for _, rows in tables)
    count = len(partners)

    def kernel(me_ref, *refs):
        table_refs = refs[count : count + len(tables)]
        for ids_ref, out_ref in zip(refs[:count], refs[count + len(tables) :]):
            hot = one_hot(ids_ref[0], docs)
            start = 0
            for table_ref in table_refs:
                stop = start + table_ref.shape[0]
                out_ref[start:stop, :] = dot(table_ref[...], hot).astype(out_ref.dtype)
                start = stop

    return call(
        kernel,
        [pltpu.HBM((features, entries), tables[0][0].dtype)] * count,
        (1,),
        [pl.BlockSpec((1, 1, entries), lambda i, me, k=k: (me[0] ^ k, 0, 0)) for k in partners]
        + [pl.BlockSpec((rows, docs), lambda i, me: (0, 0)) for _, rows in tables],
        [pl.BlockSpec((features, entries), lambda i, me: (0, 0))] * count,
        1000,
        1000,
        prefetch=1,
    )(me, *[ids] * count, *[table for table, _ in tables])


def padded(values, above, below):
    zeros = lambda rows: [jnp.zeros((rows, values.shape[1]), values.dtype)] if rows else []
    return jnp.concatenate([*zeros(above), values, *zeros(below)], axis=0)


def score_pieces(me, prepared, chosen, total, width, scale):
    queries = prepared.shape[0]
    features, entries = next(iter(chosen.values())).shape
    count = len(chosen)
    whole = pl.BlockSpec((queries, entries), lambda i, me: (0, 0))

    def kernel(me_ref, *refs):
        out = refs[-2][...]
        for prepared_ref, chosen_ref in zip(refs[:count], refs[count : 2 * count]):
            out = out + dot(prepared_ref[...], padded(chosen_ref[...], 0, width - features))
        refs[-1][...] = out * scale

    return call(
        kernel,
        jax.ShapeDtypeStruct((queries, entries), jnp.float32),
        (1,),
        [pl.BlockSpec((queries, width), lambda i, me, k=k: (0, me[0] ^ k)) for k in chosen]
        + [pl.BlockSpec((features, entries), lambda i, me: (0, 0))] * count
        + [whole],
        whole,
        2 * count * features * queries * entries,
        2 * count * features * (queries + entries) + 8 * queries * entries,
        prefetch=1,
    )(me, *[prepared] * count, *chosen.values(), total)


def score_near(base, prepared, chosen, width, half):
    queries = prepared.shape[0]
    count, features, entries = chosen.shape
    tail = features - width
    block = max(tail, LANES)
    stride = width // block

    def kernel(base_ref, own_ref, far_ref, chosen_ref, out_ref):
        part = dot(own_ref[...], chosen_ref[0, :width, :])
        part += dot(far_ref[...], padded(chosen_ref[0, width:, :], block - tail, 0))

        @pl.when(pl.program_id(0) == 0)
        def _():
            out_ref[...] = part

        @pl.when(pl.program_id(0) > 0)
        def _():
            out_ref[...] += part

    return call(
        kernel,
        jax.ShapeDtypeStruct((queries, entries), jnp.float32),
        (count,),
        [
            pl.BlockSpec((queries, width), lambda j, base: (0, base[0] + j)),
            pl.BlockSpec(
                (queries, block), lambda j, base: (0, ((base[0] + j) ^ half) * stride + stride - 1)
            ),
            pl.BlockSpec((1, features, entries), lambda j, base: (j, 0, 0)),
        ],
        pl.BlockSpec((queries, entries), lambda j, base: (0, 0)),
        2 * count * features * queries * entries,
        2 * count * features * (queries + entries) + 4 * queries * entries,
        prefetch=1,
    )(base, prepared, prepared, chosen)


def score_all(prepared, chosen, scale):
    queries = prepared.shape[0]
    devices, width, entries = chosen.shape

    def kernel(prepared_ref, chosen_ref, out_ref):
        part = dot(prepared_ref[...], chosen_ref[...]) * scale

        @pl.when(pl.program_id(0) == 0)
        def _():
            out_ref[...] = part

        @pl.when(pl.program_id(0) > 0)
        def _():
            out_ref[...] += part

    steps = 4
    block = devices * width // steps
    return call(
        kernel,
        jax.ShapeDtypeStruct((queries, entries), jnp.float32),
        (steps,),
        [
            pl.BlockSpec((queries, block), lambda i: (0, i)),
            pl.BlockSpec((block, entries), lambda i: (i, 0)),
        ],
        pl.BlockSpec((queries, entries), lambda i: (0, 0)),
        2 * devices * width * queries * entries,
        2 * devices * width * (queries + entries) + 4 * queries * entries,
    )(prepared, chosen.reshape(devices * width, entries))


def precondition(queries, left_inv, right_inv):
    total, features = queries.shape
    layers, k_out, _ = left_inv.shape
    k_in = right_inv.shape[1]
    group = MXU // k_out
    pair = MXU // k_in
    rows = 64
    wide = k_out // pair
    both = 2 * group

    def spread(values, times):
        size = values.shape[0]
        rows = lax.broadcasted_iota(jnp.int32, (MXU, size), 0) // times
        picks = (rows == lax.broadcasted_iota(jnp.int32, (MXU, size), 1)).astype(values.dtype)
        wide = dot(picks, values).astype(values.dtype)
        wide = lax.dot_general(
            wide, picks, (((1,), (1,)), ((), ())), preferred_element_type=jnp.float32
        )
        row = lax.broadcasted_iota(jnp.int32, (MXU, MXU), 0) % times
        column = lax.broadcasted_iota(jnp.int32, (MXU, MXU), 1) % times
        return jnp.where(row == column, wide, 0.0).astype(values.dtype)

    def repeat(values, times):
        empty = jnp.zeros_like(values)
        return jnp.concatenate(
            [
                jnp.concatenate([values if i == j else empty for j in range(times)], axis=1)
                for i in range(times)
            ],
            axis=0,
        )

    def kernel(queries_ref, left_inv_ref, right_inv_ref, out_ref, middle_ref, left_ref, right_ref):
        @pl.when(pl.program_id(0) == 0)
        def _():
            for layer in range(layers):
                left_ref[layer] = spread(left_inv_ref[layer], group)
                right_ref[layer] = repeat(right_inv_ref[layer], pair)

        for layer in range(layers):
            first = layer * k_out * k_in
            stack = jnp.concatenate(
                [queries_ref[:, first + p * MXU : first + (p + 1) * MXU] for p in range(wide)], axis=0
            )
            middle_ref[...] = dot(stack, right_ref[layer])
            for q in range(0, rows, both):
                halves = []
                for start in (q, q + group):
                    tiles = []
                    for p in range(wide):
                        at = p * rows + start
                        for s in range(pair):
                            tiles.append(middle_ref[at : at + group, s * k_in : (s + 1) * k_in])
                    halves.append(jnp.concatenate(tiles, axis=0))
                middle = jnp.concatenate(halves, axis=1).astype(queries_ref.dtype)
                result = dot(left_ref[layer], middle)
                for a in range(k_out):
                    at = a * group
                    tile = jnp.concatenate(
                        [result[at : at + group, :k_in], result[at : at + group, k_in:]], axis=0
                    )
                    lanes = first + a * k_in
                    out_ref[q : q + both, lanes : lanes + k_in] = tile.astype(out_ref.dtype)

    return call(
        kernel,
        jax.ShapeDtypeStruct(queries.shape, queries.dtype),
        (total // rows,),
        [
            pl.BlockSpec((rows, features), lambda i: (i, 0)),
            pl.BlockSpec(left_inv.shape, lambda i: (0, 0, 0)),
            pl.BlockSpec(right_inv.shape, lambda i: (0, 0, 0)),
        ],
        pl.BlockSpec((rows, features), lambda i: (i, 0)),
        40000 * total * features,
        4 * total * features,
        scratch=[
            pltpu.VMEM((wide * rows, MXU), jnp.float32),
            pltpu.VMEM((layers, MXU, MXU), left_inv.dtype),
            pltpu.VMEM((layers, MXU, MXU), right_inv.dtype),
        ],
    )(queries, left_inv, right_inv)


def after(value, *earlier):
    return lax.optimization_barrier((value, *earlier))[0]


def on_device(doc_grads, query_grads, left_inv, right_inv, cand_owner, cand_row):
    devices = lax.axis_size("docs")
    half = devices // 2
    me = lax.axis_index("docs").astype(jnp.int32).reshape(1)
    base = me & -half
    doc_count = doc_grads.shape[0] // devices
    entries = cand_row.shape[0]
    width = doc_grads.shape[1]
    scale = query_grads.shape[1] ** (-0.5)

    def swap(values, k):
        return lax.ppermute(values, "docs", [(i, i ^ k) for i in range(devices)])

    def exchange(values):
        return lax.all_to_all(values, "docs", split_axis=0, concat_axis=0, tiled=True)

    tail = width // 8 if width % (4 * LANES) == 0 else 0
    if not tail:
        own_ids = cand_owner[:, 0] * doc_count + cand_row
        ids = exchange(jnp.broadcast_to(own_ids, (devices, 1, entries)))
        picked = gather_rows(jnp.zeros((1,), jnp.int32), ids, [doc_grads.T], devices)
        return score_all(precondition(query_grads, left_inv, right_inv), exchange(picked), scale)

    own_tail, own_ids = prepare(doc_grads, cand_owner, cand_row, devices, tail)
    across = swap(own_tail, half)
    ids = exchange(own_ids)
    table = after(doc_grads, own_ids).T
    quarter = half // 2
    first, second = list(range(half + quarter, devices)), list(range(half, half + quarter))
    body = [(table, width - tail)]
    ids = after(ids, across)
    pieces = dict(zip(first, gather_pieces(me, ids, body, first)))
    came = {k: swap(pieces[k], k) for k in first}
    ids = after(ids, pieces[first[0]])
    picked = gather_rows(base, ids, [table, across], half)
    near = lax.all_to_all(
        picked,
        "docs",
        split_axis=0,
        concat_axis=0,
        axis_index_groups=[list(range(half)), list(range(half, devices))],
        tiled=True,
    )
    ids = after(ids, picked)
    pieces.update(zip(second, gather_pieces(me, ids, body, second)))
    prepared = precondition(after(query_grads, *[came[k] for k in first[:2]]), left_inv, right_inv)
    for i, k in enumerate(second):
        before = [came[first[i - 1]]] if i else []
        if i == quarter - 1:
            before.append(prepared)
        came[k] = swap(after(pieces[k], *before) if before else pieces[k], k)
    total = score_near(base, prepared, near, width, half)
    last = second[-1:]
    others = [k for k in came if k not in last]
    total = score_pieces(me, prepared, {k: came[k] for k in others}, total, width, 1.0)
    return score_pieces(me, prepared, {k: came[k] for k in last}, total, width, scale)


def solution(mesh):
    placed = (
        P("parts", "docs"),
        P(("parts", "docs"), None),
        P(),
        P(),
        P(("parts", "docs"), None),
        P(("parts", "docs")),
    )
    return jax.shard_map(
        on_device, mesh=mesh, in_specs=placed, out_specs=P(("parts", "docs"), None), check_vma=False
    )
```

```python
import jax
import jax.numpy as jnp
from jax import lax
from jax.experimental import pallas as pl
from jax.experimental.pallas import tpu as pltpu
from jax.sharding import PartitionSpec as P

LANES = 128
SUBLANES = 8
MXU = 256
VMEM_BYTES = 48 << 20
ALL_VMEM_BYTES = 63 << 20


def call(kernel, out_shape, grid, in_specs, out_specs, flops, bytes_accessed, scratch=(), prefetch=0, vmem=VMEM_BYTES):
    return pl.pallas_call(
        kernel,
        grid_spec=pltpu.PrefetchScalarGridSpec(
            num_scalar_prefetch=prefetch,
            grid=grid,
            in_specs=in_specs,
            out_specs=out_specs,
            scratch_shapes=scratch,
        ),
        out_shape=out_shape,
        compiler_params=pltpu.CompilerParams(vmem_limit_bytes=vmem),
        cost_estimate=pl.CostEstimate(flops=flops, bytes_accessed=bytes_accessed, transcendentals=0),
    )


def dot(a, b):
    return jnp.dot(a, b, preferred_element_type=jnp.float32)


def one_hot(ids, docs):
    group, row = ids // LANES, ids % LANES
    in_group = (lax.broadcasted_iota(jnp.int32, (LANES, ids.shape[1]), 0) == row).astype(jnp.bfloat16)
    return jnp.concatenate(
        [in_group * (group == g).astype(jnp.bfloat16) for g in range(docs // LANES)], axis=0
    )


def prepare(doc_grads, owners, rows, devices, tail):
    docs, width = doc_grads.shape
    entries = rows.shape[0]
    doc_count = docs // devices
    block = max(tail, LANES)

    def kernel(docs_hbm, owners_hbm, rows_hbm, tail_ref, ids_ref, docs_ref, owners_ref, rows_ref, sems):
        copies = [
            pltpu.make_async_copy(docs_hbm.at[:, width - block :], docs_ref, sems.at[0]),
            pltpu.make_async_copy(owners_hbm, owners_ref, sems.at[1]),
            pltpu.make_async_copy(rows_hbm, rows_ref, sems.at[2]),
        ]
        for copy in copies:
            copy.start()
        for copy in copies:
            copy.wait()
        tail_ref[...] = docs_ref[...].T[block - tail :, :]
        ids = owners_ref[...] * doc_count + rows_ref[...]
        ids_ref[...] = jnp.broadcast_to(ids[None], ids_ref.shape)

    return call(
        kernel,
        [
            pltpu.HBM((tail, docs), doc_grads.dtype),
            pltpu.HBM((devices, 1, entries), jnp.int32),
        ],
        (1,),
        [pl.BlockSpec(memory_space=pltpu.HBM)] * 3,
        [
            pl.BlockSpec((tail, docs), lambda i: (0, 0)),
            pl.BlockSpec((devices, 1, entries), lambda i: (0, 0, 0)),
        ],
        0,
        2 * docs * (block + tail),
        scratch=[
            pltpu.VMEM((docs, block), doc_grads.dtype),
            pltpu.VMEM((1, entries), jnp.int32),
            pltpu.VMEM((1, entries), jnp.int32),
            pltpu.SemaphoreType.DMA((3,)),
        ],
        vmem=ALL_VMEM_BYTES,
    )(doc_grads, owners.reshape(1, entries), rows.reshape(1, entries))


def gather_rows(base, ids, tables, count):
    entries = ids.shape[2]
    docs = tables[0].shape[1]
    features = sum(t.shape[0] for t in tables)

    def kernel(base_ref, ids_ref, *refs):
        out_ref = refs[-1]
        hot = one_hot(ids_ref[0], docs)
        start = 0
        for table_ref in refs[:-1]:
            stop = start + table_ref.shape[0]
            out_ref[0, start:stop, :] = dot(table_ref[...], hot).astype(out_ref.dtype)
            start = stop

    return call(
        kernel,
        pltpu.HBM((count, features, entries), tables[0].dtype),
        (count,),
        [pl.BlockSpec((1, 1, entries), lambda b, base: (base[0] + b, 0, 0))]
        + [pl.BlockSpec(t.shape, lambda b, base: (0, 0)) for t in tables],
        pl.BlockSpec((1, features, entries), lambda b, base: (b, 0, 0)),
        1000,
        1000,
        prefetch=1,
    )(base, ids, *tables)


def gather_pieces(me, ids, tables, partners):
    entries = ids.shape[2]
    docs = tables[0][0].shape[1]
    features = sum(rows for _, rows in tables)
    count = len(partners)

    def kernel(me_ref, *refs):
        table_refs = refs[count : count + len(tables)]
        for ids_ref, out_ref in zip(refs[:count], refs[count + len(tables) :]):
            hot = one_hot(ids_ref[0], docs)
            start = 0
            for table_ref in table_refs:
                stop = start + table_ref.shape[0]
                out_ref[start:stop, :] = dot(table_ref[...], hot).astype(out_ref.dtype)
                start = stop

    return call(
        kernel,
        [pltpu.HBM((features, entries), tables[0][0].dtype)] * count,
        (1,),
        [pl.BlockSpec((1, 1, entries), lambda i, me, k=k: (me[0] ^ k, 0, 0)) for k in partners]
        + [pl.BlockSpec((rows, docs), lambda i, me: (0, 0)) for _, rows in tables],
        [pl.BlockSpec((features, entries), lambda i, me: (0, 0))] * count,
        1000,
        1000,
        prefetch=1,
    )(me, *[ids] * count, *[table for table, _ in tables])


def padded(values, above, below):
    zeros = lambda rows: [jnp.zeros((rows, values.shape[1]), values.dtype)] if rows else []
    return jnp.concatenate([*zeros(above), values, *zeros(below)], axis=0)


def score_pieces(me, prepared, chosen, total, width, scale):
    queries = prepared.shape[0]
    features, entries = next(iter(chosen.values()))[0].shape
    count = len(chosen)
    parts = [part for parts in chosen.values() for part in parts]
    whole = pl.BlockSpec((queries, entries), lambda i, me: (0, 0))

    def kernel(me_ref, *refs):
        out = refs[-2][...]
        part_refs = iter(refs[count:-2])
        for prepared_ref, pieces in zip(refs[:count], chosen.values()):
            piece = sum((next(part_refs)[...] for _ in pieces[1:]), next(part_refs)[...])
            out = out + dot(prepared_ref[...], padded(piece, 0, width - features))
        refs[-1][...] = out * scale

    return call(
        kernel,
        jax.ShapeDtypeStruct((queries, entries), jnp.float32),
        (1,),
        [pl.BlockSpec((queries, width), lambda i, me, k=k: (0, me[0] ^ k)) for k in chosen]
        + [pl.BlockSpec((features, entries), lambda i, me: (0, 0))] * len(parts)
        + [whole],
        whole,
        1000,
        1000,
        prefetch=1,
    )(me, *[prepared] * count, *parts, total)


def score_near(base, prepared, chosen, width, half):
    queries = prepared.shape[0]
    count, features, entries = chosen.shape
    tail = features - width
    block = max(tail, LANES)
    stride = width // block

    def kernel(base_ref, own_ref, far_ref, chosen_ref, out_ref):
        part = dot(own_ref[...], chosen_ref[0, :width, :])
        part += dot(far_ref[...], padded(chosen_ref[0, width:, :], block - tail, 0))

        @pl.when(pl.program_id(0) == 0)
        def _():
            out_ref[...] = part

        @pl.when(pl.program_id(0) > 0)
        def _():
            out_ref[...] += part

    return call(
        kernel,
        jax.ShapeDtypeStruct((queries, entries), jnp.float32),
        (count,),
        [
            pl.BlockSpec((queries, width), lambda j, base: (0, base[0] + j)),
            pl.BlockSpec(
                (queries, block), lambda j, base: (0, ((base[0] + j) ^ half) * stride + stride - 1)
            ),
            pl.BlockSpec((1, features, entries), lambda j, base: (j, 0, 0)),
        ],
        pl.BlockSpec((queries, entries), lambda j, base: (0, 0)),
        1000,
        1000,
        prefetch=1,
    )(base, prepared, prepared, chosen)


def score_all(prepared, chosen, scale):
    queries = prepared.shape[0]
    devices, width, entries = chosen.shape

    def kernel(prepared_ref, chosen_ref, out_ref):
        part = dot(prepared_ref[...], chosen_ref[...]) * scale

        @pl.when(pl.program_id(0) == 0)
        def _():
            out_ref[...] = part

        @pl.when(pl.program_id(0) > 0)
        def _():
            out_ref[...] += part

    steps = 4
    block = devices * width // steps
    return call(
        kernel,
        jax.ShapeDtypeStruct((queries, entries), jnp.float32),
        (steps,),
        [
            pl.BlockSpec((queries, block), lambda i: (0, i)),
            pl.BlockSpec((block, entries), lambda i: (i, 0)),
        ],
        pl.BlockSpec((queries, entries), lambda i: (0, 0)),
        2 * devices * width * queries * entries,
        2 * devices * width * (queries + entries) + 4 * queries * entries,
    )(prepared, chosen.reshape(devices * width, entries))


def precondition(queries, left_inv, right_inv):
    total, features = queries.shape
    layers, k_out, _ = left_inv.shape
    k_in = right_inv.shape[1]
    group = MXU // k_out
    pair = MXU // k_in
    rows = 64
    wide = k_out // pair
    both = 2 * group

    def spread(values, times):
        size = values.shape[0]
        rows = lax.broadcasted_iota(jnp.int32, (MXU, size), 0) // times
        picks = (rows == lax.broadcasted_iota(jnp.int32, (MXU, size), 1)).astype(values.dtype)
        wide = dot(picks, values).astype(values.dtype)
        wide = lax.dot_general(
            wide, picks, (((1,), (1,)), ((), ())), preferred_element_type=jnp.float32
        )
        row = lax.broadcasted_iota(jnp.int32, (MXU, MXU), 0) % times
        column = lax.broadcasted_iota(jnp.int32, (MXU, MXU), 1) % times
        return jnp.where(row == column, wide, 0.0).astype(values.dtype)

    def repeat(values, times):
        empty = jnp.zeros_like(values)
        return jnp.concatenate(
            [
                jnp.concatenate([values if i == j else empty for j in range(times)], axis=1)
                for i in range(times)
            ],
            axis=0,
        )

    def kernel(queries_ref, left_inv_ref, right_inv_ref, out_ref, middle_ref, left_ref, right_ref):
        @pl.when(pl.program_id(0) == 0)
        def _():
            for layer in range(layers):
                left_ref[layer] = spread(left_inv_ref[layer], group)
                right_ref[layer] = repeat(right_inv_ref[layer], pair)

        for layer in range(layers):
            first = layer * k_out * k_in
            stack = jnp.concatenate(
                [queries_ref[:, first + p * MXU : first + (p + 1) * MXU] for p in range(wide)], axis=0
            )
            middle_ref[...] = dot(stack, right_ref[layer])
            for q in range(0, rows, both):
                halves = []
                for start in (q, q + group):
                    tiles = []
                    for p in range(wide):
                        at = p * rows + start
                        for s in range(pair):
                            tiles.append(middle_ref[at : at + group, s * k_in : (s + 1) * k_in])
                    halves.append(jnp.concatenate(tiles, axis=0))
                middle = jnp.concatenate(halves, axis=1).astype(queries_ref.dtype)
                result = dot(left_ref[layer], middle)
                for a in range(k_out):
                    at = a * group
                    tile = jnp.concatenate(
                        [result[at : at + group, :k_in], result[at : at + group, k_in:]], axis=0
                    )
                    lanes = first + a * k_in
                    out_ref[q : q + both, lanes : lanes + k_in] = tile.astype(out_ref.dtype)

    return call(
        kernel,
        jax.ShapeDtypeStruct(queries.shape, queries.dtype),
        (total // rows,),
        [
            pl.BlockSpec((rows, features), lambda i: (i, 0)),
            pl.BlockSpec(left_inv.shape, lambda i: (0, 0, 0)),
            pl.BlockSpec(right_inv.shape, lambda i: (0, 0, 0)),
        ],
        pl.BlockSpec((rows, features), lambda i: (i, 0)),
        40000 * total * features,
        4 * total * features,
        scratch=[
            pltpu.VMEM((wide * rows, MXU), jnp.float32),
            pltpu.VMEM((layers, MXU, MXU), left_inv.dtype),
            pltpu.VMEM((layers, MXU, MXU), right_inv.dtype),
        ],
    )(queries, left_inv, right_inv)


def after(value, *earlier):
    return lax.optimization_barrier((value, *earlier))[0]


def on_device(doc_grads, query_grads, left_inv, right_inv, cand_owner, cand_row):
    devices = lax.axis_size("docs")
    half = devices // 2
    me = lax.axis_index("docs").astype(jnp.int32).reshape(1)
    base = me & -half
    doc_count = doc_grads.shape[0] // devices
    entries = cand_row.shape[0]
    width = doc_grads.shape[1]
    scale = query_grads.shape[1] ** (-0.5)

    def swap(values, k, members=range(devices)):
        return lax.ppermute(values, "docs", [(i, i ^ k) for i in members])

    def exchange(values):
        return lax.all_to_all(values, "docs", split_axis=0, concat_axis=0, tiled=True)

    tail = width // 8 if width % (4 * LANES) == 0 else 0
    if not tail:
        own_ids = cand_owner[:, 0] * doc_count + cand_row
        ids = exchange(jnp.broadcast_to(own_ids, (devices, 1, entries)))
        picked = gather_rows(jnp.zeros((1,), jnp.int32), ids, [doc_grads.T], devices)
        return score_all(precondition(query_grads, left_inv, right_inv), exchange(picked), scale)

    own_tail, own_ids = prepare(doc_grads, cand_owner, cand_row, devices, tail)
    across = swap(own_tail, half)
    ids = exchange(own_ids)
    table = after(doc_grads, own_ids).T
    quarter = half // 2
    inner, outer = range(quarter, 3 * quarter), [*range(quarter), *range(3 * quarter, devices)]
    first, third, second = [half, half + 1], list(range(half + 2, half + quarter)), list(range(half + quarter, devices))
    body = [(table, width - tail)]
    ids = after(ids, across)
    pieces = dict(zip(first, gather_pieces(me, ids, body, first)))
    came = {k: [swap(pieces[k], k)] for k in first}
    ready = [came[k][0] for k in first]
    ids = after(ids, pieces[first[0]])
    picked = gather_rows(base, ids, [table, across], half)
    near = lax.all_to_all(
        picked,
        "docs",
        split_axis=0,
        concat_axis=0,
        axis_index_groups=[list(range(half)), list(range(half, devices))],
        tiled=True,
    )
    ids = after(ids, picked)
    pieces.update(zip(second + third, gather_pieces(me, ids, body, second + third)))
    prepared = precondition(after(query_grads, *ready), left_inv, right_inv)
    for k in second:
        came[k] = [swap(after(pieces[k], *ready), k, inner)]
    before = [near, prepared]
    for k in second:
        came[k].append(swap(after(pieces[k], *before), k, outer))
    for i, k in enumerate(third):
        came[k] = [swap(after(pieces[k], *before, *[came[second[0]][1]][:i]), k)]
    total = score_near(base, prepared, near, width, half)
    last = third[-1:]
    others = [k for k in came if k not in last]
    total = score_pieces(me, prepared, {k: came[k] for k in others}, total, width, 1.0)
    return score_pieces(me, prepared, {k: came[k] for k in last}, total, width, scale)


def solution(mesh):
    placed = (
        P("parts", "docs"),
        P(("parts", "docs"), None),
        P(),
        P(),
        P(("parts", "docs"), None),
        P(("parts", "docs")),
    )
    return jax.shard_map(
        on_device, mesh=mesh, in_specs=placed, out_specs=P(("parts", "docs"), None), check_vma=False
    )
```

```python
import jax
import jax.numpy as jnp
from jax import lax
from jax.experimental import pallas as pl
from jax.experimental.pallas import tpu as pltpu
from jax.sharding import PartitionSpec as P

LANES = 128
SUBLANES = 8
MXU = 256
VMEM_BYTES = 48 << 20
ALL_VMEM_BYTES = 63 << 20


def call(kernel, out_shape, grid, in_specs, out_specs, flops, bytes_accessed, scratch=(), prefetch=0, vmem=VMEM_BYTES):
    return pl.pallas_call(
        kernel,
        grid_spec=pltpu.PrefetchScalarGridSpec(
            num_scalar_prefetch=prefetch,
            grid=grid,
            in_specs=in_specs,
            out_specs=out_specs,
            scratch_shapes=scratch,
        ),
        out_shape=out_shape,
        compiler_params=pltpu.CompilerParams(vmem_limit_bytes=vmem),
        cost_estimate=pl.CostEstimate(flops=flops, bytes_accessed=bytes_accessed, transcendentals=0),
    )


def dot(a, b):
    return jnp.dot(a, b, preferred_element_type=jnp.float32)


def one_hot(ids, docs):
    group, row = ids // LANES, ids % LANES
    in_group = (lax.broadcasted_iota(jnp.int32, (LANES, ids.shape[1]), 0) == row).astype(jnp.bfloat16)
    return jnp.concatenate(
        [in_group * (group == g).astype(jnp.bfloat16) for g in range(docs // LANES)], axis=0
    )


def prepare(doc_grads, owners, rows, devices, tail):
    docs, width = doc_grads.shape
    entries = rows.shape[0]
    doc_count = docs // devices
    block = max(tail, LANES)

    def kernel(docs_hbm, owners_hbm, rows_hbm, tail_ref, ids_ref, docs_ref, owners_ref, rows_ref, sems):
        copies = [
            pltpu.make_async_copy(docs_hbm.at[:, width - block :], docs_ref, sems.at[0]),
            pltpu.make_async_copy(owners_hbm, owners_ref, sems.at[1]),
            pltpu.make_async_copy(rows_hbm, rows_ref, sems.at[2]),
        ]
        for copy in copies:
            copy.start()
        for copy in copies:
            copy.wait()
        tail_ref[...] = docs_ref[...].T[block - tail :, :]
        ids = owners_ref[...] * doc_count + rows_ref[...]
        ids_ref[...] = jnp.broadcast_to(ids[None], ids_ref.shape)

    return call(
        kernel,
        [
            pltpu.HBM((tail, docs), doc_grads.dtype),
            pltpu.HBM((devices, 1, entries), jnp.int32),
        ],
        (1,),
        [pl.BlockSpec(memory_space=pltpu.HBM)] * 3,
        [
            pl.BlockSpec((tail, docs), lambda i: (0, 0)),
            pl.BlockSpec((devices, 1, entries), lambda i: (0, 0, 0)),
        ],
        0,
        2 * docs * (block + tail),
        scratch=[
            pltpu.VMEM((docs, block), doc_grads.dtype),
            pltpu.VMEM((1, entries), jnp.int32),
            pltpu.VMEM((1, entries), jnp.int32),
            pltpu.SemaphoreType.DMA((3,)),
        ],
        vmem=ALL_VMEM_BYTES,
    )(doc_grads, owners.reshape(1, entries), rows.reshape(1, entries))


def gather_rows(base, ids, tables, count):
    entries = ids.shape[2]
    docs = tables[0].shape[1]
    features = sum(t.shape[0] for t in tables)

    def kernel(base_ref, ids_ref, *refs):
        out_ref = refs[-1]
        hot = one_hot(ids_ref[0], docs)
        start = 0
        for table_ref in refs[:-1]:
            stop = start + table_ref.shape[0]
            out_ref[0, start:stop, :] = dot(table_ref[...], hot).astype(out_ref.dtype)
            start = stop

    return call(
        kernel,
        pltpu.HBM((count, features, entries), tables[0].dtype),
        (count,),
        [pl.BlockSpec((1, 1, entries), lambda b, base: (base[0] + b, 0, 0))]
        + [pl.BlockSpec(t.shape, lambda b, base: (0, 0)) for t in tables],
        pl.BlockSpec((1, features, entries), lambda b, base: (b, 0, 0)),
        1000,
        1000,
        prefetch=1,
    )(base, ids, *tables)


def gather_pieces(me, ids, tables, partners):
    entries = ids.shape[2]
    docs = tables[0][0].shape[1]
    features = sum(rows for _, rows in tables)
    count = len(partners)

    def kernel(me_ref, *refs):
        table_refs = refs[count : count + len(tables)]
        for ids_ref, out_ref in zip(refs[:count], refs[count + len(tables) :]):
            hot = one_hot(ids_ref[0], docs)
            start = 0
            for table_ref in table_refs:
                stop = start + table_ref.shape[0]
                out_ref[start:stop, :] = dot(table_ref[...], hot).astype(out_ref.dtype)
                start = stop

    return call(
        kernel,
        [pltpu.HBM((features, entries), tables[0][0].dtype)] * count,
        (1,),
        [pl.BlockSpec((1, 1, entries), lambda i, me, k=k: (me[0] ^ k, 0, 0)) for k in partners]
        + [pl.BlockSpec((rows, docs), lambda i, me: (0, 0)) for _, rows in tables],
        [pl.BlockSpec((features, entries), lambda i, me: (0, 0))] * count,
        1000,
        1000,
        prefetch=1,
    )(me, *[ids] * count, *[table for table, _ in tables])


def padded(values, above, below):
    zeros = lambda rows: [jnp.zeros((rows, values.shape[1]), values.dtype)] if rows else []
    return jnp.concatenate([*zeros(above), values, *zeros(below)], axis=0)


def score_pieces(me, prepared, chosen, total, width, scale):
    queries = prepared.shape[0]
    features, entries = next(iter(chosen.values()))[0].shape
    count = len(chosen)
    parts = [part for parts in chosen.values() for part in parts]
    whole = pl.BlockSpec((queries, entries), lambda i, me: (0, 0))

    def kernel(me_ref, *refs):
        out = refs[-2][...]
        part_refs = iter(refs[count:-2])
        for prepared_ref, pieces in zip(refs[:count], chosen.values()):
            piece = sum((next(part_refs)[...] for _ in pieces[1:]), next(part_refs)[...])
            out = out + dot(prepared_ref[...], padded(piece, 0, width - features))
        refs[-1][...] = out * scale

    return call(
        kernel,
        jax.ShapeDtypeStruct((queries, entries), jnp.float32),
        (1,),
        [pl.BlockSpec((queries, width), lambda i, me, k=k: (0, me[0] ^ k)) for k in chosen]
        + [pl.BlockSpec((features, entries), lambda i, me: (0, 0))] * len(parts)
        + [whole],
        whole,
        1000,
        1000,
        prefetch=1,
    )(me, *[prepared] * count, *parts, total)


def score_near(base, prepared, chosen, width, half):
    queries = prepared.shape[0]
    count, features, entries = chosen.shape
    tail = features - width
    block = max(tail, LANES)
    stride = width // block

    def kernel(base_ref, own_ref, far_ref, chosen_ref, out_ref):
        part = dot(own_ref[...], chosen_ref[0, :width, :])
        part += dot(far_ref[...], padded(chosen_ref[0, width:, :], block - tail, 0))

        @pl.when(pl.program_id(0) == 0)
        def _():
            out_ref[...] = part

        @pl.when(pl.program_id(0) > 0)
        def _():
            out_ref[...] += part

    return call(
        kernel,
        jax.ShapeDtypeStruct((queries, entries), jnp.float32),
        (count,),
        [
            pl.BlockSpec((queries, width), lambda j, base: (0, base[0] + j)),
            pl.BlockSpec(
                (queries, block), lambda j, base: (0, ((base[0] + j) ^ half) * stride + stride - 1)
            ),
            pl.BlockSpec((1, features, entries), lambda j, base: (j, 0, 0)),
        ],
        pl.BlockSpec((queries, entries), lambda j, base: (0, 0)),
        1000,
        1000,
        prefetch=1,
    )(base, prepared, prepared, chosen)


def score_all(prepared, chosen, scale):
    queries = prepared.shape[0]
    devices, width, entries = chosen.shape

    def kernel(prepared_ref, chosen_ref, out_ref):
        part = dot(prepared_ref[...], chosen_ref[...]) * scale

        @pl.when(pl.program_id(0) == 0)
        def _():
            out_ref[...] = part

        @pl.when(pl.program_id(0) > 0)
        def _():
            out_ref[...] += part

    steps = 4
    block = devices * width // steps
    return call(
        kernel,
        jax.ShapeDtypeStruct((queries, entries), jnp.float32),
        (steps,),
        [
            pl.BlockSpec((queries, block), lambda i: (0, i)),
            pl.BlockSpec((block, entries), lambda i: (i, 0)),
        ],
        pl.BlockSpec((queries, entries), lambda i: (0, 0)),
        2 * devices * width * queries * entries,
        2 * devices * width * (queries + entries) + 4 * queries * entries,
    )(prepared, chosen.reshape(devices * width, entries))


def precondition(queries, left_inv, right_inv):
    total, features = queries.shape
    layers, k_out, _ = left_inv.shape
    k_in = right_inv.shape[1]
    group = MXU // k_out
    pair = MXU // k_in
    rows = 64
    wide = k_out // pair
    both = 2 * group

    def spread(values, times):
        size = values.shape[0]
        rows = lax.broadcasted_iota(jnp.int32, (MXU, size), 0) // times
        picks = (rows == lax.broadcasted_iota(jnp.int32, (MXU, size), 1)).astype(values.dtype)
        wide = dot(picks, values).astype(values.dtype)
        wide = lax.dot_general(
            wide, picks, (((1,), (1,)), ((), ())), preferred_element_type=jnp.float32
        )
        row = lax.broadcasted_iota(jnp.int32, (MXU, MXU), 0) % times
        column = lax.broadcasted_iota(jnp.int32, (MXU, MXU), 1) % times
        return jnp.where(row == column, wide, 0.0).astype(values.dtype)

    def repeat(values, times):
        empty = jnp.zeros_like(values)
        return jnp.concatenate(
            [
                jnp.concatenate([values if i == j else empty for j in range(times)], axis=1)
                for i in range(times)
            ],
            axis=0,
        )

    def kernel(queries_ref, left_inv_ref, right_inv_ref, out_ref, middle_ref, left_ref, right_ref):
        @pl.when(pl.program_id(0) == 0)
        def _():
            for layer in range(layers):
                left_ref[layer] = spread(left_inv_ref[layer], group)
                right_ref[layer] = repeat(right_inv_ref[layer], pair)

        for layer in range(layers):
            first = layer * k_out * k_in
            stack = jnp.concatenate(
                [queries_ref[:, first + p * MXU : first + (p + 1) * MXU] for p in range(wide)], axis=0
            )
            middle_ref[...] = dot(stack, right_ref[layer])
            for q in range(0, rows, both):
                halves = []
                for start in (q, q + group):
                    tiles = []
                    for p in range(wide):
                        at = p * rows + start
                        for s in range(pair):
                            tiles.append(middle_ref[at : at + group, s * k_in : (s + 1) * k_in])
                    halves.append(jnp.concatenate(tiles, axis=0))
                middle = jnp.concatenate(halves, axis=1).astype(queries_ref.dtype)
                result = dot(left_ref[layer], middle)
                for a in range(k_out):
                    at = a * group
                    tile = jnp.concatenate(
                        [result[at : at + group, :k_in], result[at : at + group, k_in:]], axis=0
                    )
                    lanes = first + a * k_in
                    out_ref[q : q + both, lanes : lanes + k_in] = tile.astype(out_ref.dtype)

    return call(
        kernel,
        jax.ShapeDtypeStruct(queries.shape, queries.dtype),
        (total // rows,),
        [
            pl.BlockSpec((rows, features), lambda i: (i, 0)),
            pl.BlockSpec(left_inv.shape, lambda i: (0, 0, 0)),
            pl.BlockSpec(right_inv.shape, lambda i: (0, 0, 0)),
        ],
        pl.BlockSpec((rows, features), lambda i: (i, 0)),
        40000 * total * features,
        4 * total * features,
        scratch=[
            pltpu.VMEM((wide * rows, MXU), jnp.float32),
            pltpu.VMEM((layers, MXU, MXU), left_inv.dtype),
            pltpu.VMEM((layers, MXU, MXU), right_inv.dtype),
        ],
    )(queries, left_inv, right_inv)


def after(value, *earlier):
    return lax.optimization_barrier((value, *earlier))[0]


def on_device(doc_grads, query_grads, left_inv, right_inv, cand_owner, cand_row):
    devices = lax.axis_size("docs")
    half = devices // 2
    me = lax.axis_index("docs").astype(jnp.int32).reshape(1)
    base = me & -half
    doc_count = doc_grads.shape[0] // devices
    entries = cand_row.shape[0]
    width = doc_grads.shape[1]
    scale = query_grads.shape[1] ** (-0.5)

    def swap(values, k, members=range(devices)):
        return lax.ppermute(values, "docs", [(i, i ^ k) for i in members])

    def exchange(values):
        return lax.all_to_all(values, "docs", split_axis=0, concat_axis=0, tiled=True)

    tail = width // 8 if width % (4 * LANES) == 0 else 0
    if not tail:
        own_ids = cand_owner[:, 0] * doc_count + cand_row
        ids = exchange(jnp.broadcast_to(own_ids, (devices, 1, entries)))
        picked = gather_rows(jnp.zeros((1,), jnp.int32), ids, [doc_grads.T], devices)
        return score_all(precondition(query_grads, left_inv, right_inv), exchange(picked), scale)

    own_tail, own_ids = prepare(doc_grads, cand_owner, cand_row, devices, tail)
    across = swap(own_tail, half)
    ids = exchange(own_ids)
    table = after(doc_grads, own_ids).T
    quarter = half // 2
    inner, outer = range(quarter, 3 * quarter), [*range(quarter), *range(3 * quarter, devices)]
    first, third, second = [half, half + 1], list(range(half + 2, half + quarter)), list(range(half + quarter, devices))
    body = [(table, width - tail)]
    ids = after(ids, across)
    pieces = dict(zip(first, gather_pieces(me, ids, body, first)))
    came = {k: [swap(pieces[k], k)] for k in first}
    ready = [came[k][0] for k in first]
    ids = after(ids, pieces[first[0]])
    picked = gather_rows(base, ids, [table, across], half)
    near = lax.all_to_all(
        picked,
        "docs",
        split_axis=0,
        concat_axis=0,
        axis_index_groups=[list(range(half)), list(range(half, devices))],
        tiled=True,
    )
    ids = after(ids, picked)
    pieces.update(zip(second + third, gather_pieces(me, ids, body, second + third)))
    prepared = precondition(after(query_grads, *ready), left_inv, right_inv)
    for k in second:
        came[k] = [swap(after(pieces[k], *ready), k, inner)]
    before = [near, prepared, *[came[k][0] for k in second]]
    for k in second:
        came[k].append(swap(after(pieces[k], *before), k, outer))
    for i, k in enumerate(third):
        came[k] = [swap(after(pieces[k], *before, *[came[j][1] for j in second[:i]]), k)]
    total = score_near(base, prepared, near, width, half)
    last = third[-1:]
    others = [k for k in came if k not in last]
    total = score_pieces(me, prepared, {k: came[k] for k in others}, total, width, 1.0)
    return score_pieces(me, prepared, {k: came[k] for k in last}, total, width, scale)


def solution(mesh):
    placed = (
        P("parts", "docs"),
        P(("parts", "docs"), None),
        P(),
        P(),
        P(("parts", "docs"), None),
        P(("parts", "docs")),
    )
    return jax.shard_map(
        on_device, mesh=mesh, in_specs=placed, out_specs=P(("parts", "docs"), None), check_vma=False
    )
```

```python
import jax
import jax.numpy as jnp
from jax import lax
from jax.experimental import pallas as pl
from jax.experimental.pallas import tpu as pltpu
from jax.sharding import PartitionSpec as P

LANES = 128
SUBLANES = 8
MXU = 256
VMEM_BYTES = 48 << 20
ALL_VMEM_BYTES = 63 << 20


def call(kernel, out_shape, grid, in_specs, out_specs, flops, bytes_accessed, scratch=(), prefetch=0, vmem=VMEM_BYTES):
    return pl.pallas_call(
        kernel,
        grid_spec=pltpu.PrefetchScalarGridSpec(
            num_scalar_prefetch=prefetch,
            grid=grid,
            in_specs=in_specs,
            out_specs=out_specs,
            scratch_shapes=scratch,
        ),
        out_shape=out_shape,
        compiler_params=pltpu.CompilerParams(vmem_limit_bytes=vmem),
        cost_estimate=pl.CostEstimate(flops=flops, bytes_accessed=bytes_accessed, transcendentals=0),
    )


def dot(a, b):
    return jnp.dot(a, b, preferred_element_type=jnp.float32)


def one_hot(ids, docs):
    group, row = ids // LANES, ids % LANES
    in_group = (lax.broadcasted_iota(jnp.int32, (LANES, ids.shape[1]), 0) == row).astype(jnp.bfloat16)
    return jnp.concatenate(
        [in_group * (group == g).astype(jnp.bfloat16) for g in range(docs // LANES)], axis=0
    )


def prepare(doc_grads, owners, rows, devices, tail):
    docs, width = doc_grads.shape
    entries = rows.shape[0]
    doc_count = docs // devices
    block = max(tail, LANES)

    def kernel(docs_hbm, owners_hbm, rows_hbm, tail_ref, ids_ref, docs_ref, owners_ref, rows_ref, sems):
        copies = [
            pltpu.make_async_copy(docs_hbm.at[:, width - block :], docs_ref, sems.at[0]),
            pltpu.make_async_copy(owners_hbm, owners_ref, sems.at[1]),
            pltpu.make_async_copy(rows_hbm, rows_ref, sems.at[2]),
        ]
        for copy in copies:
            copy.start()
        for copy in copies:
            copy.wait()
        tail_ref[...] = docs_ref[...].T[block - tail :, :]
        ids = owners_ref[...] * doc_count + rows_ref[...]
        ids_ref[...] = jnp.broadcast_to(ids[None], ids_ref.shape)

    return call(
        kernel,
        [
            pltpu.HBM((tail, docs), doc_grads.dtype),
            pltpu.HBM((devices, 1, entries), jnp.int32),
        ],
        (1,),
        [pl.BlockSpec(memory_space=pltpu.HBM)] * 3,
        [
            pl.BlockSpec((tail, docs), lambda i: (0, 0)),
            pl.BlockSpec((devices, 1, entries), lambda i: (0, 0, 0)),
        ],
        0,
        2 * docs * (block + tail),
        scratch=[
            pltpu.VMEM((docs, block), doc_grads.dtype),
            pltpu.VMEM((1, entries), jnp.int32),
            pltpu.VMEM((1, entries), jnp.int32),
            pltpu.SemaphoreType.DMA((3,)),
        ],
        vmem=ALL_VMEM_BYTES,
    )(doc_grads, owners.reshape(1, entries), rows.reshape(1, entries))


def gather_rows(base, ids, tables, count):
    entries = ids.shape[2]
    docs = tables[0].shape[1]
    features = sum(t.shape[0] for t in tables)

    def kernel(base_ref, ids_ref, *refs):
        out_ref = refs[-1]
        hot = one_hot(ids_ref[0], docs)
        start = 0
        for table_ref in refs[:-1]:
            stop = start + table_ref.shape[0]
            out_ref[0, start:stop, :] = dot(table_ref[...], hot).astype(out_ref.dtype)
            start = stop

    return call(
        kernel,
        pltpu.HBM((count, features, entries), tables[0].dtype),
        (count,),
        [pl.BlockSpec((1, 1, entries), lambda b, base: (base[0] + b, 0, 0))]
        + [pl.BlockSpec(t.shape, lambda b, base: (0, 0)) for t in tables],
        pl.BlockSpec((1, features, entries), lambda b, base: (b, 0, 0)),
        1000,
        1000,
        prefetch=1,
    )(base, ids, *tables)


def gather_pieces(me, ids, tables, partners):
    entries = ids.shape[2]
    docs = tables[0][0].shape[1]
    features = sum(rows for _, rows in tables)
    count = len(partners)

    def kernel(me_ref, *refs):
        table_refs = refs[count : count + len(tables)]
        for ids_ref, out_ref in zip(refs[:count], refs[count + len(tables) :]):
            hot = one_hot(ids_ref[0], docs)
            start = 0
            for table_ref in table_refs:
                stop = start + table_ref.shape[0]
                out_ref[start:stop, :] = dot(table_ref[...], hot).astype(out_ref.dtype)
                start = stop

    return call(
        kernel,
        [pltpu.HBM((features, entries), tables[0][0].dtype)] * count,
        (1,),
        [pl.BlockSpec((1, 1, entries), lambda i, me, k=k: (me[0] ^ k, 0, 0)) for k in partners]
        + [pl.BlockSpec((rows, docs), lambda i, me: (0, 0)) for _, rows in tables],
        [pl.BlockSpec((features, entries), lambda i, me: (0, 0))] * count,
        1000,
        1000,
        prefetch=1,
    )(me, *[ids] * count, *[table for table, _ in tables])


def padded(values, above, below):
    zeros = lambda rows: [jnp.zeros((rows, values.shape[1]), values.dtype)] if rows else []
    return jnp.concatenate([*zeros(above), values, *zeros(below)], axis=0)


def score_pieces(me, prepared, chosen, total, width, scale):
    queries = prepared.shape[0]
    features, entries = next(iter(chosen.values())).shape
    count = len(chosen)
    whole = pl.BlockSpec((queries, entries), lambda i, me: (0, 0))

    def kernel(me_ref, *refs):
        out = refs[-2][...]
        for prepared_ref, chosen_ref in zip(refs[:count], refs[count : 2 * count]):
            out = out + dot(prepared_ref[...], padded(chosen_ref[...], 0, width - features))
        refs[-1][...] = out * scale

    return call(
        kernel,
        jax.ShapeDtypeStruct((queries, entries), jnp.float32),
        (1,),
        [pl.BlockSpec((queries, width), lambda i, me, k=k: (0, me[0] ^ k)) for k in chosen]
        + [pl.BlockSpec((features, entries), lambda i, me: (0, 0))] * count
        + [whole],
        whole,
        2 * count * features * queries * entries,
        2 * count * features * (queries + entries) + 8 * queries * entries,
        prefetch=1,
    )(me, *[prepared] * count, *chosen.values(), total)


def score_near(base, prepared, chosen, width, half):
    queries = prepared.shape[0]
    count, features, entries = chosen.shape
    tail = features - width
    block = max(tail, LANES)
    stride = width // block

    def kernel(base_ref, own_ref, far_ref, chosen_ref, out_ref):
        part = dot(own_ref[...], chosen_ref[0, :width, :])
        part += dot(far_ref[...], padded(chosen_ref[0, width:, :], block - tail, 0))

        @pl.when(pl.program_id(0) == 0)
        def _():
            out_ref[...] = part

        @pl.when(pl.program_id(0) > 0)
        def _():
            out_ref[...] += part

    return call(
        kernel,
        jax.ShapeDtypeStruct((queries, entries), jnp.float32),
        (count,),
        [
            pl.BlockSpec((queries, width), lambda j, base: (0, base[0] + j)),
            pl.BlockSpec(
                (queries, block), lambda j, base: (0, ((base[0] + j) ^ half) * stride + stride - 1)
            ),
            pl.BlockSpec((1, features, entries), lambda j, base: (j, 0, 0)),
        ],
        pl.BlockSpec((queries, entries), lambda j, base: (0, 0)),
        2 * count * features * queries * entries,
        2 * count * features * (queries + entries) + 4 * queries * entries,
        prefetch=1,
    )(base, prepared, prepared, chosen)


def score_all(prepared, chosen, scale):
    queries = prepared.shape[0]
    devices, width, entries = chosen.shape

    def kernel(prepared_ref, chosen_ref, out_ref):
        part = dot(prepared_ref[...], chosen_ref[...]) * scale

        @pl.when(pl.program_id(0) == 0)
        def _():
            out_ref[...] = part

        @pl.when(pl.program_id(0) > 0)
        def _():
            out_ref[...] += part

    steps = 4
    block = devices * width // steps
    return call(
        kernel,
        jax.ShapeDtypeStruct((queries, entries), jnp.float32),
        (steps,),
        [
            pl.BlockSpec((queries, block), lambda i: (0, i)),
            pl.BlockSpec((block, entries), lambda i: (i, 0)),
        ],
        pl.BlockSpec((queries, entries), lambda i: (0, 0)),
        2 * devices * width * queries * entries,
        2 * devices * width * (queries + entries) + 4 * queries * entries,
    )(prepared, chosen.reshape(devices * width, entries))


def precondition(queries, left_inv, right_inv):
    total, features = queries.shape
    layers, k_out, _ = left_inv.shape
    k_in = right_inv.shape[1]
    group = MXU // k_out
    pair = MXU // k_in
    rows = 64
    wide = k_out // pair
    both = 2 * group

    def spread(values, times):
        size = values.shape[0]
        rows = lax.broadcasted_iota(jnp.int32, (MXU, size), 0) // times
        picks = (rows == lax.broadcasted_iota(jnp.int32, (MXU, size), 1)).astype(values.dtype)
        wide = dot(picks, values).astype(values.dtype)
        wide = lax.dot_general(
            wide, picks, (((1,), (1,)), ((), ())), preferred_element_type=jnp.float32
        )
        row = lax.broadcasted_iota(jnp.int32, (MXU, MXU), 0) % times
        column = lax.broadcasted_iota(jnp.int32, (MXU, MXU), 1) % times
        return jnp.where(row == column, wide, 0.0).astype(values.dtype)

    def repeat(values, times):
        empty = jnp.zeros_like(values)
        return jnp.concatenate(
            [
                jnp.concatenate([values if i == j else empty for j in range(times)], axis=1)
                for i in range(times)
            ],
            axis=0,
        )

    def kernel(queries_ref, left_inv_ref, right_inv_ref, out_ref, middle_ref, left_ref, right_ref):
        @pl.when(pl.program_id(0) == 0)
        def _():
            for layer in range(layers):
                left_ref[layer] = spread(left_inv_ref[layer], group)
                right_ref[layer] = repeat(right_inv_ref[layer], pair)

        for layer in range(layers):
            first = layer * k_out * k_in
            stack = jnp.concatenate(
                [queries_ref[:, first + p * MXU : first + (p + 1) * MXU] for p in range(wide)], axis=0
            )
            middle_ref[...] = dot(stack, right_ref[layer])
            for q in range(0, rows, both):
                halves = []
                for start in (q, q + group):
                    tiles = []
                    for p in range(wide):
                        at = p * rows + start
                        for s in range(pair):
                            tiles.append(middle_ref[at : at + group, s * k_in : (s + 1) * k_in])
                    halves.append(jnp.concatenate(tiles, axis=0))
                middle = jnp.concatenate(halves, axis=1).astype(queries_ref.dtype)
                result = dot(left_ref[layer], middle)
                for a in range(k_out):
                    at = a * group
                    tile = jnp.concatenate(
                        [result[at : at + group, :k_in], result[at : at + group, k_in:]], axis=0
                    )
                    lanes = first + a * k_in
                    out_ref[q : q + both, lanes : lanes + k_in] = tile.astype(out_ref.dtype)

    return call(
        kernel,
        jax.ShapeDtypeStruct(queries.shape, queries.dtype),
        (total // rows,),
        [
            pl.BlockSpec((rows, features), lambda i: (i, 0)),
            pl.BlockSpec(left_inv.shape, lambda i: (0, 0, 0)),
            pl.BlockSpec(right_inv.shape, lambda i: (0, 0, 0)),
        ],
        pl.BlockSpec((rows, features), lambda i: (i, 0)),
        40000 * total * features,
        4 * total * features,
        scratch=[
            pltpu.VMEM((wide * rows, MXU), jnp.float32),
            pltpu.VMEM((layers, MXU, MXU), left_inv.dtype),
            pltpu.VMEM((layers, MXU, MXU), right_inv.dtype),
        ],
    )(queries, left_inv, right_inv)


def after(value, *earlier):
    return lax.optimization_barrier((value, *earlier))[0]


def on_device(doc_grads, query_grads, left_inv, right_inv, cand_owner, cand_row):
    devices = lax.axis_size("docs")
    half = devices // 2
    me = lax.axis_index("docs").astype(jnp.int32).reshape(1)
    base = me & -half
    doc_count = doc_grads.shape[0] // devices
    entries = cand_row.shape[0]
    width = doc_grads.shape[1]
    scale = query_grads.shape[1] ** (-0.5)

    def swap(values, k):
        return lax.ppermute(values, "docs", [(i, i ^ k) for i in range(devices)])

    def exchange(values):
        return lax.all_to_all(values, "docs", split_axis=0, concat_axis=0, tiled=True)

    tail = width // 8 if width % (4 * LANES) == 0 else 0
    if not tail:
        own_ids = cand_owner[:, 0] * doc_count + cand_row
        ids = exchange(jnp.broadcast_to(own_ids, (devices, 1, entries)))
        picked = gather_rows(jnp.zeros((1,), jnp.int32), ids, [doc_grads.T], devices)
        return score_all(precondition(query_grads, left_inv, right_inv), exchange(picked), scale)

    own_tail, own_ids = prepare(doc_grads, cand_owner, cand_row, devices, tail)
    across = swap(own_tail, half)
    ids = exchange(own_ids)
    table = after(doc_grads, own_ids).T
    quarter = half // 2
    far = [half, half + 1, *range(half + quarter, devices), *range(half + 2, half + quarter)]
    first, second, third = far[:2], far[2 : 2 + quarter], far[2 + quarter :]
    body = [(table, width - tail)]
    ids = after(ids, across)
    pieces = dict(zip(far, gather_pieces(me, ids, body, first)))
    came = {k: swap(pieces[k], k) for k in first}
    ids = after(ids, pieces[first[0]])
    pieces.update(zip(far[2:], gather_pieces(me, ids, body, far[2:])))
    ids = after(ids, pieces[second[0]])
    picked = gather_rows(base, ids, [table, across], half)
    near = lax.all_to_all(
        picked,
        "docs",
        split_axis=0,
        concat_axis=0,
        axis_index_groups=[list(range(half)), list(range(half, devices))],
        tiled=True,
    )
    ready = [came[k] for k in first]
    prepared = precondition(after(query_grads, *ready), left_inv, right_inv)
    for k in second:
        came[k] = swap(after(pieces[k], *ready), k)
    for i, k in enumerate(third):
        before = [came[second[0]]] if i else ready
        came[k] = swap(after(pieces[k], prepared, *before), k)
    total = score_near(base, prepared, near, width, half)
    others = [*first, *second, *third[:-1]]
    total = score_pieces(me, prepared, {k: came[k] for k in others}, total, width, 1.0)
    return score_pieces(me, prepared, {k: came[k] for k in third[-1:]}, total, width, scale)


def solution(mesh):
    placed = (
        P("parts", "docs"),
        P(("parts", "docs"), None),
        P(),
        P(),
        P(("parts", "docs"), None),
        P(("parts", "docs")),
    )
    return jax.shard_map(
        on_device, mesh=mesh, in_specs=placed, out_specs=P(("parts", "docs"), None), check_vma=False
    )
```

```python
import jax
import jax.numpy as jnp
from jax import lax
from jax.experimental import pallas as pl
from jax.experimental.pallas import tpu as pltpu
from jax.sharding import PartitionSpec as P

LANES = 128
SUBLANES = 8
MXU = 256
VMEM_BYTES = 48 << 20
ALL_VMEM_BYTES = 63 << 20


def call(kernel, out_shape, grid, in_specs, out_specs, flops, bytes_accessed, scratch=(), prefetch=0, vmem=VMEM_BYTES):
    return pl.pallas_call(
        kernel,
        grid_spec=pltpu.PrefetchScalarGridSpec(
            num_scalar_prefetch=prefetch,
            grid=grid,
            in_specs=in_specs,
            out_specs=out_specs,
            scratch_shapes=scratch,
        ),
        out_shape=out_shape,
        compiler_params=pltpu.CompilerParams(vmem_limit_bytes=vmem),
        cost_estimate=pl.CostEstimate(flops=flops, bytes_accessed=bytes_accessed, transcendentals=0),
    )


def dot(a, b):
    return jnp.dot(a, b, preferred_element_type=jnp.float32)


def one_hot(ids, docs):
    group, row = ids // LANES, ids % LANES
    in_group = (lax.broadcasted_iota(jnp.int32, (LANES, ids.shape[1]), 0) == row).astype(jnp.bfloat16)
    return jnp.concatenate(
        [in_group * (group == g).astype(jnp.bfloat16) for g in range(docs // LANES)], axis=0
    )


def prepare(doc_grads, owners, rows, devices, tail):
    docs, width = doc_grads.shape
    entries = rows.shape[0]
    doc_count = docs // devices
    block = max(tail, LANES)

    def kernel(docs_hbm, owners_hbm, rows_hbm, tail_ref, ids_ref, docs_ref, owners_ref, rows_ref, sems):
        copies = [
            pltpu.make_async_copy(docs_hbm.at[:, width - block :], docs_ref, sems.at[0]),
            pltpu.make_async_copy(owners_hbm, owners_ref, sems.at[1]),
            pltpu.make_async_copy(rows_hbm, rows_ref, sems.at[2]),
        ]
        for copy in copies:
            copy.start()
        for copy in copies:
            copy.wait()
        tail_ref[...] = docs_ref[...].T[block - tail :, :]
        ids = owners_ref[...] * doc_count + rows_ref[...]
        ids_ref[...] = jnp.broadcast_to(ids[None], ids_ref.shape)

    return call(
        kernel,
        [
            pltpu.HBM((tail, docs), doc_grads.dtype),
            pltpu.HBM((devices, 1, entries), jnp.int32),
        ],
        (1,),
        [pl.BlockSpec(memory_space=pltpu.HBM)] * 3,
        [
            pl.BlockSpec((tail, docs), lambda i: (0, 0)),
            pl.BlockSpec((devices, 1, entries), lambda i: (0, 0, 0)),
        ],
        0,
        2 * docs * (block + tail),
        scratch=[
            pltpu.VMEM((docs, block), doc_grads.dtype),
            pltpu.VMEM((1, entries), jnp.int32),
            pltpu.VMEM((1, entries), jnp.int32),
            pltpu.SemaphoreType.DMA((3,)),
        ],
        vmem=ALL_VMEM_BYTES,
    )(doc_grads, owners.reshape(1, entries), rows.reshape(1, entries))


def gather_rows(base, ids, tables, count):
    entries = ids.shape[2]
    docs = tables[0].shape[1]
    features = sum(t.shape[0] for t in tables)

    def kernel(base_ref, ids_ref, *refs):
        out_ref = refs[-1]
        hot = one_hot(ids_ref[0], docs)
        start = 0
        for table_ref in refs[:-1]:
            stop = start + table_ref.shape[0]
            out_ref[0, start:stop, :] = dot(table_ref[...], hot).astype(out_ref.dtype)
            start = stop

    return call(
        kernel,
        pltpu.HBM((count, features, entries), tables[0].dtype),
        (count,),
        [pl.BlockSpec((1, 1, entries), lambda b, base: (base[0] + b, 0, 0))]
        + [pl.BlockSpec(t.shape, lambda b, base: (0, 0)) for t in tables],
        pl.BlockSpec((1, features, entries), lambda b, base: (b, 0, 0)),
        1000,
        1000,
        prefetch=1,
    )(base, ids, *tables)


def gather_pieces(me, ids, tables, partners):
    entries = ids.shape[2]
    docs = tables[0][0].shape[1]
    features = sum(rows for _, rows in tables)
    count = len(partners)

    def kernel(me_ref, *refs):
        table_refs = refs[count : count + len(tables)]
        for ids_ref, out_ref in zip(refs[:count], refs[count + len(tables) :]):
            hot = one_hot(ids_ref[0], docs)
            start = 0
            for table_ref in table_refs:
                stop = start + table_ref.shape[0]
                out_ref[start:stop, :] = dot(table_ref[...], hot).astype(out_ref.dtype)
                start = stop

    return call(
        kernel,
        [pltpu.HBM((features, entries), tables[0][0].dtype)] * count,
        (1,),
        [pl.BlockSpec((1, 1, entries), lambda i, me, k=k: (me[0] ^ k, 0, 0)) for k in partners]
        + [pl.BlockSpec((rows, docs), lambda i, me: (0, 0)) for _, rows in tables],
        [pl.BlockSpec((features, entries), lambda i, me: (0, 0))] * count,
        1000,
        1000,
        prefetch=1,
    )(me, *[ids] * count, *[table for table, _ in tables])


def padded(values, above, below):
    zeros = lambda rows: [jnp.zeros((rows, values.shape[1]), values.dtype)] if rows else []
    return jnp.concatenate([*zeros(above), values, *zeros(below)], axis=0)


def score_pieces(me, prepared, chosen, total, width, scale):
    queries = prepared.shape[0]
    features, entries = next(iter(chosen.values())).shape
    count = len(chosen)
    whole = pl.BlockSpec((queries, entries), lambda i, me: (0, 0))

    def kernel(me_ref, *refs):
        out = refs[-2][...]
        for prepared_ref, chosen_ref in zip(refs[:count], refs[count : 2 * count]):
            out = out + dot(prepared_ref[...], padded(chosen_ref[...], 0, width - features))
        refs[-1][...] = out * scale

    return call(
        kernel,
        jax.ShapeDtypeStruct((queries, entries), jnp.float32),
        (1,),
        [pl.BlockSpec((queries, width), lambda i, me, k=k: (0, me[0] ^ k)) for k in chosen]
        + [pl.BlockSpec((features, entries), lambda i, me: (0, 0))] * count
        + [whole],
        whole,
        2 * count * features * queries * entries,
        2 * count * features * (queries + entries) + 8 * queries * entries,
        prefetch=1,
    )(me, *[prepared] * count, *chosen.values(), total)


def score_near(base, prepared, chosen, width, half):
    queries = prepared.shape[0]
    count, features, entries = chosen.shape
    tail = features - width
    block = max(tail, LANES)
    stride = width // block

    def kernel(base_ref, own_ref, far_ref, chosen_ref, out_ref):
        part = dot(own_ref[...], chosen_ref[0, :width, :])
        part += dot(far_ref[...], padded(chosen_ref[0, width:, :], block - tail, 0))

        @pl.when(pl.program_id(0) == 0)
        def _():
            out_ref[...] = part

        @pl.when(pl.program_id(0) > 0)
        def _():
            out_ref[...] += part

    return call(
        kernel,
        jax.ShapeDtypeStruct((queries, entries), jnp.float32),
        (count,),
        [
            pl.BlockSpec((queries, width), lambda j, base: (0, base[0] + j)),
            pl.BlockSpec(
                (queries, block), lambda j, base: (0, ((base[0] + j) ^ half) * stride + stride - 1)
            ),
            pl.BlockSpec((1, features, entries), lambda j, base: (j, 0, 0)),
        ],
        pl.BlockSpec((queries, entries), lambda j, base: (0, 0)),
        2 * count * features * queries * entries,
        2 * count * features * (queries + entries) + 4 * queries * entries,
        prefetch=1,
    )(base, prepared, prepared, chosen)


def score_all(prepared, chosen, scale):
    queries = prepared.shape[0]
    devices, width, entries = chosen.shape

    def kernel(prepared_ref, chosen_ref, out_ref):
        part = dot(prepared_ref[...], chosen_ref[...]) * scale

        @pl.when(pl.program_id(0) == 0)
        def _():
            out_ref[...] = part

        @pl.when(pl.program_id(0) > 0)
        def _():
            out_ref[...] += part

    steps = 4
    block = devices * width // steps
    return call(
        kernel,
        jax.ShapeDtypeStruct((queries, entries), jnp.float32),
        (steps,),
        [
            pl.BlockSpec((queries, block), lambda i: (0, i)),
            pl.BlockSpec((block, entries), lambda i: (i, 0)),
        ],
        pl.BlockSpec((queries, entries), lambda i: (0, 0)),
        2 * devices * width * queries * entries,
        2 * devices * width * (queries + entries) + 4 * queries * entries,
    )(prepared, chosen.reshape(devices * width, entries))


def precondition(queries, left_inv, right_inv):
    total, features = queries.shape
    layers, k_out, _ = left_inv.shape
    k_in = right_inv.shape[1]
    group = MXU // k_out
    pair = MXU // k_in
    rows = 64
    wide = k_out // pair
    both = 2 * group

    def spread(values, times):
        size = values.shape[0]
        rows = lax.broadcasted_iota(jnp.int32, (MXU, size), 0) // times
        picks = (rows == lax.broadcasted_iota(jnp.int32, (MXU, size), 1)).astype(values.dtype)
        wide = dot(picks, values).astype(values.dtype)
        wide = lax.dot_general(
            wide, picks, (((1,), (1,)), ((), ())), preferred_element_type=jnp.float32
        )
        row = lax.broadcasted_iota(jnp.int32, (MXU, MXU), 0) % times
        column = lax.broadcasted_iota(jnp.int32, (MXU, MXU), 1) % times
        return jnp.where(row == column, wide, 0.0).astype(values.dtype)

    def repeat(values, times):
        empty = jnp.zeros_like(values)
        return jnp.concatenate(
            [
                jnp.concatenate([values if i == j else empty for j in range(times)], axis=1)
                for i in range(times)
            ],
            axis=0,
        )

    def kernel(queries_ref, left_inv_ref, right_inv_ref, out_ref, middle_ref, left_ref, right_ref):
        @pl.when(pl.program_id(0) == 0)
        def _():
            for layer in range(layers):
                left_ref[layer] = spread(left_inv_ref[layer], group)
                right_ref[layer] = repeat(right_inv_ref[layer], pair)

        for layer in range(layers):
            first = layer * k_out * k_in
            stack = jnp.concatenate(
                [queries_ref[:, first + p * MXU : first + (p + 1) * MXU] for p in range(wide)], axis=0
            )
            middle_ref[...] = dot(stack, right_ref[layer])
            for q in range(0, rows, both):
                halves = []
                for start in (q, q + group):
                    tiles = []
                    for p in range(wide):
                        at = p * rows + start
                        for s in range(pair):
                            tiles.append(middle_ref[at : at + group, s * k_in : (s + 1) * k_in])
                    halves.append(jnp.concatenate(tiles, axis=0))
                middle = jnp.concatenate(halves, axis=1).astype(queries_ref.dtype)
                result = dot(left_ref[layer], middle)
                for a in range(k_out):
                    at = a * group
                    tile = jnp.concatenate(
                        [result[at : at + group, :k_in], result[at : at + group, k_in:]], axis=0
                    )
                    lanes = first + a * k_in
                    out_ref[q : q + both, lanes : lanes + k_in] = tile.astype(out_ref.dtype)

    return call(
        kernel,
        jax.ShapeDtypeStruct(queries.shape, queries.dtype),
        (total // rows,),
        [
            pl.BlockSpec((rows, features), lambda i: (i, 0)),
            pl.BlockSpec(left_inv.shape, lambda i: (0, 0, 0)),
            pl.BlockSpec(right_inv.shape, lambda i: (0, 0, 0)),
        ],
        pl.BlockSpec((rows, features), lambda i: (i, 0)),
        40000 * total * features,
        4 * total * features,
        scratch=[
            pltpu.VMEM((wide * rows, MXU), jnp.float32),
            pltpu.VMEM((layers, MXU, MXU), left_inv.dtype),
            pltpu.VMEM((layers, MXU, MXU), right_inv.dtype),
        ],
    )(queries, left_inv, right_inv)


def after(value, *earlier):
    return lax.optimization_barrier((value, *earlier))[0]


def on_device(doc_grads, query_grads, left_inv, right_inv, cand_owner, cand_row):
    devices = lax.axis_size("docs")
    half = devices // 2
    me = lax.axis_index("docs").astype(jnp.int32).reshape(1)
    base = me & -half
    doc_count = doc_grads.shape[0] // devices
    entries = cand_row.shape[0]
    width = doc_grads.shape[1]
    scale = query_grads.shape[1] ** (-0.5)

    def swap(values, k):
        return lax.ppermute(values, "docs", [(i, i ^ k) for i in range(devices)])

    def exchange(values):
        return lax.all_to_all(values, "docs", split_axis=0, concat_axis=0, tiled=True)

    tail = width // 8 if width % (4 * LANES) == 0 else 0
    if not tail:
        own_ids = cand_owner[:, 0] * doc_count + cand_row
        ids = exchange(jnp.broadcast_to(own_ids, (devices, 1, entries)))
        picked = gather_rows(jnp.zeros((1,), jnp.int32), ids, [doc_grads.T], devices)
        return score_all(precondition(query_grads, left_inv, right_inv), exchange(picked), scale)

    own_tail, own_ids = prepare(doc_grads, cand_owner, cand_row, devices, tail)
    across = swap(own_tail, half)
    ids = exchange(own_ids)
    table = after(doc_grads, own_ids).T
    quarter = half // 2
    far = [half, half + 1, *range(half + quarter, devices), *range(half + 2, half + quarter)]
    first, second, third = far[:2], far[2 : 2 + quarter], far[2 + quarter :]
    body = [(table, width - tail)]
    ids = after(ids, across)
    pieces = dict(zip(far, gather_pieces(me, ids, body, first)))
    came = {k: swap(pieces[k], k) for k in first}
    ids = after(ids, pieces[first[0]])
    picked = gather_rows(base, ids, [table, across], half)
    near = lax.all_to_all(
        picked,
        "docs",
        split_axis=0,
        concat_axis=0,
        axis_index_groups=[list(range(half)), list(range(half, devices))],
        tiled=True,
    )
    ids = after(ids, picked)
    pieces.update(zip(far[2:], gather_pieces(me, ids, body, far[2:])))
    ready = [came[k] for k in first]
    prepared = precondition(after(query_grads, *ready), left_inv, right_inv)
    for k in second:
        came[k] = swap(after(pieces[k], *ready), k)
    for i, k in enumerate(third):
        before = [came[second[0]]] if i else ready
        came[k] = swap(after(pieces[k], prepared, *before), k)
    total = score_near(base, prepared, near, width, half)
    others = [*first, *second, *third[:-1]]
    total = score_pieces(me, prepared, {k: came[k] for k in others}, total, width, 1.0)
    return score_pieces(me, prepared, {k: came[k] for k in third[-1:]}, total, width, scale)


def solution(mesh):
    placed = (
        P("parts", "docs"),
        P(("parts", "docs"), None),
        P(),
        P(),
        P(("parts", "docs"), None),
        P(("parts", "docs")),
    )
    return jax.shard_map(
        on_device, mesh=mesh, in_specs=placed, out_specs=P(("parts", "docs"), None), check_vma=False
    )
```

```python
import jax
import jax.numpy as jnp
from jax import lax
from jax.experimental import pallas as pl
from jax.experimental.pallas import tpu as pltpu
from jax.sharding import PartitionSpec as P

LANES = 128
SUBLANES = 8
MXU = 256
VMEM_BYTES = 48 << 20
ALL_VMEM_BYTES = 63 << 20


def call(kernel, out_shape, grid, in_specs, out_specs, flops, bytes_accessed, scratch=(), prefetch=0, vmem=VMEM_BYTES):
    return pl.pallas_call(
        kernel,
        grid_spec=pltpu.PrefetchScalarGridSpec(
            num_scalar_prefetch=prefetch,
            grid=grid,
            in_specs=in_specs,
            out_specs=out_specs,
            scratch_shapes=scratch,
        ),
        out_shape=out_shape,
        compiler_params=pltpu.CompilerParams(vmem_limit_bytes=vmem),
        cost_estimate=pl.CostEstimate(flops=flops, bytes_accessed=bytes_accessed, transcendentals=0),
    )


def dot(a, b):
    return jnp.dot(a, b, preferred_element_type=jnp.float32)


def one_hot(ids, docs):
    group, row = ids // LANES, ids % LANES
    in_group = (lax.broadcasted_iota(jnp.int32, (LANES, ids.shape[1]), 0) == row).astype(jnp.bfloat16)
    return jnp.concatenate(
        [in_group * (group == g).astype(jnp.bfloat16) for g in range(docs // LANES)], axis=0
    )


def prepare(doc_grads, owners, rows, devices, tail):
    docs, width = doc_grads.shape
    entries = rows.shape[0]
    doc_count = docs // devices
    block = max(tail, LANES)

    def kernel(docs_hbm, owners_hbm, rows_hbm, tail_ref, ids_ref, docs_ref, owners_ref, rows_ref, sems):
        copies = [
            pltpu.make_async_copy(docs_hbm.at[:, width - block :], docs_ref, sems.at[0]),
            pltpu.make_async_copy(owners_hbm, owners_ref, sems.at[1]),
            pltpu.make_async_copy(rows_hbm, rows_ref, sems.at[2]),
        ]
        for copy in copies:
            copy.start()
        for copy in copies:
            copy.wait()
        tail_ref[...] = docs_ref[...].T[block - tail :, :]
        ids = owners_ref[...] * doc_count + rows_ref[...]
        ids_ref[...] = jnp.broadcast_to(ids[None], ids_ref.shape)

    return call(
        kernel,
        [
            pltpu.HBM((tail, docs), doc_grads.dtype),
            pltpu.HBM((devices, 1, entries), jnp.int32),
        ],
        (1,),
        [pl.BlockSpec(memory_space=pltpu.HBM)] * 3,
        [
            pl.BlockSpec((tail, docs), lambda i: (0, 0)),
            pl.BlockSpec((devices, 1, entries), lambda i: (0, 0, 0)),
        ],
        0,
        2 * docs * (block + tail),
        scratch=[
            pltpu.VMEM((docs, block), doc_grads.dtype),
            pltpu.VMEM((1, entries), jnp.int32),
            pltpu.VMEM((1, entries), jnp.int32),
            pltpu.SemaphoreType.DMA((3,)),
        ],
        vmem=ALL_VMEM_BYTES,
    )(doc_grads, owners.reshape(1, entries), rows.reshape(1, entries))


def gather_rows(base, ids, tables, count):
    entries = ids.shape[2]
    docs = tables[0].shape[1]
    features = sum(t.shape[0] for t in tables)

    def kernel(base_ref, ids_ref, *refs):
        out_ref = refs[-1]
        hot = one_hot(ids_ref[0], docs)
        start = 0
        for table_ref in refs[:-1]:
            stop = start + table_ref.shape[0]
            out_ref[0, start:stop, :] = dot(table_ref[...], hot).astype(out_ref.dtype)
            start = stop

    return call(
        kernel,
        pltpu.HBM((count, features, entries), tables[0].dtype),
        (count,),
        [pl.BlockSpec((1, 1, entries), lambda b, base: (base[0] + b, 0, 0))]
        + [pl.BlockSpec(t.shape, lambda b, base: (0, 0)) for t in tables],
        pl.BlockSpec((1, features, entries), lambda b, base: (b, 0, 0)),
        1000,
        1000,
        prefetch=1,
    )(base, ids, *tables)


def gather_pieces(me, ids, tables, partners):
    entries = ids.shape[2]
    docs = tables[0][0].shape[1]
    features = sum(rows for _, rows in tables)
    count = len(partners)

    def kernel(me_ref, *refs):
        table_refs = refs[count : count + len(tables)]
        for ids_ref, out_ref in zip(refs[:count], refs[count + len(tables) :]):
            hot = one_hot(ids_ref[0], docs)
            start = 0
            for table_ref in table_refs:
                stop = start + table_ref.shape[0]
                out_ref[start:stop, :] = dot(table_ref[...], hot).astype(out_ref.dtype)
                start = stop

    return call(
        kernel,
        [pltpu.HBM((features, entries), tables[0][0].dtype)] * count,
        (1,),
        [pl.BlockSpec((1, 1, entries), lambda i, me, k=k: (me[0] ^ k, 0, 0)) for k in partners]
        + [pl.BlockSpec((rows, docs), lambda i, me: (0, 0)) for _, rows in tables],
        [pl.BlockSpec((features, entries), lambda i, me: (0, 0))] * count,
        1000,
        1000,
        prefetch=1,
    )(me, *[ids] * count, *[table for table, _ in tables])


def padded(values, above, below):
    zeros = lambda rows: [jnp.zeros((rows, values.shape[1]), values.dtype)] if rows else []
    return jnp.concatenate([*zeros(above), values, *zeros(below)], axis=0)


def score_pieces(me, prepared, chosen, total, width, scale):
    queries = prepared.shape[0]
    features, entries = next(iter(chosen.values())).shape
    count = len(chosen)
    whole = pl.BlockSpec((queries, entries), lambda i, me: (0, 0))

    def kernel(me_ref, *refs):
        out = refs[-2][...]
        for prepared_ref, chosen_ref in zip(refs[:count], refs[count : 2 * count]):
            out = out + dot(prepared_ref[...], padded(chosen_ref[...], 0, width - features))
        refs[-1][...] = out * scale

    return call(
        kernel,
        jax.ShapeDtypeStruct((queries, entries), jnp.float32),
        (1,),
        [pl.BlockSpec((queries, width), lambda i, me, k=k: (0, me[0] ^ k)) for k in chosen]
        + [pl.BlockSpec((features, entries), lambda i, me: (0, 0))] * count
        + [whole],
        whole,
        2 * count * features * queries * entries,
        2 * count * features * (queries + entries) + 8 * queries * entries,
        prefetch=1,
    )(me, *[prepared] * count, *chosen.values(), total)


def score_near(base, prepared, chosen, width, half):
    queries = prepared.shape[0]
    count, features, entries = chosen.shape
    tail = features - width
    block = max(tail, LANES)
    stride = width // block

    def kernel(base_ref, own_ref, far_ref, chosen_ref, out_ref):
        part = dot(own_ref[...], chosen_ref[0, :width, :])
        part += dot(far_ref[...], padded(chosen_ref[0, width:, :], block - tail, 0))

        @pl.when(pl.program_id(0) == 0)
        def _():
            out_ref[...] = part

        @pl.when(pl.program_id(0) > 0)
        def _():
            out_ref[...] += part

    return call(
        kernel,
        jax.ShapeDtypeStruct((queries, entries), jnp.float32),
        (count,),
        [
            pl.BlockSpec((queries, width), lambda j, base: (0, base[0] + j)),
            pl.BlockSpec(
                (queries, block), lambda j, base: (0, ((base[0] + j) ^ half) * stride + stride - 1)
            ),
            pl.BlockSpec((1, features, entries), lambda j, base: (j, 0, 0)),
        ],
        pl.BlockSpec((queries, entries), lambda j, base: (0, 0)),
        2 * count * features * queries * entries,
        2 * count * features * (queries + entries) + 4 * queries * entries,
        prefetch=1,
    )(base, prepared, prepared, chosen)


def score_all(prepared, chosen, scale):
    queries = prepared.shape[0]
    devices, width, entries = chosen.shape

    def kernel(prepared_ref, chosen_ref, out_ref):
        part = dot(prepared_ref[...], chosen_ref[...]) * scale

        @pl.when(pl.program_id(0) == 0)
        def _():
            out_ref[...] = part

        @pl.when(pl.program_id(0) > 0)
        def _():
            out_ref[...] += part

    steps = 4
    block = devices * width // steps
    return call(
        kernel,
        jax.ShapeDtypeStruct((queries, entries), jnp.float32),
        (steps,),
        [
            pl.BlockSpec((queries, block), lambda i: (0, i)),
            pl.BlockSpec((block, entries), lambda i: (i, 0)),
        ],
        pl.BlockSpec((queries, entries), lambda i: (0, 0)),
        2 * devices * width * queries * entries,
        2 * devices * width * (queries + entries) + 4 * queries * entries,
    )(prepared, chosen.reshape(devices * width, entries))


def precondition(queries, left_inv, right_inv):
    total, features = queries.shape
    layers, k_out, _ = left_inv.shape
    k_in = right_inv.shape[1]
    group = MXU // k_out
    pair = MXU // k_in
    rows = 64
    wide = k_out // pair
    both = 2 * group

    def spread(values, times):
        size = values.shape[0]
        rows = lax.broadcasted_iota(jnp.int32, (MXU, size), 0) // times
        picks = (rows == lax.broadcasted_iota(jnp.int32, (MXU, size), 1)).astype(values.dtype)
        wide = dot(picks, values).astype(values.dtype)
        wide = lax.dot_general(
            wide, picks, (((1,), (1,)), ((), ())), preferred_element_type=jnp.float32
        )
        row = lax.broadcasted_iota(jnp.int32, (MXU, MXU), 0) % times
        column = lax.broadcasted_iota(jnp.int32, (MXU, MXU), 1) % times
        return jnp.where(row == column, wide, 0.0).astype(values.dtype)

    def repeat(values, times):
        empty = jnp.zeros_like(values)
        return jnp.concatenate(
            [
                jnp.concatenate([values if i == j else empty for j in range(times)], axis=1)
                for i in range(times)
            ],
            axis=0,
        )

    def kernel(queries_ref, left_inv_ref, right_inv_ref, out_ref, middle_ref, left_ref, right_ref):
        @pl.when(pl.program_id(0) == 0)
        def _():
            for layer in range(layers):
                left_ref[layer] = spread(left_inv_ref[layer], group)
                right_ref[layer] = repeat(right_inv_ref[layer], pair)

        for layer in range(layers):
            first = layer * k_out * k_in
            stack = jnp.concatenate(
                [queries_ref[:, first + p * MXU : first + (p + 1) * MXU] for p in range(wide)], axis=0
            )
            middle_ref[...] = dot(stack, right_ref[layer])
            for q in range(0, rows, both):
                halves = []
                for start in (q, q + group):
                    tiles = []
                    for p in range(wide):
                        at = p * rows + start
                        for s in range(pair):
                            tiles.append(middle_ref[at : at + group, s * k_in : (s + 1) * k_in])
                    halves.append(jnp.concatenate(tiles, axis=0))
                middle = jnp.concatenate(halves, axis=1).astype(queries_ref.dtype)
                result = dot(left_ref[layer], middle)
                for a in range(k_out):
                    at = a * group
                    tile = jnp.concatenate(
                        [result[at : at + group, :k_in], result[at : at + group, k_in:]], axis=0
                    )
                    lanes = first + a * k_in
                    out_ref[q : q + both, lanes : lanes + k_in] = tile.astype(out_ref.dtype)

    return call(
        kernel,
        jax.ShapeDtypeStruct(queries.shape, queries.dtype),
        (total // rows,),
        [
            pl.BlockSpec((rows, features), lambda i: (i, 0)),
            pl.BlockSpec(left_inv.shape, lambda i: (0, 0, 0)),
            pl.BlockSpec(right_inv.shape, lambda i: (0, 0, 0)),
        ],
        pl.BlockSpec((rows, features), lambda i: (i, 0)),
        40000 * total * features,
        4 * total * features,
        scratch=[
            pltpu.VMEM((wide * rows, MXU), jnp.float32),
            pltpu.VMEM((layers, MXU, MXU), left_inv.dtype),
            pltpu.VMEM((layers, MXU, MXU), right_inv.dtype),
        ],
    )(queries, left_inv, right_inv)


def after(value, *earlier):
    return lax.optimization_barrier((value, *earlier))[0]


def on_device(doc_grads, query_grads, left_inv, right_inv, cand_owner, cand_row):
    devices = lax.axis_size("docs")
    half = devices // 2
    me = lax.axis_index("docs").astype(jnp.int32).reshape(1)
    base = me & -half
    doc_count = doc_grads.shape[0] // devices
    entries = cand_row.shape[0]
    width = doc_grads.shape[1]
    scale = query_grads.shape[1] ** (-0.5)

    def swap(values, k):
        return lax.ppermute(values, "docs", [(i, i ^ k) for i in range(devices)])

    def exchange(values):
        return lax.all_to_all(values, "docs", split_axis=0, concat_axis=0, tiled=True)

    tail = width // 32 * 3 if width % (4 * LANES) == 0 else 0
    if not tail:
        own_ids = cand_owner[:, 0] * doc_count + cand_row
        ids = exchange(jnp.broadcast_to(own_ids, (devices, 1, entries)))
        picked = gather_rows(jnp.zeros((1,), jnp.int32), ids, [doc_grads.T], devices)
        return score_all(precondition(query_grads, left_inv, right_inv), exchange(picked), scale)

    own_tail, own_ids = prepare(doc_grads, cand_owner, cand_row, devices, tail)
    across = swap(own_tail, half)
    ids = exchange(own_ids)
    table = after(doc_grads, own_ids).T
    quarter = half // 2
    first, second = list(range(half + quarter, devices)), list(range(half, half + quarter))
    body = [(table, width - tail)]
    ids = after(ids, across)
    pieces = dict(zip(first, gather_pieces(me, ids, body, first)))
    came = {k: swap(pieces[k], k) for k in first}
    ids = after(ids, pieces[first[0]])
    picked = gather_rows(base, ids, [table, across], half)
    near = lax.all_to_all(
        picked,
        "docs",
        split_axis=0,
        concat_axis=0,
        axis_index_groups=[list(range(half)), list(range(half, devices))],
        tiled=True,
    )
    ids = after(ids, picked)
    pieces.update(zip(second, gather_pieces(me, ids, body, second)))
    prepared = precondition(after(query_grads, *[came[k] for k in first[:2]]), left_inv, right_inv)
    for i, k in enumerate(second):
        before = [came[first[i - 1]]] if i else []
        if i == quarter - 1:
            before.append(prepared)
        came[k] = swap(after(pieces[k], *before) if before else pieces[k], k)
    total = score_near(base, prepared, near, width, half)
    last = second[-1:]
    others = [k for k in came if k not in last]
    total = score_pieces(me, prepared, {k: came[k] for k in others}, total, width, 1.0)
    return score_pieces(me, prepared, {k: came[k] for k in last}, total, width, scale)


def solution(mesh):
    placed = (
        P("parts", "docs"),
        P(("parts", "docs"), None),
        P(),
        P(),
        P(("parts", "docs"), None),
        P(("parts", "docs")),
    )
    return jax.shard_map(
        on_device, mesh=mesh, in_specs=placed, out_specs=P(("parts", "docs"), None), check_vma=False
    )
```

```python
import jax
import jax.numpy as jnp
from jax import lax
from jax.experimental import pallas as pl
from jax.experimental.pallas import tpu as pltpu
from jax.sharding import PartitionSpec as P

LANES = 128
SUBLANES = 8
MXU = 256
VMEM_BYTES = 48 << 20
ALL_VMEM_BYTES = 63 << 20


def call(kernel, out_shape, grid, in_specs, out_specs, flops, bytes_accessed, scratch=(), prefetch=0, vmem=VMEM_BYTES):
    return pl.pallas_call(
        kernel,
        grid_spec=pltpu.PrefetchScalarGridSpec(
            num_scalar_prefetch=prefetch,
            grid=grid,
            in_specs=in_specs,
            out_specs=out_specs,
            scratch_shapes=scratch,
        ),
        out_shape=out_shape,
        compiler_params=pltpu.CompilerParams(vmem_limit_bytes=vmem),
        cost_estimate=pl.CostEstimate(flops=flops, bytes_accessed=bytes_accessed, transcendentals=0),
    )


def dot(a, b):
    return jnp.dot(a, b, preferred_element_type=jnp.float32)


def one_hot(ids, docs):
    group, row = ids // LANES, ids % LANES
    in_group = (lax.broadcasted_iota(jnp.int32, (LANES, ids.shape[1]), 0) == row).astype(jnp.bfloat16)
    return jnp.concatenate(
        [in_group * (group == g).astype(jnp.bfloat16) for g in range(docs // LANES)], axis=0
    )


def prepare(doc_grads, owners, rows, devices, tail):
    docs, width = doc_grads.shape
    entries = rows.shape[0]
    doc_count = docs // devices
    block = max(tail, LANES)

    def kernel(docs_hbm, owners_hbm, rows_hbm, tail_ref, ids_ref, docs_ref, owners_ref, rows_ref, sems):
        copies = [
            pltpu.make_async_copy(docs_hbm.at[:, width - block :], docs_ref, sems.at[0]),
            pltpu.make_async_copy(owners_hbm, owners_ref, sems.at[1]),
            pltpu.make_async_copy(rows_hbm, rows_ref, sems.at[2]),
        ]
        for copy in copies:
            copy.start()
        for copy in copies:
            copy.wait()
        tail_ref[...] = docs_ref[...].T[block - tail :, :]
        ids = owners_ref[...] * doc_count + rows_ref[...]
        ids_ref[...] = jnp.broadcast_to(ids[None], ids_ref.shape)

    return call(
        kernel,
        [
            pltpu.HBM((tail, docs), doc_grads.dtype),
            pltpu.HBM((devices, 1, entries), jnp.int32),
        ],
        (1,),
        [pl.BlockSpec(memory_space=pltpu.HBM)] * 3,
        [
            pl.BlockSpec((tail, docs), lambda i: (0, 0)),
            pl.BlockSpec((devices, 1, entries), lambda i: (0, 0, 0)),
        ],
        0,
        2 * docs * (block + tail),
        scratch=[
            pltpu.VMEM((docs, block), doc_grads.dtype),
            pltpu.VMEM((1, entries), jnp.int32),
            pltpu.VMEM((1, entries), jnp.int32),
            pltpu.SemaphoreType.DMA((3,)),
        ],
        vmem=ALL_VMEM_BYTES,
    )(doc_grads, owners.reshape(1, entries), rows.reshape(1, entries))


def gather_rows(base, ids, tables, count):
    entries = ids.shape[2]
    docs = tables[0].shape[1]
    features = sum(t.shape[0] for t in tables)

    def kernel(base_ref, ids_ref, *refs):
        out_ref = refs[-1]
        hot = one_hot(ids_ref[0], docs)
        start = 0
        for table_ref in refs[:-1]:
            stop = start + table_ref.shape[0]
            out_ref[0, start:stop, :] = dot(table_ref[...], hot).astype(out_ref.dtype)
            start = stop

    return call(
        kernel,
        pltpu.HBM((count, features, entries), tables[0].dtype),
        (count,),
        [pl.BlockSpec((1, 1, entries), lambda b, base: (base[0] + b, 0, 0))]
        + [pl.BlockSpec(t.shape, lambda b, base: (0, 0)) for t in tables],
        pl.BlockSpec((1, features, entries), lambda b, base: (b, 0, 0)),
        1000,
        1000,
        prefetch=1,
    )(base, ids, *tables)


def gather_pieces(me, ids, tables, partners):
    entries = ids.shape[2]
    docs = tables[0][0].shape[1]
    features = sum(rows for _, rows in tables)
    count = len(partners)

    def kernel(me_ref, *refs):
        table_refs = refs[count : count + len(tables)]
        for ids_ref, out_ref in zip(refs[:count], refs[count + len(tables) :]):
            hot = one_hot(ids_ref[0], docs)
            start = 0
            for table_ref in table_refs:
                stop = start + table_ref.shape[0]
                out_ref[start:stop, :] = dot(table_ref[...], hot).astype(out_ref.dtype)
                start = stop

    return call(
        kernel,
        [pltpu.HBM((features, entries), tables[0][0].dtype)] * count,
        (1,),
        [pl.BlockSpec((1, 1, entries), lambda i, me, k=k: (me[0] ^ k, 0, 0)) for k in partners]
        + [pl.BlockSpec((rows, docs), lambda i, me: (0, 0)) for _, rows in tables],
        [pl.BlockSpec((features, entries), lambda i, me: (0, 0))] * count,
        1000,
        1000,
        prefetch=1,
    )(me, *[ids] * count, *[table for table, _ in tables])


def padded(values, above, below):
    zeros = lambda rows: [jnp.zeros((rows, values.shape[1]), values.dtype)] if rows else []
    return jnp.concatenate([*zeros(above), values, *zeros(below)], axis=0)


def score_pieces(me, prepared, chosen, total, width, scale):
    queries = prepared.shape[0]
    features, entries = next(iter(chosen.values())).shape
    count = len(chosen)
    whole = pl.BlockSpec((queries, entries), lambda i, me: (0, 0))

    def kernel(me_ref, *refs):
        out = refs[-2][...]
        for prepared_ref, chosen_ref in zip(refs[:count], refs[count : 2 * count]):
            out = out + dot(prepared_ref[...], padded(chosen_ref[...], 0, width - features))
        refs[-1][...] = out * scale

    return call(
        kernel,
        jax.ShapeDtypeStruct((queries, entries), jnp.float32),
        (1,),
        [pl.BlockSpec((queries, width), lambda i, me, k=k: (0, me[0] ^ k)) for k in chosen]
        + [pl.BlockSpec((features, entries), lambda i, me: (0, 0))] * count
        + [whole],
        whole,
        2 * count * features * queries * entries,
        2 * count * features * (queries + entries) + 8 * queries * entries,
        prefetch=1,
    )(me, *[prepared] * count, *chosen.values(), total)


def score_near(base, prepared, chosen, width, half):
    queries = prepared.shape[0]
    count, features, entries = chosen.shape
    tail = features - width
    block = max(tail, LANES)
    stride = width // block

    def kernel(base_ref, own_ref, far_ref, chosen_ref, out_ref):
        part = dot(own_ref[...], chosen_ref[0, :width, :])
        part += dot(far_ref[...], padded(chosen_ref[0, width:, :], block - tail, 0))

        @pl.when(pl.program_id(0) == 0)
        def _():
            out_ref[...] = part

        @pl.when(pl.program_id(0) > 0)
        def _():
            out_ref[...] += part

    return call(
        kernel,
        jax.ShapeDtypeStruct((queries, entries), jnp.float32),
        (count,),
        [
            pl.BlockSpec((queries, width), lambda j, base: (0, base[0] + j)),
            pl.BlockSpec(
                (queries, block), lambda j, base: (0, ((base[0] + j) ^ half) * stride + stride - 1)
            ),
            pl.BlockSpec((1, features, entries), lambda j, base: (j, 0, 0)),
        ],
        pl.BlockSpec((queries, entries), lambda j, base: (0, 0)),
        2 * count * features * queries * entries,
        2 * count * features * (queries + entries) + 4 * queries * entries,
        prefetch=1,
    )(base, prepared, prepared, chosen)


def score_all(prepared, chosen, scale):
    queries = prepared.shape[0]
    devices, width, entries = chosen.shape

    def kernel(prepared_ref, chosen_ref, out_ref):
        part = dot(prepared_ref[...], chosen_ref[...]) * scale

        @pl.when(pl.program_id(0) == 0)
        def _():
            out_ref[...] = part

        @pl.when(pl.program_id(0) > 0)
        def _():
            out_ref[...] += part

    steps = 4
    block = devices * width // steps
    return call(
        kernel,
        jax.ShapeDtypeStruct((queries, entries), jnp.float32),
        (steps,),
        [
            pl.BlockSpec((queries, block), lambda i: (0, i)),
            pl.BlockSpec((block, entries), lambda i: (i, 0)),
        ],
        pl.BlockSpec((queries, entries), lambda i: (0, 0)),
        2 * devices * width * queries * entries,
        2 * devices * width * (queries + entries) + 4 * queries * entries,
    )(prepared, chosen.reshape(devices * width, entries))


def precondition(queries, left_inv, right_inv):
    total, features = queries.shape
    layers, k_out, _ = left_inv.shape
    k_in = right_inv.shape[1]
    group = MXU // k_out
    pair = MXU // k_in
    rows = 64
    wide = k_out // pair
    both = 2 * group

    def spread(values, times):
        size = values.shape[0]
        rows = lax.broadcasted_iota(jnp.int32, (MXU, size), 0) // times
        picks = (rows == lax.broadcasted_iota(jnp.int32, (MXU, size), 1)).astype(values.dtype)
        wide = dot(picks, values).astype(values.dtype)
        wide = lax.dot_general(
            wide, picks, (((1,), (1,)), ((), ())), preferred_element_type=jnp.float32
        )
        row = lax.broadcasted_iota(jnp.int32, (MXU, MXU), 0) % times
        column = lax.broadcasted_iota(jnp.int32, (MXU, MXU), 1) % times
        return jnp.where(row == column, wide, 0.0).astype(values.dtype)

    def repeat(values, times):
        empty = jnp.zeros_like(values)
        return jnp.concatenate(
            [
                jnp.concatenate([values if i == j else empty for j in range(times)], axis=1)
                for i in range(times)
            ],
            axis=0,
        )

    def kernel(queries_ref, left_inv_ref, right_inv_ref, out_ref, middle_ref, left_ref, right_ref):
        @pl.when(pl.program_id(0) == 0)
        def _():
            for layer in range(layers):
                left_ref[layer] = spread(left_inv_ref[layer], group)
                right_ref[layer] = repeat(right_inv_ref[layer], pair)

        for layer in range(layers):
            first = layer * k_out * k_in
            stack = jnp.concatenate(
                [queries_ref[:, first + p * MXU : first + (p + 1) * MXU] for p in range(wide)], axis=0
            )
            middle_ref[...] = dot(stack, right_ref[layer])
            for q in range(0, rows, both):
                halves = []
                for start in (q, q + group):
                    tiles = []
                    for p in range(wide):
                        at = p * rows + start
                        for s in range(pair):
                            tiles.append(middle_ref[at : at + group, s * k_in : (s + 1) * k_in])
                    halves.append(jnp.concatenate(tiles, axis=0))
                middle = jnp.concatenate(halves, axis=1).astype(queries_ref.dtype)
                result = dot(left_ref[layer], middle)
                for a in range(k_out):
                    at = a * group
                    tile = jnp.concatenate(
                        [result[at : at + group, :k_in], result[at : at + group, k_in:]], axis=0
                    )
                    lanes = first + a * k_in
                    out_ref[q : q + both, lanes : lanes + k_in] = tile.astype(out_ref.dtype)

    return call(
        kernel,
        jax.ShapeDtypeStruct(queries.shape, queries.dtype),
        (total // rows,),
        [
            pl.BlockSpec((rows, features), lambda i: (i, 0)),
            pl.BlockSpec(left_inv.shape, lambda i: (0, 0, 0)),
            pl.BlockSpec(right_inv.shape, lambda i: (0, 0, 0)),
        ],
        pl.BlockSpec((rows, features), lambda i: (i, 0)),
        40000 * total * features,
        4 * total * features,
        scratch=[
            pltpu.VMEM((wide * rows, MXU), jnp.float32),
            pltpu.VMEM((layers, MXU, MXU), left_inv.dtype),
            pltpu.VMEM((layers, MXU, MXU), right_inv.dtype),
        ],
    )(queries, left_inv, right_inv)


def after(value, *earlier):
    return lax.optimization_barrier((value, *earlier))[0]


def on_device(doc_grads, query_grads, left_inv, right_inv, cand_owner, cand_row):
    devices = lax.axis_size("docs")
    half = devices // 2
    me = lax.axis_index("docs").astype(jnp.int32).reshape(1)
    base = me & -half
    doc_count = doc_grads.shape[0] // devices
    entries = cand_row.shape[0]
    width = doc_grads.shape[1]
    scale = query_grads.shape[1] ** (-0.5)

    def swap(values, k):
        return lax.ppermute(values, "docs", [(i, i ^ k) for i in range(devices)])

    def exchange(values):
        return lax.all_to_all(values, "docs", split_axis=0, concat_axis=0, tiled=True)

    tail = width // 8 if width % (4 * LANES) == 0 else 0
    if not tail:
        own_ids = cand_owner[:, 0] * doc_count + cand_row
        ids = exchange(jnp.broadcast_to(own_ids, (devices, 1, entries)))
        picked = gather_rows(jnp.zeros((1,), jnp.int32), ids, [doc_grads.T], devices)
        return score_all(precondition(query_grads, left_inv, right_inv), exchange(picked), scale)

    own_tail, own_ids = prepare(doc_grads, cand_owner, cand_row, devices, tail)
    across = swap(own_tail, half)
    ids = exchange(own_ids)
    table = after(doc_grads, own_ids).T
    quarter = half // 2
    first, second = list(range(half + quarter, devices)), list(range(half, half + quarter))
    body = [(table, width - tail)]
    ids = after(ids, across)
    pieces = dict(zip(first, gather_pieces(me, ids, body, first[:2])))
    came = {k: swap(pieces[k], k) for k in first[:2]}
    ids = after(ids, pieces[first[0]])
    picked = gather_rows(base, ids, [table, across], half)
    near = lax.all_to_all(
        picked,
        "docs",
        split_axis=0,
        concat_axis=0,
        axis_index_groups=[list(range(half)), list(range(half, devices))],
        tiled=True,
    )
    ids = after(ids, picked)
    rest = first[2:] + second
    pieces.update(zip(rest, gather_pieces(me, ids, body, rest)))
    came.update({k: swap(pieces[k], k) for k in first[2:]})
    prepared = precondition(after(query_grads, *[came[k] for k in first[:2]]), left_inv, right_inv)
    for i, k in enumerate(second):
        before = [came[first[i - 1]]] if i else []
        if i == quarter - 1:
            before.append(prepared)
        came[k] = swap(after(pieces[k], *before) if before else pieces[k], k)
    total = score_near(base, prepared, near, width, half)
    last = second[-1:]
    others = [k for k in came if k not in last]
    total = score_pieces(me, prepared, {k: came[k] for k in others}, total, width, 1.0)
    return score_pieces(me, prepared, {k: came[k] for k in last}, total, width, scale)


def solution(mesh):
    placed = (
        P("parts", "docs"),
        P(("parts", "docs"), None),
        P(),
        P(),
        P(("parts", "docs"), None),
        P(("parts", "docs")),
    )
    return jax.shard_map(
        on_device, mesh=mesh, in_specs=placed, out_specs=P(("parts", "docs"), None), check_vma=False
    )
```
